512 devices in a mesh: lat: 8 (over z_hi, core), lon: 16 (over y, x), tp: 4 (over z_lo).
Axes of the slice: x: 4, y: 4, z: 16 (z_hi: 4, z_lo: 4; z = z_hi * 4 + z_lo), core: 2. Of those that a mesh axis runs over, the one named last changes fastest.
Arguments:
- fields: bfloat16 [128, 256, 1536], P('lat', 'lon', 'tp'), may hold values from -6 to 6
- w_qkv: bfloat16 [1536, 3, 768], P(None, None, 'tp'), may hold values from -0.15625 to 0.15625
- w_out: bfloat16 [768, 1536], P('tp'), may hold values from -0.21875 to 0.21875
- log_scale: float32 [12], P('tp'), may hold values from 0.7 to 3.4
- bias_table: float32 [225, 12], P(None, 'tp'), may hold values from -6 to 6
- bias_index: int32 [64, 64], replicated, may hold values from 0 to 224
- mask_ids: int32 [128, 256], P('lat', 'lon'), may hold values from 0 to 2
- norm_gain: float32 [1536], P('tp'), may hold values from 0.1 to 1.9
- norm_shift: float32 [1536], P('tp'), may hold values from -2 to 2
- cotangent: bfloat16 [128, 256, 1536], P('lat', 'lon', 'tp'), may hold values from -6 to 6
Outputs:
- block_out: bfloat16 [128, 256, 1536], P('lat', 'lon', 'tp')
- grad_fields: bfloat16 [128, 256, 1536], P('lat', 'lon', 'tp')
- grad_w_out: bfloat16 [768, 1536], P('tp')
- grad_table: float32 [225, 12], P(None, 'tp')
- grad_scale: float32 [12], P('tp')
- grad_gain: float32 [1536], P('tp')
- grad_shift: float32 [1536], P('tp')
The draws below stay inside these ranges and needn't reach their ends.
Inputs may be any that keep to these rules, and one draw needn't show every extreme that they name: `bias_index`: each entry names a row of bias_table. `mask_ids`: two cells of one shifted window attend to each other only when their labels are equal.
All inputs are finite; a program needn't handle non-finite values.
Results may differ from the reference program's by a relative error of at most 0.02.
Values may be sent and summed in bfloat16 or wider, within the bound.
A program may use at most 64 MiB of HBM per device.

```python
import jax
import jax.numpy as jnp
from jax import lax

C = 1536
HEADS = 12
WIN = 8
SHIFT = 4
NB = 225
ATT = 768
NLAT = 128
NLON = 256


def touch_ends(array, stream_key, smallest, top_value):
    place = [jax.random.randint(jax.random.fold_in(stream_key, axis), (), 0, length) for axis, length in enumerate(array.shape)]
    main_axis = array.shape.index(max(array.shape))
    neighbour = place[:main_axis] + [(place[main_axis] + 1) % array.shape[main_axis]] + place[main_axis + 1:]
    return array.at[tuple(place)].set(smallest).at[tuple(neighbour)].set(top_value)


def block_scale(key, shape, cuts, smallest, high):
    def one(dim, shards_of):
        heights = jax.random.uniform(jax.random.fold_in(jax.random.fold_in(key, 6), dim), (shards_of,), jnp.float32, smallest / len(cuts), high / len(cuts))
        return jnp.repeat(jnp.exp(heights), shape[dim] // shards_of).reshape((-1,) + (1,) * (len(shape) - dim - 1))

    level = one(*cuts[0])
    for cut in cuts[1:]:
        level = level * one(*cut)
    return level


def scatter_about(rng, shape, width, limit, split=(), kind=jnp.bfloat16):
    factor_of = block_scale(rng, shape, split, -0.22, 0.18) if split else 1.0
    array = jax.random.normal(rng, shape, jnp.float32) * width * factor_of
    return jnp.minimum(jnp.maximum(array, -limit), limit).astype(kind)


def setup_inputs(seed: int = 0) -> dict:
    key_list = jax.random.split(jax.random.key(seed), 11)
    fields = scatter_about(key_list[0], (NLAT, NLON, C), 1.0, 6.0, ((0, 8), (1, 16), (2, 4)))
    w_qkv = scatter_about(key_list[1], (C, 3, ATT), C ** -0.5, 0.15625, ((2, 4),))
    w_out = scatter_about(key_list[2], (ATT, C), ATT ** -0.5, 0.21875, ((0, 4),))
    log_scale = jnp.clip(0.7 + 2.7 * jax.random.uniform(key_list[3], (HEADS,), jnp.float32) ** block_scale(key_list[3], (HEADS,), ((0, 4),), -0.2, 0.2), 0.7, 3.4)
    bias_table = scatter_about(key_list[4], (NB, HEADS), 1.5, 6.0, ((1, 4),), jnp.float32)
    bias_index = touch_ends(jax.random.randint(key_list[5], (WIN * WIN, WIN * WIN), 0, NB), jax.random.fold_in(key_list[5], 1), 0, NB - 1).astype(jnp.int32)
    mask_ids = touch_ends(jax.random.randint(key_list[6], (NLAT, NLON), 0, 3), jax.random.fold_in(key_list[6], 1), 0, 2).astype(jnp.int32)
    norm_gain = jnp.clip(1.0 + 0.18 * jax.random.normal(key_list[7], (C,), jnp.float32), 0.1, 1.9)
    norm_shift = scatter_about(key_list[8], (C,), 0.3, 2.0, ((0, 4),), jnp.float32)
    cotangent = scatter_about(key_list[9], (NLAT, NLON, C), 1.0, 6.0, ((0, 8), (1, 16), (2, 4)))
    return {"fields": fields, "w_qkv": w_qkv, "w_out": w_out, "log_scale": log_scale, "bias_table": bias_table, "bias_index": bias_index, "mask_ids": mask_ids, "norm_gain": norm_gain, "norm_shift": norm_shift, "cotangent": cotangent}


def mult(spec, left, right):
    return jnp.einsum(spec, left.astype(jnp.float32), right.astype(jnp.float32))

def to_windows(tensor):
    extent_a, extent_b, heads_n, feature = tensor.shape
    tensor = tensor.reshape(extent_a // WIN, WIN, extent_b // WIN, WIN, heads_n, feature)
    tensor = tensor.transpose(0, 2, 4, 1, 3, 5)
    return tensor.reshape(extent_a // WIN * (extent_b // WIN), heads_n, WIN * WIN, feature)

def from_windows(tensor, extent_a, extent_b):
    n_windows, heads_n, win_cells, feature = tensor.shape
    tensor = tensor.reshape(extent_a // WIN, extent_b // WIN, heads_n, WIN, WIN, feature)
    tensor = tensor.transpose(0, 3, 1, 4, 2, 5)
    return tensor.reshape(extent_a, extent_b, heads_n * feature)

def window_ids(labels):
    extent_a, extent_b = labels.shape
    labels = labels.reshape(extent_a // WIN, WIN, extent_b // WIN, WIN).transpose(0, 2, 1, 3)
    return labels.reshape(-1, WIN * WIN)

def window_forward(proj_grid, log_scale, bias_sig, same_id):
    query = to_windows(proj_grid[:, :, 0])
    keys = to_windows(proj_grid[:, :, 1])
    values = to_windows(proj_grid[:, :, 2]).astype(jnp.bfloat16)
    q_len = jnp.sqrt(lax.optimization_barrier(jnp.sum(query * query, -1, keepdims=True)) + 1e-06)
    k_len = jnp.sqrt(lax.optimization_barrier(jnp.sum(keys * keys, -1, keepdims=True)) + 1e-06)
    q_hat = (query / q_len).astype(jnp.bfloat16)
    k_hat = (keys / k_len).astype(jnp.bfloat16)
    scale = jnp.exp(log_scale)[None, :, None, None]
    cosine = mult('nhie,nhje->nhij', q_hat, k_hat)
    logits = scale * cosine + 16.0 * bias_sig[None]
    weight = jnp.where(same_id, jnp.exp(logits - scale - 16.0), jnp.float32(0.0))
    prob = (weight / lax.optimization_barrier(jnp.sum(weight, -1, keepdims=True))).astype(jnp.bfloat16)
    attended = mult('nhij,nhje->nhie', prob, values).astype(jnp.bfloat16)
    return (attended, (q_hat, k_hat, values, q_len, k_len, cosine, prob))

def window_backward(grad_grid, saved, log_scale, bias_sig):
    q_hat, k_hat, values, q_len, k_len, cosine, prob = saved
    extent_a, extent_b = (grad_grid.shape[0], grad_grid.shape[1])
    grad_att = to_windows(grad_grid)
    prob_f = prob.astype(jnp.float32)
    grad_prob = mult('nhie,nhje->nhij', grad_att, values)
    grad_logit = prob_f * (grad_prob - lax.optimization_barrier(jnp.sum(prob_f * grad_prob, -1, keepdims=True)))
    grad_values = mult('nhij,nhie->nhje', prob, grad_att).astype(jnp.bfloat16)
    table_terms = lax.optimization_barrier(jnp.sum(grad_logit, 0)) * 16.0 * bias_sig * (1.0 - bias_sig)
    scale_terms = lax.optimization_barrier(jnp.sum(grad_logit * cosine, (0, 2, 3))) * jnp.exp(log_scale)
    scale = jnp.exp(log_scale)[None, :, None, None]
    grad_cos = (grad_logit * scale).astype(jnp.bfloat16)
    grad_qhat = mult('nhij,nhje->nhie', grad_cos, k_hat)
    grad_khat = mult('nhij,nhie->nhje', grad_cos, q_hat)
    q_float = q_hat.astype(jnp.float32)
    k_float = k_hat.astype(jnp.float32)
    grad_query = ((grad_qhat - q_float * lax.optimization_barrier(jnp.sum(q_float * grad_qhat, -1, keepdims=True))) / q_len).astype(jnp.bfloat16)
    grad_key = ((grad_khat - k_float * lax.optimization_barrier(jnp.sum(k_float * grad_khat, -1, keepdims=True))) / k_len).astype(jnp.bfloat16)
    stacked = jnp.stack([from_windows(grad_query, extent_a, extent_b), from_windows(grad_key, extent_a, extent_b), from_windows(grad_values, extent_a, extent_b)], 2)
    return (stacked, table_terms, scale_terms)

def reference(fields, w_qkv, w_out, log_scale, bias_table, bias_index, mask_ids, norm_gain, norm_shift, cotangent):
    extent_a, extent_b, channels = fields.shape
    heads_all = log_scale.shape[0]
    att_width = w_out.shape[0]
    head_size = att_width // heads_all
    shifted = jnp.roll(fields, (-SHIFT, -SHIFT), (0, 1))
    w_flat = w_qkv.reshape(channels, 3 * att_width)
    proj = jnp.dot(shifted.reshape(-1, channels), w_flat, preferred_element_type=jnp.float32)
    proj = proj.reshape(extent_a, extent_b, 3, heads_all, head_size)
    bias_sig = jax.nn.sigmoid(bias_table[bias_index]).transpose(2, 0, 1)
    labels = window_ids(mask_ids)
    same_id = (labels[:, :, None] == labels[:, None, :])[:, None]
    attended, saved = window_forward(proj, log_scale, bias_sig, same_id)
    att_grid = from_windows(attended, extent_a, extent_b).reshape(-1, att_width)
    mixed = jnp.dot(att_grid, w_out, preferred_element_type=jnp.float32)
    row_mean = lax.optimization_barrier(jnp.sum(mixed, 1, keepdims=True)) / channels
    row_var = lax.optimization_barrier(jnp.sum(mixed * mixed, 1, keepdims=True)) / channels - row_mean * row_mean
    inv_std = 1.0 / jnp.sqrt(row_var + 1e-05)
    normed = (mixed - row_mean) * inv_std
    branch = (norm_gain * normed + norm_shift).reshape(extent_a, extent_b, channels)
    block_out = (fields.astype(jnp.float32) + jnp.roll(branch, (SHIFT, SHIFT), (0, 1))).astype(jnp.bfloat16)
    grad_rows = jnp.roll(cotangent, (-SHIFT, -SHIFT), (0, 1)).reshape(-1, channels).astype(jnp.float32)
    grad_gain = lax.optimization_barrier(jnp.sum(grad_rows * normed, 0))
    grad_shift = lax.optimization_barrier(jnp.sum(grad_rows, 0))
    grad_norm = grad_rows * norm_gain
    sum_grad = lax.optimization_barrier(jnp.sum(grad_norm, 1, keepdims=True)) / channels
    sum_cross = lax.optimization_barrier(jnp.sum(grad_norm * normed, 1, keepdims=True)) / channels
    grad_mixed = (inv_std * (grad_norm - sum_grad - normed * sum_cross)).astype(jnp.bfloat16)
    grad_w_out = jnp.dot(att_grid.T, grad_mixed, preferred_element_type=jnp.float32).astype(jnp.bfloat16)
    grad_att = jnp.dot(grad_mixed, w_out.T, preferred_element_type=jnp.float32).astype(jnp.bfloat16)
    stacked, table_terms, grad_scale = window_backward(grad_att.reshape(extent_a, extent_b, heads_all, head_size), saved, log_scale, bias_sig)
    flat_terms = table_terms.transpose(1, 2, 0).reshape(-1, heads_all)
    grad_table = jnp.zeros((bias_table.shape[0], heads_all), jnp.float32).at[bias_index.reshape(-1)].add(flat_terms)
    grad_shifted = jnp.dot(stacked.reshape(-1, 3 * att_width), w_flat.T, preferred_element_type=jnp.float32)
    grad_shifted = grad_shifted.reshape(extent_a, extent_b, channels)
    grad_fields = (cotangent.astype(jnp.float32) + jnp.roll(grad_shifted, (SHIFT, SHIFT), (0, 1))).astype(jnp.bfloat16)
    return (block_out, grad_fields, grad_w_out, grad_table, grad_scale, grad_gain, grad_shift)
```

```python
import jax
import jax.numpy as jnp
from jax import lax
from jax.experimental import pallas as pl
from jax.experimental.pallas import tpu as pltpu
from jax.sharding import PartitionSpec as P

MESH = pl.DeviceIdType.MESH
BF = jnp.bfloat16
F32 = jnp.float32

CH = 1536
SH = 384
HEADS = 3
HD = 64
AW = HEADS * HD
CELLS = 64
NWIN = 4
GROUPS = 2
WIN = 8
TABLE = 256
NPAIR = 4096

SLOTS = {}
COUNT = 0
for _name, _n in (
    ("halo_f", 5), ("halo_c", 5), ("fields", 16), ("wcol_z", 3), ("wcol_p", 15), ("att", 8), ("stat", 6),
    ("gatt", 8), ("gsh", 8), ("out_f", 5), ("out_g", 5), ("w_core", 1), ("w_p", 15), ("w_z", 16),
    ("w_zs", 8), ("back_p", 15), ("back_core", 12), ("s_p", 15), ("s_l", 7),
):
    SLOTS[_name] = COUNT
    COUNT += _n

PLANE = [(dy, dx) for dy in range(4) for dx in range(4)][1:]


def nn(a, b):
    return lax.dot_general(a, b, (((1,), (0,)), ((), ())), preferred_element_type=F32)


def nt(a, b):
    return lax.dot_general(a, b, (((1,), (1,)), ((), ())), preferred_element_type=F32)


def tn(a, b):
    return lax.dot_general(a, b, (((0,), (0,)), ((), ())), preferred_element_type=F32)


def split3(value):
    high = value.astype(BF).astype(F32)
    middle = (value - high).astype(BF).astype(F32)
    return high, middle, value - high - middle


def swap_halves(first, second):
    low = lax.broadcasted_iota(jnp.int32, first.shape, 0) < 4
    return jnp.where(low, first, pltpu.roll(second, 4, 0)), jnp.where(low, pltpu.roll(first, 4, 0), second)


def cut_blocks(grid, blocks):
    for i in range(4):
        tiles = [[None, None] for _ in range(4)]
        for half in (0, 1):
            upper = grid[4 * i + 2 * half].astype(F32)
            lower = grid[4 * i + 2 * half + 1].astype(F32)
            for k in (0, 1):
                pair = swap_halves(upper[8 * k:8 * k + 8], lower[8 * k:8 * k + 8])
                tiles[2 * k][half], tiles[2 * k + 1][half] = pair
        for j in range(4):
            blocks[i, j] = jnp.concatenate(tiles[j], axis=0).astype(BF)


def join_blocks(blocks, grid):
    for i in range(4):
        for half in (0, 1):
            upper, lower = [], []
            for k in (0, 1):
                rows = slice(8 * half, 8 * half + 8)
                pair = swap_halves(blocks[i, 2 * k].astype(F32)[rows], blocks[i, 2 * k + 1].astype(F32)[rows])
                upper.append(pair[0])
                lower.append(pair[1])
            grid[4 * i + 2 * half] = jnp.concatenate(upper, axis=0).astype(BF)
            grid[4 * i + 2 * half + 1] = jnp.concatenate(lower, axis=0).astype(BF)


def write_kernel(blocks_f, blocks_g, weights, small, out_f, out_g, out_w, out_t, out_s, out_a, out_b):
    out_w[...] = weights[...]
    join_blocks(blocks_f, out_f)
    join_blocks(blocks_g, out_g)
    out_t[...] = small[2:2 + HEADS, 0:out_t.shape[1]]
    spare = small[2:2 + HEADS, TABLE - 1:TABLE]
    scales = jnp.transpose(jnp.concatenate([jnp.broadcast_to(spare, (HEADS, 128)), jnp.zeros((8 - HEADS, 128), F32)], axis=0))
    out_s[...] = scales[0:1, 0:HEADS].reshape(HEADS)
    out_a[...] = small[0]
    out_b[...] = small[1]


def whole_kernel(
    fields_grid, cot_grid, wt, wout, logs, table, index, mask, gain_ref, shift_ref,
    out_f, out_g, out_w, out_s,
    fields, cot, xbuf, cbuf, wcol, abuf, onehot, bsrow, idx_row, tab_pad, bsig, lab_col, qs, ks, vs, probs, coss, rqs, rks,
    mixed, stat_all, gmix, ga_send, ga_recv, ga_relay, gs_send, gs_recv, gs_relay, obuf, gobuf, tacc, sacc, gacc, flat,
    wc_send, wc_recv, wacc, wp_send, wp_recv, wp_sum, bz, sm_p, sm_l, local_sem, ssem, rsem,
):
    lat = lax.axis_index("lat")
    lon = lax.axis_index("lon")
    t = lax.axis_index("tp")
    zh = lat // 2
    core = lat % 2
    ly = lon // 4
    lx = lon % 4

    def ring(value, by, count):
        return lax.rem(value + by + count, count)

    lat_p, lat_n = ring(lat, -1, 8), ring(lat, 1, 8)
    lon_p, lon_n = ring(lon, -1, 16), ring(lon, 1, 16)
    sib = (zh * 2 + (1 - core), lon, t)

    def tp_dev(d):
        return (lat, lon, ring(t, d, 4))

    def plane(o):
        return ring(ly, PLANE[o][0], 4), ring(lx, PLANE[o][1], 4)

    def plane_from(o):
        return ring(ly, -PLANE[o][0], 4), ring(lx, -PLANE[o][1], 4)

    def plane_dev(o):
        y, x = plane(o)
        return (lat, y * 4 + x, t)

    def z_dev(d):
        return (ring(zh, d, 4) * 2 + core, lon, t)

    def copy(src, dst, slot, dev, send_slot=None):
        return pltpu.make_async_remote_copy(
            src_ref=src, dst_ref=dst, send_sem=ssem.at[slot if send_slot is None else send_slot],
            recv_sem=rsem.at[slot], device_id=dev, device_id_type=MESH,
        )

    def send(src, dst, slot, dev, send_slot=None):
        copy(src, dst, slot, dev, send_slot).start()

    def got(dst, slot):
        copy(dst, dst, slot, sib).wait_recv()

    def sent(src, slot):
        copy(src, src, slot, sib).wait_send()

    partners = [plane_dev(o) for o in range(15)] + [(ring(lat, d, 8), lon, t) for d in range(1, 8)]
    partners += [(lat_p, lon_p, t), (lat_n, lon_n, t)] + [tp_dev(d) for d in (1, 2, 3)]
    partners += [(ring(zh, dz, 4) * 2 + core, lon, ring(t, dt, 4)) for dz in (1, 2, 3) for dt in (1, 2, 3)]
    barrier = pltpu.get_barrier_semaphore()
    for dev in partners:
        pl.semaphore_signal(barrier, inc=1, device_id=dev, device_id_type=MESH)

    own = []

    def keep(src, dst):
        own.append(pltpu.make_async_copy(src, dst, local_sem.at[len(own)]))
        own[-1].start()

    def keep_grid(grid, dst):
        keep(grid.at[1:3, 1:3], dst.at[0])
        keep(grid.at[1:3, 3], dst.at[1, :, 0])
        keep(grid.at[3, 1:3], dst.at[2, 0])
        keep(grid.at[3, 3], dst.at[3, 0, 0])

    x_own = xbuf.at[t]
    cut_blocks(fields_grid, fields)
    keep_grid(fields, x_own)

    pl.semaphore_wait(barrier, len(partners))

    def halo(grid, dst, base):
        send(grid.at[1:3, 0], dst.at[1, :, 1], base, (lat, lon_p, t))
        send(grid.at[0, 1:3], dst.at[2, 1], base + 1, (lat_p, lon, t))
        send(grid.at[3, 0], dst.at[3, 0, 1], base + 2, (lat, lon_p, t))
        send(grid.at[0, 3], dst.at[3, 1, 0], base + 3, (lat_p, lon, t))
        send(grid.at[0, 0], dst.at[3, 1, 1], base + 4, (lat_p, lon_p, t))

    def halo_parts(dst):
        return [dst.at[1, :, 1], dst.at[2, 1], dst.at[3, 0, 1], dst.at[3, 1, 0], dst.at[3, 1, 1]]

    side = t // 2
    is_mid = (t == 1) | (t == 2)
    is_edge = jnp.logical_not(is_mid)
    partner = 2 * side + 1 - t % 2
    far_mid = 2 - side
    far_edge = 3 - 3 * side
    far_slot = jnp.where(is_mid, 1, 2)

    def on_line(where):
        return (lat, lon, where)

    def spread_start(name, n, src, dst, i):
        base = SLOTS[name] + i
        send(src, dst, base + n * far_slot, on_line(far_mid), base + n)

        @pl.when(is_mid)
        def _():
            send(src, dst, base + n, on_line(far_edge), base + 2 * n)

        send(src, dst, base, on_line(partner), base)

    def spread_relay(name, n, buf, i):
        base = SLOTS[name] + i

        @pl.when(is_mid)
        def _():
            chunk = buf.at[far_edge, i]
            got(chunk, base + 2 * n)
            send(chunk, chunk, base + 2 * n, on_line(partner), base + 3 * n)

    def spread_wait(name, n, buf, i):
        base = SLOTS[name] + i
        got(buf.at[partner, i], base)
        got(buf.at[far_mid, i], base + n)

        @pl.when(is_edge)
        def _():
            got(buf.at[far_edge, i], base + 2 * n)

    def spread_drain(name, n, chunk, i):
        base = SLOTS[name] + i
        sent(chunk, base)
        sent(chunk, base + n)

        @pl.when(is_mid)
        def _():
            sent(chunk, base + 2 * n)
            sent(chunk, base + 3 * n)

    def sum_start(name, part, recv, relay, g):
        base = SLOTS[name] + g

        @pl.when(is_edge)
        def _():
            send(part.at[far_edge, g], relay.at[g], base + 6, on_line(partner), base + 4)

        send(part.at[far_mid, g], recv.at[t, g], base + 2 * far_slot, on_line(far_mid), base + 2)
        send(part.at[partner, g], recv.at[t, g], base, on_line(partner), base)

    def sum_relay(name, part, recv, relay, g):
        base = SLOTS[name] + g

        @pl.when(is_mid)
        def _():
            got(relay.at[g], base + 6)
            part[far_edge, g] = (part[far_edge, g].astype(F32) + relay[g].astype(F32)).astype(BF)
            send(part.at[far_edge, g], recv.at[t, g], base + 2, on_line(far_edge), base + 4)

    def sum_end(name, part, recv, g):
        base = SLOTS[name] + g
        got(recv.at[partner, g], base)
        got(recv.at[far_mid, g], base + 2)

        @pl.when(is_mid)
        def _():
            got(recv.at[far_edge, g], base + 4)

        @pl.when(is_edge)
        def _():
            recv[far_edge, g] = jnp.zeros(recv.shape[2:], BF)

        total = part[t, g].astype(F32)
        for src in (partner, far_mid, far_edge):
            total = total + recv[src, g].astype(F32)
        return total

    def give_fields(w, src):
        spread_start("fields", 4, src, x_own.at[w], w)

    halo(fields, x_own, SLOTS["halo_f"])

    piece_rows = pl.ds(pl.multiple_of(lx * 48, 16), 48)
    has_piece = ly < 3

    def piece(y, x):
        rows = pl.ds(pl.multiple_of(x * 48, 16), 48)
        return wcol.at[1:4, rows, pl.ds(pl.multiple_of(y * 128, 128), 128)]

    @pl.when(has_piece)
    def _():
        for d in (1, 2, 3):
            cols = pl.ds(pl.multiple_of(ring(t, d, 4) * SH + ly * 128, 128), 128)
            here = pl.ds(pl.multiple_of(ly * 128, 128), 128)
            send(wout.at[piece_rows, cols], wcol.at[d, piece_rows, here], SLOTS["wcol_z"] + d - 1, tp_dev(d))

    give_fields(0, fields.at[1:3, 1:3])
    cut_blocks(cot_grid, cot)
    keep_grid(cot, cbuf)
    keep(wout.at[:, pl.ds(pl.multiple_of(t * SH, 128), SH)], wcol.at[0])

    def place(n):
        a, b, c, d = (n >> 5) & 1, (n >> 4) & 1, (n >> 2) & 3, n & 3
        return 4 * a + c, 4 * b + d

    def iota(shape, dim):
        return lax.broadcasted_iota(jnp.int32, shape, dim)

    def hot(flag):
        return jnp.where(flag, 1.0, 0.0)

    row_of, col_of = place(iota((CELLS, CELLS), 0))
    order = hot(iota((CELLS, CELLS), 1) == row_of * WIN + col_of).astype(BF)
    swapped = nn(order, index[...].astype(F32).astype(BF)).astype(BF)
    idx = nt(swapped, order)
    for c in range(NPAIR // 128):
        idx_row[0:1, c * 128:(c + 1) * 128] = jnp.concatenate([idx[2 * c:2 * c + 1], idx[2 * c + 1:2 * c + 2]], axis=1)

    cell = iota((NWIN * CELLS, 16), 0)
    row_of, col_of = place(cell)
    row_of, col_of = row_of + WIN * (cell >> 7), col_of + WIN * ((cell >> 6) & 1)
    picked_rows = nn(hot(iota((NWIN * CELLS, 16), 1) == row_of).astype(BF), mask[...].astype(F32).astype(BF))
    labels = jnp.sum(hot(iota((NWIN * CELLS, 16), 1) == col_of) * picked_rows, axis=1, keepdims=True)
    lab_col[...] = labels + 4.0 * (iota((NWIN * CELLS, 1), 0) >> 6).astype(F32)

    own[1].wait()
    got(halo_parts(x_own)[0], SLOTS["halo_f"])
    give_fields(1, x_own.at[1])
    own[2].wait()
    got(halo_parts(x_own)[1], SLOTS["halo_f"] + 1)
    give_fields(2, x_own.at[2])
    own[3].wait()
    for part in (2, 3, 4):
        got(halo_parts(x_own)[part], SLOTS["halo_f"] + part)
    give_fields(3, x_own.at[3])

    @pl.when(has_piece)
    def _():
        for d in (1, 2, 3):
            here = pl.ds(pl.multiple_of(ly * 128, 128), 128)
            got(wcol.at[d, piece_rows, here], SLOTS["wcol_z"] + d - 1)
        for o in range(15):
            send(piece(ly, lx), piece(ly, lx), SLOTS["wcol_p"] + o, plane_dev(o))

    halo(cot, cbuf, SLOTS["halo_c"])

    tab_pad[...] = jnp.zeros_like(tab_pad)
    tab_pad[0:HEADS, 0:table.shape[1]] = table[...]
    tab = jnp.concatenate([*split3(tab_pad[...]), jnp.zeros((8, TABLE), F32)], axis=0).astype(BF)
    entry = iota((TABLE, 512), 0).astype(F32)
    for c in range(NPAIR // 512):
        span = slice(c * 512, (c + 1) * 512)
        picked = hot(entry == idx_row[0:1, span]).astype(BF)
        onehot[:, span] = picked
        parts = nn(tab, picked)
        bias = parts[0:8] + parts[8:16] + parts[16:24]
        sig = 1.0 / (1.0 + jnp.exp(-bias))
        bsrow[:, span] = sig
        for k in range(8):
            for h in range(HEADS):
                at = 8 * c + k
                pair = jnp.concatenate([16.0 * sig[h:h + 1, k * CELLS:(k + 1) * CELLS]] * 2, axis=1)
                bsig[h, at:at + 1, :] = pair
                bsig[h, CELLS + at:CELLS + at + 1, :] = pair
    tacc[...] = jnp.zeros_like(tacc)
    sacc[...] = jnp.zeros_like(sacc)
    gacc[...] = jnp.zeros_like(gacc)
    scales = jnp.exp(logs[...])

    own[0].wait()

    eye = iota((2 * CELLS, 2 * CELLS), 0) == iota((2 * CELLS, 2 * CELLS), 1)

    def forward(g):
        for w in (2 * g, 2 * g + 1):
            spread_relay("fields", 4, xbuf, w)
        for w in (2 * g, 2 * g + 1):
            spread_wait("fields", 4, xbuf, w)
        proj = jnp.zeros((2 * CELLS, 3 * AW), F32)
        for src in range(4):
            proj = proj + nt(xbuf[src, 2 * g:2 * g + 2].reshape(2 * CELLS, SH), wt[:, src * SH:(src + 1) * SH])
        column = lab_col[2 * g * CELLS:2 * (g + 1) * CELLS]
        row = jnp.sum(jnp.where(eye, column, 0.0), axis=0, keepdims=True)
        same = row == column
        heads = range(HEADS)

        def slot(kind, h):
            at = kind * AW + h * HD
            return proj[:, at:at + HD]

        q = [slot(0, h) for h in heads]
        k = [slot(1, h) for h in heads]
        v = [slot(2, h).astype(BF) for h in heads]
        rq = [lax.rsqrt(jnp.sum(q[h] * q[h], axis=1, keepdims=True) + 1e-06) for h in heads]
        rk = [lax.rsqrt(jnp.sum(k[h] * k[h], axis=1, keepdims=True) + 1e-06) for h in heads]
        q_hat = [(q[h] * rq[h]).astype(BF) for h in heads]
        k_hat = [(k[h] * rk[h]).astype(BF) for h in heads]
        cosine = [nt(q_hat[h], k_hat[h]) for h in heads]
        power = [scales[:, h:h + 1] * (cosine[h] - 1.0) + (bsig[h] - 16.0) for h in heads]
        weight = [jnp.where(same, jnp.exp(power[h]), 0.0) for h in heads]
        total = [jnp.sum(weight[h], axis=1, keepdims=True) for h in heads]
        prob = [(weight[h] * (1.0 / total[h])).astype(BF) for h in heads]
        attended = [nn(prob[h], v[h]).astype(BF) for h in heads]
        for i in (0, 1):
            for h in heads:
                at = i * AW + h * HD
                abuf[t, g, :, at:at + HD] = attended[h][i * CELLS:(i + 1) * CELLS]
        for h in heads:
            qs[g, h] = q_hat[h]
            ks[g, h] = k_hat[h]
            vs[g, h] = v[h]
            probs[g, h] = prob[h]
            coss[g, h] = cosine[h]
            rqs[g, h] = rq[h]
            rks[g, h] = rk[h]
        spread_start("att", 2, abuf.at[t, g], abuf.at[t, g], g)

    gain = gain_ref[...].reshape(1, SH)
    shift = shift_ref[...].reshape(1, SH)
    lane = iota((2 * CELLS, 128), 1)

    def unpack(pair):
        return jnp.concatenate([pair[:, :AW], pair[:, AW:]], axis=0)

    def cells_of(buf, g):
        return buf[2 * g:2 * g + 2].reshape(2 * CELLS, SH).astype(F32)

    def mix(g):
        spread_relay("att", 2, abuf, g)
        spread_wait("att", 2, abuf, g)
        total = jnp.zeros((2 * CELLS, SH), F32)
        for d in range(4):
            total = total + nn(unpack(abuf[ring(t, -d, 4), g]), wcol[d])
        mixed[g] = total
        grad_norm = cells_of(cbuf, g) * gain
        packed = jnp.zeros((2 * CELLS, 128), F32)
        for i, v in enumerate((total, total * total, grad_norm, grad_norm * total)):
            packed = jnp.where(lane == i, jnp.sum(v, axis=1, keepdims=True), packed)
        stat_all[t, g] = jnp.transpose(packed)[0:8]
        mine = stat_all.at[t, g]
        for d in (1, 2, 3):
            send(mine, mine, SLOTS["stat"] + (d - 1) * 2 + g, tp_dev(d))

    def normalise(g):
        for d in (1, 2, 3):
            got(stat_all.at[ring(t, -d, 4), g], SLOTS["stat"] + (d - 1) * 2 + g)
        totals = stat_all[0, g] + stat_all[1, g] + stat_all[2, g] + stat_all[3, g]
        packed = jnp.transpose(jnp.concatenate([totals, jnp.zeros((120, 128), F32)], axis=0))
        mean = packed[:, 0:1] / CH
        variance = packed[:, 1:2] / CH - mean * mean
        inv_std = 1.0 / jnp.sqrt(variance + 1e-05)
        grad_mean = packed[:, 2:3] / CH
        cross_mean = inv_std * (packed[:, 3:4] - mean * packed[:, 2:3]) / CH
        normed = (mixed[g] - mean) * inv_std
        rows = cells_of(cbuf, g)
        grad = (inv_std * (rows * gain - grad_mean - normed * cross_mean)).astype(BF)
        gmix[g] = grad
        for d in (2, 1, 3, 0):
            dst = ring(t, d, 4)
            part = nt(grad, wcol[(4 - d) % 4])
            ga_send[dst, g] = jnp.concatenate([part[:CELLS], part[CELLS:]], axis=1).astype(BF)
        sum_start("gatt", ga_send, ga_recv, ga_relay, g)
        base = xbuf[t, 2 * g:2 * g + 2].reshape(2 * CELLS, SH).astype(F32)
        obuf[2 * g:2 * g + 2] = (base + (gain * normed + shift)).astype(BF).reshape(2, 2, 2, 16, SH)
        gacc[0:1, :] += jnp.sum(rows * normed, axis=0, keepdims=True)
        gacc[1:2, :] += jnp.sum(rows, axis=0, keepdims=True)

    def backward(g):
        total = sum_end("gatt", ga_send, ga_recv, g)
        grad_att = unpack(total.astype(BF))
        heads = range(HEADS)
        ga = [grad_att[:, h * HD:(h + 1) * HD] for h in heads]
        prob = [probs[g, h] for h in heads]
        q_hat = [qs[g, h] for h in heads]
        k_hat = [ks[g, h] for h in heads]
        grad_prob = [nt(ga[h], vs[g, h]) for h in heads]
        grads_v = [tn(prob[h], ga[h]) for h in heads]
        prob_f = [prob[h].astype(F32) for h in heads]
        inner = [jnp.sum(prob_f[h] * grad_prob[h], axis=1, keepdims=True) for h in heads]
        grad_logit = [prob_f[h] * (grad_prob[h] - inner[h]) for h in heads]
        grad_cos = [(grad_logit[h] * scales[:, h:h + 1]).astype(BF) for h in heads]
        gq = [nn(grad_cos[h], k_hat[h]) for h in heads]
        gk = [tn(grad_cos[h], q_hat[h]) for h in heads]
        for h in heads:
            tacc[h] += grad_logit[h]
            sacc[h] += grad_logit[h] * coss[g, h]
        q_float = [q_hat[h].astype(F32) for h in heads]
        k_float = [k_hat[h].astype(F32) for h in heads]
        q_in = [jnp.sum(q_float[h] * gq[h], axis=1, keepdims=True) for h in heads]
        k_in = [jnp.sum(k_float[h] * gk[h], axis=1, keepdims=True) for h in heads]
        grads_q = [(gq[h] - q_float[h] * q_in[h]) * rqs[g, h] for h in heads]
        grads_k = [(gk[h] - k_float[h] * k_in[h]) * rks[g, h] for h in heads]
        stacked = jnp.concatenate(grads_q + grads_k + grads_v, axis=1).astype(BF)
        for d in (2, 1, 3, 0):
            dst = ring(t, d, 4)
            gs_send[dst, g] = nn(stacked, wt[:, pl.ds(pl.multiple_of(dst * SH, 128), SH)]).astype(BF)
        sum_start("gsh", gs_send, gs_recv, gs_relay, g)

    def finish(g):
        total = sum_end("gsh", gs_send, gs_recv, g) + cells_of(cbuf, g)
        gobuf[2 * g:2 * g + 2] = total.astype(BF).reshape(2, 2, 2, 16, SH)

    def give_first(buf, out, base):
        out[1:3, 1:3] = buf[0]
        out[1:3, 3] = buf[1, :, 0]
        send(buf.at[1, :, 1], out.at[1:3, 0], base, (lat, lon_n, t))

    def give_second(buf, out, base):
        send(buf.at[2, 1], out.at[0, 1:3], base + 1, (lat_n, lon, t))
        send(buf.at[3, 0, 1], out.at[3, 0], base + 2, (lat, lon_n, t))
        send(buf.at[3, 1, 0], out.at[0, 3], base + 3, (lat_n, lon, t))
        send(buf.at[3, 1, 1], out.at[0, 0], base + 4, (lat_n, lon_n, t))
        out[3, 1:3] = buf[2, 0]
        out[3, 3] = buf[3, 0, 0]

    def back_parts(out):
        return [out.at[1:3, 0], out.at[0, 1:3], out.at[3, 0], out.at[0, 3], out.at[0, 0]]

    def weight_first():
        for group in range(4):
            wacc[group] = tn(unpack(abuf[group, 0]), gmix[0])

    def weight_start():
        for j in (0, 1):
            far = 2 * (1 - core) + j
            wc_send[j] = (wacc[far] + tn(unpack(abuf[far, 1]), gmix[1])).astype(BF)
        send(wc_send, wc_recv, SLOTS["w_core"], sib)
        for j in (0, 1):
            near = 2 * core + j
            wacc[near] = wacc[near] + tn(unpack(abuf[near, 1]), gmix[1])

    def rows_of(y, x):
        return pl.ds(pl.multiple_of(x * 48 + y * 16, 16), 16)

    def weight_plane():
        got(wc_recv, SLOTS["w_core"])
        for j in (0, 1):
            total = wacc[2 * core + j] + wc_recv[j].astype(F32)
            wacc[2 * core + j] = total
            wp_send[j] = total.astype(BF)
        for o in range(15):
            y, x = plane(o)

            @pl.when(y < 3)
            def _():
                send(wp_send.at[:, rows_of(y, x)], wp_recv.at[o], SLOTS["w_p"] + o, plane_dev(o))

    holder = t // 2 == core

    def weight_z():
        @pl.when(has_piece)
        def _():
            for o in range(15):
                got(wp_recv.at[o], SLOTS["w_p"] + o)
            for j in (0, 1):
                total = wacc[2 * core + j, rows_of(ly, lx), :]
                for o in range(15):
                    total = total + wp_recv[o, j].astype(F32)
                wp_sum[j] = total.astype(BF)
            for j in (0, 1):
                keeper = 2 * core + j
                for dz in range(4):
                    @pl.when((keeper != t) if dz == 0 else (keeper >= 0))
                    def _():
                        dev = (ring(zh, dz, 4) * 2 + core, lon, keeper)
                        send(wp_sum.at[j], bz.at[zh, t], SLOTS["w_z"] + zh * 4 + t, dev, SLOTS["w_zs"] + 4 * j + dz)

    def weight_back_plane():
        @pl.when(holder & has_piece)
        def _():
            bz[zh, t] = wp_sum[t % 2]
            for z in range(4):
                for src in range(4):
                    @pl.when((zh != z) | (t != src))
                    def _():
                        got(bz.at[z, src], SLOTS["w_z"] + z * 4 + src)

            for src in range(4):
                total = bz[0, src].astype(F32)
                for z in range(1, 4):
                    total = total + bz[z, src].astype(F32)
                out_w[rows_of(ly, lx), src * SH:(src + 1) * SH] = total.astype(BF)
            mine = out_w.at[rows_of(ly, lx)]
            for o in range(15):
                send(mine, mine, SLOTS["back_p"] + o, plane_dev(o))
            send(mine, mine, SLOTS["back_core"] + lx * 3 + ly, sib)

    def weight_back_core():
        @pl.when(holder)
        def _():
            for o in range(15):
                y, x = plane_from(o)

                @pl.when(y < 3)
                def _():
                    mine = out_w.at[rows_of(y, x)]
                    got(mine, SLOTS["back_p"] + o)
                    send(mine, mine, SLOTS["back_core"] + x * 3 + y, sib)

    def small_start():
        folded_t = [tacc[h, :CELLS, :CELLS] + tacc[h, CELLS:, CELLS:] for h in range(HEADS)]
        for c in range(NPAIR // 128):
            for h in range(HEADS):
                pair = [folded_t[h][2 * c + i:2 * c + i + 1, :] for i in (0, 1)]
                flat[h:h + 1, c * 128:(c + 1) * 128] = jnp.concatenate(pair, axis=1)
        spread = bsrow[0:HEADS, :]
        terms = flat[0:HEADS, :] * 16.0 * spread * (1.0 - spread)
        pad = jnp.zeros((8 - HEADS, NPAIR), F32)
        pieces = jnp.concatenate([v for p in split3(terms) for v in (p, pad)], axis=0).astype(BF)
        folded = nt(pieces, onehot[...])
        sm_p[lon] = folded[0:8] + folded[8:16] + folded[16:24]
        for h in range(HEADS):
            amount = jnp.sum(jnp.sum(sacc[h], axis=1, keepdims=True), axis=0, keepdims=True) * scales[:, h:h + 1]
            sm_p[lon, h:h + 1, TABLE - 1:TABLE] = amount
        sm_p[lon, 3:5, :] = gacc[0:2, 0:TABLE]
        sm_p[lon, 5:6, :] = jnp.concatenate([gacc[0:1, TABLE:SH], gacc[1:2, TABLE:SH]], axis=1)
        for o in range(15):
            send(sm_p.at[lon], sm_p.at[lon], SLOTS["s_p"] + o, plane_dev(o))

    def small_lat():
        for o in range(15):
            y, x = plane_from(o)
            got(sm_p.at[y * 4 + x], SLOTS["s_p"] + o)
        total = sm_p[0]
        for i in range(1, 16):
            total = total + sm_p[i]
        sm_l[lat] = total
        for d in range(1, 8):
            send(sm_l.at[lat], sm_l.at[lat], SLOTS["s_l"] + d - 1, (ring(lat, d, 8), lon, t))

    def small_end():
        for d in range(1, 8):
            got(sm_l.at[ring(lat, -d, 8)], SLOTS["s_l"] + d - 1)
        total = sm_l[0]
        for i in range(1, 8):
            total = total + sm_l[i]
        out_s[...] = jnp.zeros_like(out_s)
        out_s[0:2, 0:TABLE] = total[3:5]
        out_s[0:1, TABLE:SH] = total[5:6, 0:128]
        out_s[1:2, TABLE:SH] = total[5:6, 128:256]
        out_s[2:5, 0:TABLE] = total[0:3]

    forward(0)
    forward(1)
    own[8].wait()
    for o in range(15):
        y, x = plane_from(o)

        @pl.when(y < 3)
        def _():
            got(piece(y, x), SLOTS["wcol_p"] + o)

    for i in (4, 5, 6, 7):
        own[i].wait()
    for i in range(5):
        got(halo_parts(cbuf)[i], SLOTS["halo_c"] + i)
    mix(0)
    normalise(0)
    mix(1)
    sum_relay("gatt", ga_send, ga_recv, ga_relay, 0)
    weight_first()
    normalise(1)
    weight_start()
    sum_relay("gatt", ga_send, ga_recv, ga_relay, 1)
    give_first(obuf, out_f, SLOTS["out_f"])
    give_second(obuf, out_f, SLOTS["out_f"])
    backward(0)
    weight_plane()
    backward(1)
    sum_relay("gsh", gs_send, gs_recv, gs_relay, 0)
    small_start()
    sum_relay("gsh", gs_send, gs_recv, gs_relay, 1)
    weight_z()
    finish(0)
    give_first(gobuf, out_g, SLOTS["out_g"])
    small_lat()
    weight_back_plane()
    finish(1)
    give_second(gobuf, out_g, SLOTS["out_g"])
    weight_back_core()
    small_end()

    for i in range(5):
        got(back_parts(out_f)[i], SLOTS["out_f"] + i)
        got(back_parts(out_g)[i], SLOTS["out_g"] + i)

    for base, parts in (("halo_f", halo_parts(x_own)), ("halo_c", halo_parts(cbuf)),
                        ("out_f", back_parts(out_f)), ("out_g", back_parts(out_g))):
        for i in range(5):
            sent(parts[i], SLOTS[base] + i)

    for w in range(NWIN):
        spread_drain("fields", 4, xbuf.at[0, 0], w)
    for g in range(GROUPS):
        spread_drain("att", 2, abuf.at[0, 0], g)
        for i in range(3):
            sent(stat_all.at[0, 0], SLOTS["stat"] + 2 * i + g)
            sent(ga_send.at[0, 0], SLOTS["gatt"] + 2 * i + g)
            sent(gs_send.at[0, 0], SLOTS["gsh"] + 2 * i + g)

    @pl.when(has_piece)
    def _():
        for d in range(3):
            sent(wcol.at[0, 0:48, 0:128], SLOTS["wcol_z"] + d)
            for j in (0, 1):
                sent(wp_sum.at[j], SLOTS["w_zs"] + 4 * j + d + 1)
        for o in range(15):
            sent(wcol.at[1:4, 0:48, 0:128], SLOTS["wcol_p"] + o)

        for j in (0, 1):
            @pl.when(2 * core + j != t)
            def _():
                sent(wp_sum.at[j], SLOTS["w_zs"] + 4 * j)

    @pl.when(holder & has_piece)
    def _():
        for o in range(15):
            sent(out_w.at[0:16], SLOTS["back_p"] + o)
        sent(out_w.at[0:16], SLOTS["back_core"] + lx * 3 + ly)

    for o in range(15):
        sent(sm_p.at[0], SLOTS["s_p"] + o)

        @pl.when(plane(o)[0] < 3)
        def _():
            sent(wp_send.at[:, 0:16], SLOTS["w_p"] + o)

        @pl.when(holder & (plane_from(o)[0] < 3))
        def _():
            y, x = plane_from(o)
            sent(out_w.at[0:16], SLOTS["back_core"] + x * 3 + y)

    for d in range(7):
        sent(sm_l.at[0], SLOTS["s_l"] + d)
    sent(wc_send, SLOTS["w_core"])

    @pl.when(jnp.logical_not(holder))
    def _():
        for x in range(4):
            for y in range(3):
                got(out_w.at[x * 48 + y * 16:x * 48 + y * 16 + 16], SLOTS["back_core"] + x * 3 + y)


def per_device(
    fields, w_qkv, w_out, log_scale, bias_table, bias_index, mask_ids, norm_gain, norm_shift, cotangent
):
    rows = bias_table.shape[0]
    wt = w_qkv.transpose(1, 2, 0).reshape(3 * AW, CH)
    hbm = pl.BlockSpec(memory_space=pltpu.HBM)
    vmem = pl.BlockSpec(memory_space=pltpu.VMEM)
    scratch = [
        ((4, 4, 16, SH), BF), ((4, 4, 16, SH), BF), ((4, 4, 2, 2, 16, SH), BF), ((4, 2, 2, 16, SH), BF), ((4, AW, SH), BF),
        ((4, 2, CELLS, SH), BF), ((TABLE, NPAIR), BF), ((8, NPAIR), F32), ((8, NPAIR), F32), ((8, TABLE), F32),
        ((HEADS, 2 * CELLS, 2 * CELLS), F32), ((NWIN * CELLS, 1), F32),
        ((2, HEADS, 2 * CELLS, HD), BF), ((2, HEADS, 2 * CELLS, HD), BF), ((2, HEADS, 2 * CELLS, HD), BF),
        ((2, HEADS, 2 * CELLS, 2 * CELLS), BF), ((2, HEADS, 2 * CELLS, 2 * CELLS), F32),
        ((2, HEADS, 2 * CELLS, 1), F32), ((2, HEADS, 2 * CELLS, 1), F32),
        ((2, 2 * CELLS, SH), F32), ((4, 2, 8, 128), F32), ((2, 2 * CELLS, SH), BF),
        ((4, 2, CELLS, SH), BF), ((4, 2, CELLS, SH), BF), ((2, CELLS, SH), BF),
        ((4, 2, 2 * CELLS, SH), BF), ((4, 2, 2 * CELLS, SH), BF), ((2, 2 * CELLS, SH), BF),
        ((4, 2, 2, 16, SH), BF), ((4, 2, 2, 16, SH), BF),
        ((HEADS, 2 * CELLS, 2 * CELLS), F32), ((HEADS, 2 * CELLS, 2 * CELLS), F32), ((8, SH), F32), ((8, NPAIR), F32),
        ((2, AW, SH), BF), ((2, AW, SH), BF), ((4, AW, SH), F32),
        ((2, AW, SH), BF), ((15, 2, 16, SH), BF), ((2, 16, SH), BF), ((4, 4, 16, SH), BF),
        ((16, 8, TABLE), F32), ((8, 8, TABLE), F32),
    ]
    out_f, out_g, out_w, out_s = pl.pallas_call(
        whole_kernel,
        out_shape=(
            jax.ShapeDtypeStruct((4, 4, 16, SH), BF),
            jax.ShapeDtypeStruct((4, 4, 16, SH), BF),
            jax.ShapeDtypeStruct((AW, CH), BF),
            jax.ShapeDtypeStruct((8, SH), F32),
        ),
        in_specs=[vmem, vmem, vmem, hbm, vmem, vmem, vmem, vmem, vmem, vmem],
        out_specs=(vmem, vmem, vmem, vmem),
        scratch_shapes=[pltpu.VMEM(shape, kind) for shape, kind in scratch] + [
            pltpu.SemaphoreType.DMA((9,)),
            pltpu.SemaphoreType.DMA((COUNT,)),
            pltpu.SemaphoreType.DMA((COUNT,)),
        ],
        compiler_params=pltpu.CompilerParams(
            collective_id=0, has_side_effects=True, vmem_limit_bytes=40 * 1024 * 1024
        ),
        cost_estimate=pl.CostEstimate(flops=2_000_000_000, bytes_accessed=5_000_000, transcendentals=200_000),
    )(
        fields, cotangent, wt, w_out, log_scale.reshape(1, HEADS), bias_table.T, bias_index, mask_ids,
        norm_gain, norm_shift,
    )
    shapes = (
        (fields.shape, BF), (fields.shape, BF), ((AW, CH), BF), ((HEADS, rows), F32), ((HEADS,), F32),
        ((SH,), F32), ((SH,), F32),
    )
    block_out, grad_fields, grad_w_out, grad_table, grad_scale, grad_gain, grad_shift = pl.pallas_call(
        write_kernel,
        out_shape=tuple(jax.ShapeDtypeStruct(shape, kind) for shape, kind in shapes),
        in_specs=[vmem] * 4,
        out_specs=(vmem,) * 7,
        compiler_params=pltpu.CompilerParams(vmem_limit_bytes=16 * 1024 * 1024),
        cost_estimate=pl.CostEstimate(flops=1_000_000, bytes_accessed=2_000_000, transcendentals=0),
    )(out_f, out_g, out_w, out_s)
    return (block_out, grad_fields, grad_w_out, grad_table.T, grad_scale, grad_gain, grad_shift)


def solution(mesh):
    in_specs = (
        P("lat", "lon", "tp"), P(None, None, "tp"), P("tp", None), P("tp"), P(None, "tp"), P(),
        P("lat", "lon"), P("tp"), P("tp"), P("lat", "lon", "tp"),
    )
    out_specs = (
        P("lat", "lon", "tp"), P("lat", "lon", "tp"), P("tp", None), P(None, "tp"), P("tp"), P("tp"), P("tp"),
    )
    return jax.shard_map(per_device, mesh=mesh, in_specs=in_specs, out_specs=out_specs, check_vma=False)
```

```python
import jax
import jax.numpy as jnp
from jax import lax
from jax.experimental import pallas as pl
from jax.experimental.pallas import tpu as pltpu
from jax.sharding import PartitionSpec as P

MESH = pl.DeviceIdType.MESH
BF = jnp.bfloat16
F32 = jnp.float32

CH = 1536
SH = 384
HEADS = 3
HD = 64
AW = HEADS * HD
CELLS = 64
NWIN = 4
GROUPS = 2
WIN = 8
TABLE = 256
NPAIR = 4096

SLOTS = {}
COUNT = 0
for _name, _n in (
    ("halo_f", 5), ("halo_c", 5), ("fields", 16), ("wcol_z", 3), ("wcol_p", 15), ("att", 8), ("stat", 6),
    ("gatt", 8), ("gsh", 8), ("out_f", 5), ("out_g", 5), ("w_core", 1), ("w_p", 15), ("w_z", 16),
    ("w_zs", 8), ("back_p", 15), ("back_core", 12), ("s_p", 15), ("s_l", 7),
):
    SLOTS[_name] = COUNT
    COUNT += _n

PLANE = [(dy, dx) for dy in range(4) for dx in range(4)][1:]


def nn(a, b):
    return lax.dot_general(a, b, (((1,), (0,)), ((), ())), preferred_element_type=F32)


def nt(a, b):
    return lax.dot_general(a, b, (((1,), (1,)), ((), ())), preferred_element_type=F32)


def tn(a, b):
    return lax.dot_general(a, b, (((0,), (0,)), ((), ())), preferred_element_type=F32)


def split3(value):
    high = value.astype(BF).astype(F32)
    middle = (value - high).astype(BF).astype(F32)
    return high, middle, value - high - middle


def swap_halves(first, second):
    low = lax.broadcasted_iota(jnp.int32, first.shape, 0) < 4
    return jnp.where(low, first, pltpu.roll(second, 4, 0)), jnp.where(low, pltpu.roll(first, 4, 0), second)


def cut_blocks(grid, blocks):
    for i in range(4):
        tiles = [[None, None] for _ in range(4)]
        for half in (0, 1):
            upper = grid[4 * i + 2 * half].astype(F32)
            lower = grid[4 * i + 2 * half + 1].astype(F32)
            for k in (0, 1):
                pair = swap_halves(upper[8 * k:8 * k + 8], lower[8 * k:8 * k + 8])
                tiles[2 * k][half], tiles[2 * k + 1][half] = pair
        for j in range(4):
            blocks[i, j] = jnp.concatenate(tiles[j], axis=0).astype(BF)


def join_blocks(blocks, grid):
    for i in range(4):
        for half in (0, 1):
            upper, lower = [], []
            for k in (0, 1):
                rows = slice(8 * half, 8 * half + 8)
                pair = swap_halves(blocks[i, 2 * k].astype(F32)[rows], blocks[i, 2 * k + 1].astype(F32)[rows])
                upper.append(pair[0])
                lower.append(pair[1])
            grid[4 * i + 2 * half] = jnp.concatenate(upper, axis=0).astype(BF)
            grid[4 * i + 2 * half + 1] = jnp.concatenate(lower, axis=0).astype(BF)


def write_kernel(blocks_f, blocks_g, weights, small, out_f, out_g, out_w, out_t, out_s, out_a, out_b):
    out_w[...] = weights[...]
    join_blocks(blocks_f, out_f)
    join_blocks(blocks_g, out_g)
    out_t[...] = small[2:2 + HEADS, 0:out_t.shape[1]]
    spare = small[2:2 + HEADS, TABLE - 1:TABLE]
    scales = jnp.transpose(jnp.concatenate([jnp.broadcast_to(spare, (HEADS, 128)), jnp.zeros((8 - HEADS, 128), F32)], axis=0))
    out_s[...] = scales[0:1, 0:HEADS].reshape(HEADS)
    out_a[...] = small[0]
    out_b[...] = small[1]


def whole_kernel(
    fields_hbm, cot_hbm, wt_hbm, wout, logs, table, index, mask, gain_ref, shift_ref,
    out_f, out_g, out_w, out_s,
    fields_grid, cot_grid, wt, fields, cot, xbuf, cbuf, wcol, abuf, onehot, bsrow, idx_row, tab_pad, bsig, lab_col, qs, ks, vs, probs, coss, rqs, rks,
    mixed, stat_all, gmix, ga_send, ga_recv, ga_relay, gs_send, gs_recv, gs_relay, obuf, gobuf, tacc, sacc, gacc, flat,
    wc_send, wc_recv, wacc, wp_send, wp_recv, wp_sum, bz, sm_p, sm_l, local_sem, ssem, rsem,
):
    lat = lax.axis_index("lat")
    lon = lax.axis_index("lon")
    t = lax.axis_index("tp")
    zh = lat // 2
    core = lat % 2
    ly = lon // 4
    lx = lon % 4

    def ring(value, by, count):
        return lax.rem(value + by + count, count)

    lat_p, lat_n = ring(lat, -1, 8), ring(lat, 1, 8)
    lon_p, lon_n = ring(lon, -1, 16), ring(lon, 1, 16)
    sib = (zh * 2 + (1 - core), lon, t)

    def tp_dev(d):
        return (lat, lon, ring(t, d, 4))

    def plane(o):
        return ring(ly, PLANE[o][0], 4), ring(lx, PLANE[o][1], 4)

    def plane_from(o):
        return ring(ly, -PLANE[o][0], 4), ring(lx, -PLANE[o][1], 4)

    def plane_dev(o):
        y, x = plane(o)
        return (lat, y * 4 + x, t)

    def z_dev(d):
        return (ring(zh, d, 4) * 2 + core, lon, t)

    def copy(src, dst, slot, dev, send_slot=None):
        return pltpu.make_async_remote_copy(
            src_ref=src, dst_ref=dst, send_sem=ssem.at[slot if send_slot is None else send_slot],
            recv_sem=rsem.at[slot], device_id=dev, device_id_type=MESH,
        )

    def send(src, dst, slot, dev, send_slot=None):
        copy(src, dst, slot, dev, send_slot).start()

    def got(dst, slot):
        copy(dst, dst, slot, sib).wait_recv()

    def sent(src, slot):
        copy(src, src, slot, sib).wait_send()

    own = []

    def keep(src, dst):
        own.append(pltpu.make_async_copy(src, dst, local_sem.at[len(own)]))
        own[-1].start()

    keep(fields_hbm, fields_grid)
    keep(cot_hbm, cot_grid)
    keep(wt_hbm, wt)

    partners = [plane_dev(o) for o in range(15)] + [(ring(lat, d, 8), lon, t) for d in range(1, 8)]
    partners += [(lat_p, lon_p, t), (lat_n, lon_n, t)] + [tp_dev(d) for d in (1, 2, 3)]
    partners += [(ring(zh, dz, 4) * 2 + core, lon, ring(t, dt, 4)) for dz in (1, 2, 3) for dt in (1, 2, 3)]
    barrier = pltpu.get_barrier_semaphore()
    for dev in partners:
        pl.semaphore_signal(barrier, inc=1, device_id=dev, device_id_type=MESH)

    def keep_grid(grid, dst):
        keep(grid.at[1:3, 1:3], dst.at[0])
        keep(grid.at[1:3, 3], dst.at[1, :, 0])
        keep(grid.at[3, 1:3], dst.at[2, 0])
        keep(grid.at[3, 3], dst.at[3, 0, 0])

    x_own = xbuf.at[t]
    own[0].wait()
    cut_blocks(fields_grid, fields)
    keep_grid(fields, x_own)

    pl.semaphore_wait(barrier, len(partners))

    def halo(grid, dst, base):
        send(grid.at[1:3, 0], dst.at[1, :, 1], base, (lat, lon_p, t))
        send(grid.at[0, 1:3], dst.at[2, 1], base + 1, (lat_p, lon, t))
        send(grid.at[3, 0], dst.at[3, 0, 1], base + 2, (lat, lon_p, t))
        send(grid.at[0, 3], dst.at[3, 1, 0], base + 3, (lat_p, lon, t))
        send(grid.at[0, 0], dst.at[3, 1, 1], base + 4, (lat_p, lon_p, t))

    def halo_parts(dst):
        return [dst.at[1, :, 1], dst.at[2, 1], dst.at[3, 0, 1], dst.at[3, 1, 0], dst.at[3, 1, 1]]

    side = t // 2
    is_mid = (t == 1) | (t == 2)
    is_edge = jnp.logical_not(is_mid)
    partner = 2 * side + 1 - t % 2
    far_mid = 2 - side
    far_edge = 3 - 3 * side
    far_slot = jnp.where(is_mid, 1, 2)

    def on_line(where):
        return (lat, lon, where)

    def spread_start(name, n, src, dst, i):
        base = SLOTS[name] + i
        send(src, dst, base + n * far_slot, on_line(far_mid), base + n)

        @pl.when(is_mid)
        def _():
            send(src, dst, base + n, on_line(far_edge), base + 2 * n)

        send(src, dst, base, on_line(partner), base)

    def spread_relay(name, n, buf, i):
        base = SLOTS[name] + i

        @pl.when(is_mid)
        def _():
            chunk = buf.at[far_edge, i]
            got(chunk, base + 2 * n)
            send(chunk, chunk, base + 2 * n, on_line(partner), base + 3 * n)

    def spread_wait(name, n, buf, i):
        base = SLOTS[name] + i
        got(buf.at[partner, i], base)
        got(buf.at[far_mid, i], base + n)

        @pl.when(is_edge)
        def _():
            got(buf.at[far_edge, i], base + 2 * n)

    def spread_drain(name, n, chunk, i):
        base = SLOTS[name] + i
        sent(chunk, base)
        sent(chunk, base + n)

        @pl.when(is_mid)
        def _():
            sent(chunk, base + 2 * n)
            sent(chunk, base + 3 * n)

    def sum_start(name, part, recv, relay, g):
        base = SLOTS[name] + g

        @pl.when(is_edge)
        def _():
            send(part.at[far_edge, g], relay.at[g], base + 6, on_line(partner), base + 4)

        send(part.at[far_mid, g], recv.at[t, g], base + 2 * far_slot, on_line(far_mid), base + 2)
        send(part.at[partner, g], recv.at[t, g], base, on_line(partner), base)

    def sum_relay(name, part, recv, relay, g):
        base = SLOTS[name] + g

        @pl.when(is_mid)
        def _():
            got(relay.at[g], base + 6)
            part[far_edge, g] = (part[far_edge, g].astype(F32) + relay[g].astype(F32)).astype(BF)
            send(part.at[far_edge, g], recv.at[t, g], base + 2, on_line(far_edge), base + 4)

    def sum_end(name, part, recv, g):
        base = SLOTS[name] + g
        got(recv.at[partner, g], base)
        got(recv.at[far_mid, g], base + 2)

        @pl.when(is_mid)
        def _():
            got(recv.at[far_edge, g], base + 4)

        @pl.when(is_edge)
        def _():
            recv[far_edge, g] = jnp.zeros(recv.shape[2:], BF)

        total = part[t, g].astype(F32)
        for src in (partner, far_mid, far_edge):
            total = total + recv[src, g].astype(F32)
        return total

    def give_fields(w, src):
        spread_start("fields", 4, src, x_own.at[w], w)

    halo(fields, x_own, SLOTS["halo_f"])

    piece_rows = pl.ds(pl.multiple_of(lx * 48, 16), 48)
    has_piece = ly < 3

    def piece(y, x):
        rows = pl.ds(pl.multiple_of(x * 48, 16), 48)
        return wcol.at[1:4, rows, pl.ds(pl.multiple_of(y * 128, 128), 128)]

    @pl.when(has_piece)
    def _():
        for d in (1, 2, 3):
            cols = pl.ds(pl.multiple_of(ring(t, d, 4) * SH + ly * 128, 128), 128)
            here = pl.ds(pl.multiple_of(ly * 128, 128), 128)
            send(wout.at[piece_rows, cols], wcol.at[d, piece_rows, here], SLOTS["wcol_z"] + d - 1, tp_dev(d))

    give_fields(0, fields.at[1:3, 1:3])
    own[1].wait()
    cut_blocks(cot_grid, cot)
    keep_grid(cot, cbuf)
    keep(wout.at[:, pl.ds(pl.multiple_of(t * SH, 128), SH)], wcol.at[0])

    def place(n):
        a, b, c, d = (n >> 5) & 1, (n >> 4) & 1, (n >> 2) & 3, n & 3
        return 4 * a + c, 4 * b + d

    def iota(shape, dim):
        return lax.broadcasted_iota(jnp.int32, shape, dim)

    def hot(flag):
        return jnp.where(flag, 1.0, 0.0)

    row_of, col_of = place(iota((CELLS, CELLS), 0))
    order = hot(iota((CELLS, CELLS), 1) == row_of * WIN + col_of).astype(BF)
    swapped = nn(order, index[...].astype(F32).astype(BF)).astype(BF)
    idx = nt(swapped, order)
    for c in range(NPAIR // 128):
        idx_row[0:1, c * 128:(c + 1) * 128] = jnp.concatenate([idx[2 * c:2 * c + 1], idx[2 * c + 1:2 * c + 2]], axis=1)

    cell = iota((NWIN * CELLS, 16), 0)
    row_of, col_of = place(cell)
    row_of, col_of = row_of + WIN * (cell >> 7), col_of + WIN * ((cell >> 6) & 1)
    picked_rows = nn(hot(iota((NWIN * CELLS, 16), 1) == row_of).astype(BF), mask[...].astype(F32).astype(BF))
    labels = jnp.sum(hot(iota((NWIN * CELLS, 16), 1) == col_of) * picked_rows, axis=1, keepdims=True)
    lab_col[...] = labels + 4.0 * (iota((NWIN * CELLS, 1), 0) >> 6).astype(F32)

    own[4].wait()
    got(halo_parts(x_own)[0], SLOTS["halo_f"])
    give_fields(1, x_own.at[1])
    own[5].wait()
    got(halo_parts(x_own)[1], SLOTS["halo_f"] + 1)
    give_fields(2, x_own.at[2])
    own[6].wait()
    for part in (2, 3, 4):
        got(halo_parts(x_own)[part], SLOTS["halo_f"] + part)
    give_fields(3, x_own.at[3])

    @pl.when(has_piece)
    def _():
        for d in (1, 2, 3):
            here = pl.ds(pl.multiple_of(ly * 128, 128), 128)
            got(wcol.at[d, piece_rows, here], SLOTS["wcol_z"] + d - 1)
        for o in range(15):
            send(piece(ly, lx), piece(ly, lx), SLOTS["wcol_p"] + o, plane_dev(o))

    halo(cot, cbuf, SLOTS["halo_c"])

    tab_pad[...] = jnp.zeros_like(tab_pad)
    tab_pad[0:HEADS, 0:table.shape[1]] = table[...]
    tab = jnp.concatenate([*split3(tab_pad[...]), jnp.zeros((8, TABLE), F32)], axis=0).astype(BF)
    entry = iota((TABLE, 512), 0).astype(F32)
    for c in range(NPAIR // 512):
        span = slice(c * 512, (c + 1) * 512)
        picked = hot(entry == idx_row[0:1, span]).astype(BF)
        onehot[:, span] = picked
        parts = nn(tab, picked)
        bias = parts[0:8] + parts[8:16] + parts[16:24]
        sig = 1.0 / (1.0 + jnp.exp(-bias))
        bsrow[:, span] = sig
        for k in range(8):
            for h in range(HEADS):
                at = 8 * c + k
                pair = jnp.concatenate([16.0 * sig[h:h + 1, k * CELLS:(k + 1) * CELLS]] * 2, axis=1)
                bsig[h, at:at + 1, :] = pair
                bsig[h, CELLS + at:CELLS + at + 1, :] = pair
    tacc[...] = jnp.zeros_like(tacc)
    sacc[...] = jnp.zeros_like(sacc)
    gacc[...] = jnp.zeros_like(gacc)
    scales = jnp.exp(logs[...])

    own[2].wait()
    own[3].wait()

    eye = iota((2 * CELLS, 2 * CELLS), 0) == iota((2 * CELLS, 2 * CELLS), 1)

    def forward(g):
        for w in (2 * g, 2 * g + 1):
            spread_relay("fields", 4, xbuf, w)
        for w in (2 * g, 2 * g + 1):
            spread_wait("fields", 4, xbuf, w)
        proj = jnp.zeros((2 * CELLS, 3 * AW), F32)
        for src in range(4):
            proj = proj + nt(xbuf[src, 2 * g:2 * g + 2].reshape(2 * CELLS, SH), wt[:, src * SH:(src + 1) * SH])
        column = lab_col[2 * g * CELLS:2 * (g + 1) * CELLS]
        row = jnp.sum(jnp.where(eye, column, 0.0), axis=0, keepdims=True)
        same = row == column
        heads = range(HEADS)

        def slot(kind, h):
            at = kind * AW + h * HD
            return proj[:, at:at + HD]

        q = [slot(0, h) for h in heads]
        k = [slot(1, h) for h in heads]
        v = [slot(2, h).astype(BF) for h in heads]
        rq = [lax.rsqrt(jnp.sum(q[h] * q[h], axis=1, keepdims=True) + 1e-06) for h in heads]
        rk = [lax.rsqrt(jnp.sum(k[h] * k[h], axis=1, keepdims=True) + 1e-06) for h in heads]
        q_hat = [(q[h] * rq[h]).astype(BF) for h in heads]
        k_hat = [(k[h] * rk[h]).astype(BF) for h in heads]
        cosine = [nt(q_hat[h], k_hat[h]) for h in heads]
        power = [scales[:, h:h + 1] * (cosine[h] - 1.0) + (bsig[h] - 16.0) for h in heads]
        weight = [jnp.where(same, jnp.exp(power[h]), 0.0) for h in heads]
        total = [jnp.sum(weight[h], axis=1, keepdims=True) for h in heads]
        prob = [(weight[h] * (1.0 / total[h])).astype(BF) for h in heads]
        attended = [nn(prob[h], v[h]).astype(BF) for h in heads]
        for i in (0, 1):
            for h in heads:
                at = i * AW + h * HD
                abuf[t, g, :, at:at + HD] = attended[h][i * CELLS:(i + 1) * CELLS]
        for h in heads:
            qs[g, h] = q_hat[h]
            ks[g, h] = k_hat[h]
            vs[g, h] = v[h]
            probs[g, h] = prob[h]
            coss[g, h] = cosine[h]
            rqs[g, h] = rq[h]
            rks[g, h] = rk[h]
        spread_start("att", 2, abuf.at[t, g], abuf.at[t, g], g)

    gain = gain_ref[...].reshape(1, SH)
    shift = shift_ref[...].reshape(1, SH)
    lane = iota((2 * CELLS, 128), 1)

    def unpack(pair):
        return jnp.concatenate([pair[:, :AW], pair[:, AW:]], axis=0)

    def cells_of(buf, g):
        return buf[2 * g:2 * g + 2].reshape(2 * CELLS, SH).astype(F32)

    def mix(g):
        spread_relay("att", 2, abuf, g)
        spread_wait("att", 2, abuf, g)
        total = jnp.zeros((2 * CELLS, SH), F32)
        for d in range(4):
            total = total + nn(unpack(abuf[ring(t, -d, 4), g]), wcol[d])
        mixed[g] = total
        grad_norm = cells_of(cbuf, g) * gain
        packed = jnp.zeros((2 * CELLS, 128), F32)
        for i, v in enumerate((total, total * total, grad_norm, grad_norm * total)):
            packed = jnp.where(lane == i, jnp.sum(v, axis=1, keepdims=True), packed)
        stat_all[t, g] = jnp.transpose(packed)[0:8]
        mine = stat_all.at[t, g]
        for d in (1, 2, 3):
            send(mine, mine, SLOTS["stat"] + (d - 1) * 2 + g, tp_dev(d))

    def normalise(g):
        for d in (1, 2, 3):
            got(stat_all.at[ring(t, -d, 4), g], SLOTS["stat"] + (d - 1) * 2 + g)
        totals = stat_all[0, g] + stat_all[1, g] + stat_all[2, g] + stat_all[3, g]
        packed = jnp.transpose(jnp.concatenate([totals, jnp.zeros((120, 128), F32)], axis=0))
        mean = packed[:, 0:1] / CH
        variance = packed[:, 1:2] / CH - mean * mean
        inv_std = 1.0 / jnp.sqrt(variance + 1e-05)
        grad_mean = packed[:, 2:3] / CH
        cross_mean = inv_std * (packed[:, 3:4] - mean * packed[:, 2:3]) / CH
        normed = (mixed[g] - mean) * inv_std
        rows = cells_of(cbuf, g)
        grad = (inv_std * (rows * gain - grad_mean - normed * cross_mean)).astype(BF)
        gmix[g] = grad
        for d in (2, 1, 3, 0):
            dst = ring(t, d, 4)
            part = nt(grad, wcol[(4 - d) % 4])
            ga_send[dst, g] = jnp.concatenate([part[:CELLS], part[CELLS:]], axis=1).astype(BF)
        sum_start("gatt", ga_send, ga_recv, ga_relay, g)
        base = xbuf[t, 2 * g:2 * g + 2].reshape(2 * CELLS, SH).astype(F32)
        obuf[2 * g:2 * g + 2] = (base + (gain * normed + shift)).astype(BF).reshape(2, 2, 2, 16, SH)
        gacc[0:1, :] += jnp.sum(rows * normed, axis=0, keepdims=True)
        gacc[1:2, :] += jnp.sum(rows, axis=0, keepdims=True)

    def backward(g):
        total = sum_end("gatt", ga_send, ga_recv, g)
        grad_att = unpack(total.astype(BF))
        heads = range(HEADS)
        ga = [grad_att[:, h * HD:(h + 1) * HD] for h in heads]
        prob = [probs[g, h] for h in heads]
        q_hat = [qs[g, h] for h in heads]
        k_hat = [ks[g, h] for h in heads]
        grad_prob = [nt(ga[h], vs[g, h]) for h in heads]
        grads_v = [tn(prob[h], ga[h]) for h in heads]
        prob_f = [prob[h].astype(F32) for h in heads]
        inner = [jnp.sum(prob_f[h] * grad_prob[h], axis=1, keepdims=True) for h in heads]
        grad_logit = [prob_f[h] * (grad_prob[h] - inner[h]) for h in heads]
        grad_cos = [(grad_logit[h] * scales[:, h:h + 1]).astype(BF) for h in heads]
        gq = [nn(grad_cos[h], k_hat[h]) for h in heads]
        gk = [tn(grad_cos[h], q_hat[h]) for h in heads]
        for h in heads:
            tacc[h] += grad_logit[h]
            sacc[h] += grad_logit[h] * coss[g, h]
        q_float = [q_hat[h].astype(F32) for h in heads]
        k_float = [k_hat[h].astype(F32) for h in heads]
        q_in = [jnp.sum(q_float[h] * gq[h], axis=1, keepdims=True) for h in heads]
        k_in = [jnp.sum(k_float[h] * gk[h], axis=1, keepdims=True) for h in heads]
        grads_q = [(gq[h] - q_float[h] * q_in[h]) * rqs[g, h] for h in heads]
        grads_k = [(gk[h] - k_float[h] * k_in[h]) * rks[g, h] for h in heads]
        stacked = jnp.concatenate(grads_q + grads_k + grads_v, axis=1).astype(BF)
        for d in (2, 1, 3, 0):
            dst = ring(t, d, 4)
            gs_send[dst, g] = nn(stacked, wt[:, pl.ds(pl.multiple_of(dst * SH, 128), SH)]).astype(BF)
        sum_start("gsh", gs_send, gs_recv, gs_relay, g)

    def finish(g):
        total = sum_end("gsh", gs_send, gs_recv, g) + cells_of(cbuf, g)
        gobuf[2 * g:2 * g + 2] = total.astype(BF).reshape(2, 2, 2, 16, SH)

    def give_first(buf, out, base):
        out[1:3, 1:3] = buf[0]
        out[1:3, 3] = buf[1, :, 0]
        send(buf.at[1, :, 1], out.at[1:3, 0], base, (lat, lon_n, t))

    def give_second(buf, out, base):
        send(buf.at[2, 1], out.at[0, 1:3], base + 1, (lat_n, lon, t))
        send(buf.at[3, 0, 1], out.at[3, 0], base + 2, (lat, lon_n, t))
        send(buf.at[3, 1, 0], out.at[0, 3], base + 3, (lat_n, lon, t))
        send(buf.at[3, 1, 1], out.at[0, 0], base + 4, (lat_n, lon_n, t))
        out[3, 1:3] = buf[2, 0]
        out[3, 3] = buf[3, 0, 0]

    def back_parts(out):
        return [out.at[1:3, 0], out.at[0, 1:3], out.at[3, 0], out.at[0, 3], out.at[0, 0]]

    def weight_first():
        for group in range(4):
            wacc[group] = tn(unpack(abuf[group, 0]), gmix[0])

    def weight_start():
        for j in (0, 1):
            far = 2 * (1 - core) + j
            wc_send[j] = (wacc[far] + tn(unpack(abuf[far, 1]), gmix[1])).astype(BF)
        send(wc_send, wc_recv, SLOTS["w_core"], sib)
        for j in (0, 1):
            near = 2 * core + j
            wacc[near] = wacc[near] + tn(unpack(abuf[near, 1]), gmix[1])

    def rows_of(y, x):
        return pl.ds(pl.multiple_of(x * 48 + y * 16, 16), 16)

    def weight_plane():
        got(wc_recv, SLOTS["w_core"])
        for j in (0, 1):
            total = wacc[2 * core + j] + wc_recv[j].astype(F32)
            wacc[2 * core + j] = total
            wp_send[j] = total.astype(BF)
        for o in range(15):
            y, x = plane(o)

            @pl.when(y < 3)
            def _():
                send(wp_send.at[:, rows_of(y, x)], wp_recv.at[o], SLOTS["w_p"] + o, plane_dev(o))

    holder = t // 2 == core

    def weight_z():
        @pl.when(has_piece)
        def _():
            for o in range(15):
                got(wp_recv.at[o], SLOTS["w_p"] + o)
            for j in (0, 1):
                total = wacc[2 * core + j, rows_of(ly, lx), :]
                for o in range(15):
                    total = total + wp_recv[o, j].astype(F32)
                wp_sum[j] = total.astype(BF)
            for j in (0, 1):
                keeper = 2 * core + j
                for dz in range(4):
                    @pl.when((keeper != t) if dz == 0 else (keeper >= 0))
                    def _():
                        dev = (ring(zh, dz, 4) * 2 + core, lon, keeper)
                        send(wp_sum.at[j], bz.at[zh, t], SLOTS["w_z"] + zh * 4 + t, dev, SLOTS["w_zs"] + 4 * j + dz)

    def weight_back_plane():
        @pl.when(holder & has_piece)
        def _():
            bz[zh, t] = wp_sum[t % 2]
            for z in range(4):
                for src in range(4):
                    @pl.when((zh != z) | (t != src))
                    def _():
                        got(bz.at[z, src], SLOTS["w_z"] + z * 4 + src)

            for src in range(4):
                total = bz[0, src].astype(F32)
                for z in range(1, 4):
                    total = total + bz[z, src].astype(F32)
                out_w[rows_of(ly, lx), src * SH:(src + 1) * SH] = total.astype(BF)
            mine = out_w.at[rows_of(ly, lx)]
            for o in range(15):
                send(mine, mine, SLOTS["back_p"] + o, plane_dev(o))
            send(mine, mine, SLOTS["back_core"] + lx * 3 + ly, sib)

    def weight_back_core():
        @pl.when(holder)
        def _():
            for o in range(15):
                y, x = plane_from(o)

                @pl.when(y < 3)
                def _():
                    mine = out_w.at[rows_of(y, x)]
                    got(mine, SLOTS["back_p"] + o)
                    send(mine, mine, SLOTS["back_core"] + x * 3 + y, sib)

    def small_start():
        folded_t = [tacc[h, :CELLS, :CELLS] + tacc[h, CELLS:, CELLS:] for h in range(HEADS)]
        for c in range(NPAIR // 128):
            for h in range(HEADS):
                pair = [folded_t[h][2 * c + i:2 * c + i + 1, :] for i in (0, 1)]
                flat[h:h + 1, c * 128:(c + 1) * 128] = jnp.concatenate(pair, axis=1)
        spread = bsrow[0:HEADS, :]
        terms = flat[0:HEADS, :] * 16.0 * spread * (1.0 - spread)
        pad = jnp.zeros((8 - HEADS, NPAIR), F32)
        pieces = jnp.concatenate([v for p in split3(terms) for v in (p, pad)], axis=0).astype(BF)
        folded = nt(pieces, onehot[...])
        sm_p[lon] = folded[0:8] + folded[8:16] + folded[16:24]
        for h in range(HEADS):
            amount = jnp.sum(jnp.sum(sacc[h], axis=1, keepdims=True), axis=0, keepdims=True) * scales[:, h:h + 1]
            sm_p[lon, h:h + 1, TABLE - 1:TABLE] = amount
        sm_p[lon, 3:5, :] = gacc[0:2, 0:TABLE]
        sm_p[lon, 5:6, :] = jnp.concatenate([gacc[0:1, TABLE:SH], gacc[1:2, TABLE:SH]], axis=1)
        for o in range(15):
            send(sm_p.at[lon], sm_p.at[lon], SLOTS["s_p"] + o, plane_dev(o))

    def small_lat():
        for o in range(15):
            y, x = plane_from(o)
            got(sm_p.at[y * 4 + x], SLOTS["s_p"] + o)
        total = sm_p[0]
        for i in range(1, 16):
            total = total + sm_p[i]
        sm_l[lat] = total
        for d in range(1, 8):
            send(sm_l.at[lat], sm_l.at[lat], SLOTS["s_l"] + d - 1, (ring(lat, d, 8), lon, t))

    def small_end():
        for d in range(1, 8):
            got(sm_l.at[ring(lat, -d, 8)], SLOTS["s_l"] + d - 1)
        total = sm_l[0]
        for i in range(1, 8):
            total = total + sm_l[i]
        out_s[...] = jnp.zeros_like(out_s)
        out_s[0:2, 0:TABLE] = total[3:5]
        out_s[0:1, TABLE:SH] = total[5:6, 0:128]
        out_s[1:2, TABLE:SH] = total[5:6, 128:256]
        out_s[2:5, 0:TABLE] = total[0:3]

    forward(0)
    forward(1)
    own[11].wait()
    for o in range(15):
        y, x = plane_from(o)

        @pl.when(y < 3)
        def _():
            got(piece(y, x), SLOTS["wcol_p"] + o)

    for i in (7, 8, 9, 10):
        own[i].wait()
    for i in range(5):
        got(halo_parts(cbuf)[i], SLOTS["halo_c"] + i)
    mix(0)
    normalise(0)
    mix(1)
    sum_relay("gatt", ga_send, ga_recv, ga_relay, 0)
    weight_first()
    normalise(1)
    weight_start()
    sum_relay("gatt", ga_send, ga_recv, ga_relay, 1)
    give_first(obuf, out_f, SLOTS["out_f"])
    give_second(obuf, out_f, SLOTS["out_f"])
    backward(0)
    weight_plane()
    backward(1)
    sum_relay("gsh", gs_send, gs_recv, gs_relay, 0)
    small_start()
    sum_relay("gsh", gs_send, gs_recv, gs_relay, 1)
    weight_z()
    finish(0)
    give_first(gobuf, out_g, SLOTS["out_g"])
    small_lat()
    weight_back_plane()
    finish(1)
    give_second(gobuf, out_g, SLOTS["out_g"])
    weight_back_core()
    small_end()

    for i in range(5):
        got(back_parts(out_f)[i], SLOTS["out_f"] + i)
        got(back_parts(out_g)[i], SLOTS["out_g"] + i)

    for base, parts in (("halo_f", halo_parts(x_own)), ("halo_c", halo_parts(cbuf)),
                        ("out_f", back_parts(out_f)), ("out_g", back_parts(out_g))):
        for i in range(5):
            sent(parts[i], SLOTS[base] + i)

    for w in range(NWIN):
        spread_drain("fields", 4, xbuf.at[0, 0], w)
    for g in range(GROUPS):
        spread_drain("att", 2, abuf.at[0, 0], g)
        for i in range(3):
            sent(stat_all.at[0, 0], SLOTS["stat"] + 2 * i + g)
            sent(ga_send.at[0, 0], SLOTS["gatt"] + 2 * i + g)
            sent(gs_send.at[0, 0], SLOTS["gsh"] + 2 * i + g)

    @pl.when(has_piece)
    def _():
        for d in range(3):
            sent(wcol.at[0, 0:48, 0:128], SLOTS["wcol_z"] + d)
            for j in (0, 1):
                sent(wp_sum.at[j], SLOTS["w_zs"] + 4 * j + d + 1)
        for o in range(15):
            sent(wcol.at[1:4, 0:48, 0:128], SLOTS["wcol_p"] + o)

        for j in (0, 1):
            @pl.when(2 * core + j != t)
            def _():
                sent(wp_sum.at[j], SLOTS["w_zs"] + 4 * j)

    @pl.when(holder & has_piece)
    def _():
        for o in range(15):
            sent(out_w.at[0:16], SLOTS["back_p"] + o)
        sent(out_w.at[0:16], SLOTS["back_core"] + lx * 3 + ly)

    for o in range(15):
        sent(sm_p.at[0], SLOTS["s_p"] + o)

        @pl.when(plane(o)[0] < 3)
        def _():
            sent(wp_send.at[:, 0:16], SLOTS["w_p"] + o)

        @pl.when(holder & (plane_from(o)[0] < 3))
        def _():
            y, x = plane_from(o)
            sent(out_w.at[0:16], SLOTS["back_core"] + x * 3 + y)

    for d in range(7):
        sent(sm_l.at[0], SLOTS["s_l"] + d)
    sent(wc_send, SLOTS["w_core"])

    @pl.when(jnp.logical_not(holder))
    def _():
        for x in range(4):
            for y in range(3):
                got(out_w.at[x * 48 + y * 16:x * 48 + y * 16 + 16], SLOTS["back_core"] + x * 3 + y)


def per_device(
    fields, w_qkv, w_out, log_scale, bias_table, bias_index, mask_ids, norm_gain, norm_shift, cotangent
):
    rows = bias_table.shape[0]
    wt = w_qkv.transpose(1, 2, 0).reshape(3 * AW, CH)
    hbm = pl.BlockSpec(memory_space=pltpu.HBM)
    vmem = pl.BlockSpec(memory_space=pltpu.VMEM)
    scratch = [
        ((16, 16, SH), BF), ((16, 16, SH), BF), ((576, CH), BF), ((4, 4, 16, SH), BF), ((4, 4, 16, SH), BF), ((4, 4, 2, 2, 16, SH), BF), ((4, 2, 2, 16, SH), BF), ((4, AW, SH), BF),
        ((4, 2, CELLS, SH), BF), ((TABLE, NPAIR), BF), ((8, NPAIR), F32), ((8, NPAIR), F32), ((8, TABLE), F32),
        ((HEADS, 2 * CELLS, 2 * CELLS), F32), ((NWIN * CELLS, 1), F32),
        ((2, HEADS, 2 * CELLS, HD), BF), ((2, HEADS, 2 * CELLS, HD), BF), ((2, HEADS, 2 * CELLS, HD), BF),
        ((2, HEADS, 2 * CELLS, 2 * CELLS), BF), ((2, HEADS, 2 * CELLS, 2 * CELLS), F32),
        ((2, HEADS, 2 * CELLS, 1), F32), ((2, HEADS, 2 * CELLS, 1), F32),
        ((2, 2 * CELLS, SH), F32), ((4, 2, 8, 128), F32), ((2, 2 * CELLS, SH), BF),
        ((4, 2, CELLS, SH), BF), ((4, 2, CELLS, SH), BF), ((2, CELLS, SH), BF),
        ((4, 2, 2 * CELLS, SH), BF), ((4, 2, 2 * CELLS, SH), BF), ((2, 2 * CELLS, SH), BF),
        ((4, 2, 2, 16, SH), BF), ((4, 2, 2, 16, SH), BF),
        ((HEADS, 2 * CELLS, 2 * CELLS), F32), ((HEADS, 2 * CELLS, 2 * CELLS), F32), ((8, SH), F32), ((8, NPAIR), F32),
        ((2, AW, SH), BF), ((2, AW, SH), BF), ((4, AW, SH), F32),
        ((2, AW, SH), BF), ((15, 2, 16, SH), BF), ((2, 16, SH), BF), ((4, 4, 16, SH), BF),
        ((16, 8, TABLE), F32), ((8, 8, TABLE), F32),
    ]
    out_f, out_g, out_w, out_s = pl.pallas_call(
        whole_kernel,
        out_shape=(
            jax.ShapeDtypeStruct((4, 4, 16, SH), BF),
            jax.ShapeDtypeStruct((4, 4, 16, SH), BF),
            jax.ShapeDtypeStruct((AW, CH), BF),
            jax.ShapeDtypeStruct((8, SH), F32),
        ),
        in_specs=[hbm, hbm, hbm, hbm, vmem, vmem, vmem, vmem, vmem, vmem],
        out_specs=(vmem, vmem, vmem, vmem),
        scratch_shapes=[pltpu.VMEM(shape, kind) for shape, kind in scratch] + [
            pltpu.SemaphoreType.DMA((12,)),
            pltpu.SemaphoreType.DMA((COUNT,)),
            pltpu.SemaphoreType.DMA((COUNT,)),
        ],
        compiler_params=pltpu.CompilerParams(
            collective_id=0, has_side_effects=True, vmem_limit_bytes=60 * 1024 * 1024
        ),
        cost_estimate=pl.CostEstimate(flops=2_000_000_000, bytes_accessed=5_000_000, transcendentals=200_000),
    )(
        fields, cotangent, wt, w_out, log_scale.reshape(1, HEADS), bias_table.T, bias_index, mask_ids,
        norm_gain, norm_shift,
    )
    shapes = (
        (fields.shape, BF), (fields.shape, BF), ((AW, CH), BF), ((HEADS, rows), F32), ((HEADS,), F32),
        ((SH,), F32), ((SH,), F32),
    )
    block_out, grad_fields, grad_w_out, grad_table, grad_scale, grad_gain, grad_shift = pl.pallas_call(
        write_kernel,
        out_shape=tuple(jax.ShapeDtypeStruct(shape, kind) for shape, kind in shapes),
        in_specs=[vmem] * 4,
        out_specs=(vmem,) * 7,
        compiler_params=pltpu.CompilerParams(vmem_limit_bytes=60 * 1024 * 1024),
        cost_estimate=pl.CostEstimate(flops=1_000_000, bytes_accessed=2_000_000, transcendentals=0),
    )(out_f, out_g, out_w, out_s)
    return (block_out, grad_fields, grad_w_out, grad_table.T, grad_scale, grad_gain, grad_shift)


def solution(mesh):
    in_specs = (
        P("lat", "lon", "tp"), P(None, None, "tp"), P("tp", None), P("tp"), P(None, "tp"), P(),
        P("lat", "lon"), P("tp"), P("tp"), P("lat", "lon", "tp"),
    )
    out_specs = (
        P("lat", "lon", "tp"), P("lat", "lon", "tp"), P("tp", None), P(None, "tp"), P("tp"), P("tp"), P("tp"),
    )
    return jax.shard_map(per_device, mesh=mesh, in_specs=in_specs, out_specs=out_specs, check_vma=False)
```

```python
import jax
import jax.numpy as jnp
from jax import lax
from jax.experimental import pallas as pl
from jax.experimental.pallas import tpu as pltpu
from jax.sharding import PartitionSpec as P

MESH = pl.DeviceIdType.MESH
BF = jnp.bfloat16
F32 = jnp.float32

CH = 1536
SH = 384
HEADS = 3
HD = 64
AW = HEADS * HD
CELLS = 64
NWIN = 4
GROUPS = 2
WIN = 8
TABLE = 256
NPAIR = 4096

SLOTS = {}
COUNT = 0
for _name, _n in (
    ("halo_f", 5), ("halo_c", 5), ("fields", 16), ("wcol_z", 3), ("wcol_p", 15), ("att", 8), ("stat", 6),
    ("gatt", 8), ("gsh", 8), ("out_f", 5), ("out_g", 5), ("w_core", 1), ("w_p", 15), ("w_z", 16),
    ("w_zs", 8), ("back_p", 15), ("back_core", 12), ("s_p", 15), ("s_l", 7),
):
    SLOTS[_name] = COUNT
    COUNT += _n

PLANE = [(dy, dx) for dy in range(4) for dx in range(4)][1:]


def nn(a, b):
    return lax.dot_general(a, b, (((1,), (0,)), ((), ())), preferred_element_type=F32)


def nt(a, b):
    return lax.dot_general(a, b, (((1,), (1,)), ((), ())), preferred_element_type=F32)


def tn(a, b):
    return lax.dot_general(a, b, (((0,), (0,)), ((), ())), preferred_element_type=F32)


def split3(value):
    high = value.astype(BF).astype(F32)
    middle = (value - high).astype(BF).astype(F32)
    return high, middle, value - high - middle


def swap_halves(first, second):
    low = lax.broadcasted_iota(jnp.int32, first.shape, 0) < 4
    return jnp.where(low, first, pltpu.roll(second, 4, 0)), jnp.where(low, pltpu.roll(first, 4, 0), second)


def cut_blocks(grid, blocks):
    for i in range(4):
        tiles = [[None, None] for _ in range(4)]
        for half in (0, 1):
            upper = grid[4 * i + 2 * half].astype(F32)
            lower = grid[4 * i + 2 * half + 1].astype(F32)
            for k in (0, 1):
                pair = swap_halves(upper[8 * k:8 * k + 8], lower[8 * k:8 * k + 8])
                tiles[2 * k][half], tiles[2 * k + 1][half] = pair
        for j in range(4):
            blocks[i, j] = jnp.concatenate(tiles[j], axis=0).astype(BF)


def join_blocks(blocks, grid):
    for i in range(4):
        for half in (0, 1):
            upper, lower = [], []
            for k in (0, 1):
                rows = slice(8 * half, 8 * half + 8)
                pair = swap_halves(blocks[i, 2 * k].astype(F32)[rows], blocks[i, 2 * k + 1].astype(F32)[rows])
                upper.append(pair[0])
                lower.append(pair[1])
            grid[4 * i + 2 * half] = jnp.concatenate(upper, axis=0).astype(BF)
            grid[4 * i + 2 * half + 1] = jnp.concatenate(lower, axis=0).astype(BF)


def write_kernel(blocks_f, blocks_g, weights, small, out_f, out_g, out_w, out_t, out_s, out_a, out_b):
    out_w[...] = weights[...]
    join_blocks(blocks_f, out_f)
    join_blocks(blocks_g, out_g)
    out_t[...] = small[2:2 + HEADS, 0:out_t.shape[1]]
    spare = small[2:2 + HEADS, TABLE - 1:TABLE]
    scales = jnp.transpose(jnp.concatenate([jnp.broadcast_to(spare, (HEADS, 128)), jnp.zeros((8 - HEADS, 128), F32)], axis=0))
    out_s[...] = scales[0:1, 0:HEADS].reshape(HEADS)
    out_a[...] = small[0]
    out_b[...] = small[1]


def whole_kernel(
    fields_hbm, cot_hbm, wt_hbm, wout, logs, table, index, mask, gain_ref, shift_ref,
    out_f, out_g, out_w, out_s,
    fields_grid, cot_grid, wt, fields, cot, xbuf, cbuf, wcol, abuf, onehot, bsrow, idx_row, tab_pad, bsig, lab_col, qs, ks, vs, probs, coss, rqs, rks,
    mixed, stat_all, gmix, ga_send, ga_recv, ga_relay, gs_send, gs_recv, gs_relay, obuf, gobuf, tacc, sacc, gacc, flat,
    wc_send, wc_recv, wacc, wp_send, wp_recv, wp_sum, bz, sm_p, sm_l, local_sem, ssem, rsem,
):
    lat = lax.axis_index("lat")
    lon = lax.axis_index("lon")
    t = lax.axis_index("tp")
    zh = lat // 2
    core = lat % 2
    ly = lon // 4
    lx = lon % 4

    def ring(value, by, count):
        return lax.rem(value + by + count, count)

    lat_p, lat_n = ring(lat, -1, 8), ring(lat, 1, 8)
    lon_p, lon_n = ring(lon, -1, 16), ring(lon, 1, 16)
    sib = (zh * 2 + (1 - core), lon, t)

    def tp_dev(d):
        return (lat, lon, ring(t, d, 4))

    def plane(o):
        return ring(ly, PLANE[o][0], 4), ring(lx, PLANE[o][1], 4)

    def plane_from(o):
        return ring(ly, -PLANE[o][0], 4), ring(lx, -PLANE[o][1], 4)

    def plane_dev(o):
        y, x = plane(o)
        return (lat, y * 4 + x, t)

    def z_dev(d):
        return (ring(zh, d, 4) * 2 + core, lon, t)

    def copy(src, dst, slot, dev, send_slot=None):
        return pltpu.make_async_remote_copy(
            src_ref=src, dst_ref=dst, send_sem=ssem.at[slot if send_slot is None else send_slot],
            recv_sem=rsem.at[slot], device_id=dev, device_id_type=MESH,
        )

    def send(src, dst, slot, dev, send_slot=None):
        copy(src, dst, slot, dev, send_slot).start()

    def got(dst, slot):
        copy(dst, dst, slot, sib).wait_recv()

    def sent(src, slot):
        copy(src, src, slot, sib).wait_send()

    own = []

    def keep(src, dst):
        own.append(pltpu.make_async_copy(src, dst, local_sem.at[len(own)]))
        own[-1].start()

    keep(fields_hbm, fields_grid)
    keep(cot_hbm, cot_grid)
    keep(wt_hbm, wt)

    partners = [plane_dev(o) for o in range(15)] + [(ring(lat, d, 8), lon, t) for d in range(1, 8)]
    partners += [(lat_p, lon_p, t), (lat_n, lon_n, t)] + [tp_dev(d) for d in (1, 2, 3)]
    partners += [(ring(zh, dz, 4) * 2 + core, lon, ring(t, dt, 4)) for dz in (1, 2, 3) for dt in (1, 2, 3)]
    barrier = pltpu.get_barrier_semaphore()
    for dev in partners:
        pl.semaphore_signal(barrier, inc=1, device_id=dev, device_id_type=MESH)

    def keep_grid(grid, dst):
        keep(grid.at[1:3, 1:3], dst.at[0])
        keep(grid.at[1:3, 3], dst.at[1, :, 0])
        keep(grid.at[3, 1:3], dst.at[2, 0])
        keep(grid.at[3, 3], dst.at[3, 0, 0])

    x_own = xbuf.at[t]
    own[0].wait()
    cut_blocks(fields_grid, fields)
    keep_grid(fields, x_own)

    pl.semaphore_wait(barrier, len(partners))

    def halo(grid, dst, base):
        send(grid.at[1:3, 0], dst.at[1, :, 1], base, (lat, lon_p, t))
        send(grid.at[0, 1:3], dst.at[2, 1], base + 1, (lat_p, lon, t))
        send(grid.at[3, 0], dst.at[3, 0, 1], base + 2, (lat, lon_p, t))
        send(grid.at[0, 3], dst.at[3, 1, 0], base + 3, (lat_p, lon, t))
        send(grid.at[0, 0], dst.at[3, 1, 1], base + 4, (lat_p, lon_p, t))

    def halo_parts(dst):
        return [dst.at[1, :, 1], dst.at[2, 1], dst.at[3, 0, 1], dst.at[3, 1, 0], dst.at[3, 1, 1]]

    side = t // 2
    is_mid = (t == 1) | (t == 2)
    is_edge = jnp.logical_not(is_mid)
    partner = 2 * side + 1 - t % 2
    far_mid = 2 - side
    far_edge = 3 - 3 * side
    far_slot = jnp.where(is_mid, 1, 2)

    def on_line(where):
        return (lat, lon, where)

    def spread_start(name, n, src, dst, i):
        base = SLOTS[name] + i
        send(src, dst, base + n * far_slot, on_line(far_mid), base + n)

        @pl.when(is_mid)
        def _():
            send(src, dst, base + n, on_line(far_edge), base + 2 * n)

        send(src, dst, base, on_line(partner), base)

    def spread_relay(name, n, buf, i):
        base = SLOTS[name] + i

        @pl.when(is_mid)
        def _():
            chunk = buf.at[far_edge, i]
            got(chunk, base + 2 * n)
            send(chunk, chunk, base + 2 * n, on_line(partner), base + 3 * n)

    def spread_wait(name, n, buf, i):
        base = SLOTS[name] + i
        got(buf.at[partner, i], base)
        got(buf.at[far_mid, i], base + n)

        @pl.when(is_edge)
        def _():
            got(buf.at[far_edge, i], base + 2 * n)

    def spread_drain(name, n, chunk, i):
        base = SLOTS[name] + i
        sent(chunk, base)
        sent(chunk, base + n)

        @pl.when(is_mid)
        def _():
            sent(chunk, base + 2 * n)
            sent(chunk, base + 3 * n)

    def sum_start(name, part, recv, relay, g, term):
        base = SLOTS[name] + g
        part[far_edge, g] = term(far_edge)

        @pl.when(is_edge)
        def _():
            send(part.at[far_edge, g], relay.at[g], base + 6, on_line(partner), base + 4)

        part[far_mid, g] = term(far_mid)
        send(part.at[far_mid, g], recv.at[t, g], base + 2 * far_slot, on_line(far_mid), base + 2)
        part[partner, g] = term(partner)
        send(part.at[partner, g], recv.at[t, g], base, on_line(partner), base)
        part[t, g] = term(t)

    def sum_relay(name, part, recv, relay, g):
        base = SLOTS[name] + g

        @pl.when(is_mid)
        def _():
            got(relay.at[g], base + 6)
            part[far_edge, g] = (part[far_edge, g].astype(F32) + relay[g].astype(F32)).astype(BF)
            send(part.at[far_edge, g], recv.at[t, g], base + 2, on_line(far_edge), base + 4)

    def sum_end(name, part, recv, g):
        base = SLOTS[name] + g
        got(recv.at[partner, g], base)
        got(recv.at[far_mid, g], base + 2)

        @pl.when(is_mid)
        def _():
            got(recv.at[far_edge, g], base + 4)

        @pl.when(is_edge)
        def _():
            recv[far_edge, g] = jnp.zeros(recv.shape[2:], BF)

        total = part[t, g].astype(F32)
        for src in (partner, far_mid, far_edge):
            total = total + recv[src, g].astype(F32)
        return total

    def give_fields(w, src):
        spread_start("fields", 4, src, x_own.at[w], w)

    halo(fields, x_own, SLOTS["halo_f"])

    piece_rows = pl.ds(pl.multiple_of(lx * 48, 16), 48)
    has_piece = ly < 3

    def piece(y, x):
        rows = pl.ds(pl.multiple_of(x * 48, 16), 48)
        return wcol.at[1:4, rows, pl.ds(pl.multiple_of(y * 128, 128), 128)]

    @pl.when(has_piece)
    def _():
        for d in (1, 2, 3):
            cols = pl.ds(pl.multiple_of(ring(t, d, 4) * SH + ly * 128, 128), 128)
            here = pl.ds(pl.multiple_of(ly * 128, 128), 128)
            send(wout.at[piece_rows, cols], wcol.at[d, piece_rows, here], SLOTS["wcol_z"] + d - 1, tp_dev(d))

    give_fields(0, fields.at[1:3, 1:3])
    own[1].wait()
    cut_blocks(cot_grid, cot)
    keep_grid(cot, cbuf)
    keep(wout.at[:, pl.ds(pl.multiple_of(t * SH, 128), SH)], wcol.at[0])

    def place(n):
        a, b, c, d = (n >> 5) & 1, (n >> 4) & 1, (n >> 2) & 3, n & 3
        return 4 * a + c, 4 * b + d

    def iota(shape, dim):
        return lax.broadcasted_iota(jnp.int32, shape, dim)

    def hot(flag):
        return jnp.where(flag, 1.0, 0.0)

    row_of, col_of = place(iota((CELLS, CELLS), 0))
    order = hot(iota((CELLS, CELLS), 1) == row_of * WIN + col_of).astype(BF)
    swapped = nn(order, index[...].astype(F32).astype(BF)).astype(BF)
    idx = nt(swapped, order)
    for c in range(NPAIR // 128):
        idx_row[0:1, c * 128:(c + 1) * 128] = jnp.concatenate([idx[2 * c:2 * c + 1], idx[2 * c + 1:2 * c + 2]], axis=1)

    cell = iota((NWIN * CELLS, 16), 0)
    row_of, col_of = place(cell)
    row_of, col_of = row_of + WIN * (cell >> 7), col_of + WIN * ((cell >> 6) & 1)
    picked_rows = nn(hot(iota((NWIN * CELLS, 16), 1) == row_of).astype(BF), mask[...].astype(F32).astype(BF))
    labels = jnp.sum(hot(iota((NWIN * CELLS, 16), 1) == col_of) * picked_rows, axis=1, keepdims=True)
    lab_col[...] = labels + 4.0 * (iota((NWIN * CELLS, 1), 0) >> 6).astype(F32)

    own[4].wait()
    got(halo_parts(x_own)[0], SLOTS["halo_f"])
    give_fields(1, x_own.at[1])
    own[5].wait()
    got(halo_parts(x_own)[1], SLOTS["halo_f"] + 1)
    give_fields(2, x_own.at[2])
    own[6].wait()
    for part in (2, 3, 4):
        got(halo_parts(x_own)[part], SLOTS["halo_f"] + part)
    give_fields(3, x_own.at[3])

    @pl.when(has_piece)
    def _():
        for d in (1, 2, 3):
            here = pl.ds(pl.multiple_of(ly * 128, 128), 128)
            got(wcol.at[d, piece_rows, here], SLOTS["wcol_z"] + d - 1)
        for o in range(15):
            send(piece(ly, lx), piece(ly, lx), SLOTS["wcol_p"] + o, plane_dev(o))

    halo(cot, cbuf, SLOTS["halo_c"])

    tab_pad[...] = jnp.zeros_like(tab_pad)
    tab_pad[0:HEADS, 0:table.shape[1]] = table[...]
    tab = jnp.concatenate([*split3(tab_pad[...]), jnp.zeros((8, TABLE), F32)], axis=0).astype(BF)
    entry = iota((TABLE, 512), 0).astype(F32)
    for c in range(NPAIR // 512):
        span = slice(c * 512, (c + 1) * 512)
        picked = hot(entry == idx_row[0:1, span]).astype(BF)
        onehot[:, span] = picked
        parts = nn(tab, picked)
        bias = parts[0:8] + parts[8:16] + parts[16:24]
        sig = 1.0 / (1.0 + jnp.exp(-bias))
        bsrow[:, span] = sig
        for k in range(8):
            for h in range(HEADS):
                at = 8 * c + k
                pair = jnp.concatenate([16.0 * sig[h:h + 1, k * CELLS:(k + 1) * CELLS]] * 2, axis=1)
                bsig[h, at:at + 1, :] = pair
                bsig[h, CELLS + at:CELLS + at + 1, :] = pair
    tacc[...] = jnp.zeros_like(tacc)
    sacc[...] = jnp.zeros_like(sacc)
    gacc[...] = jnp.zeros_like(gacc)
    scales = jnp.exp(logs[...])

    own[2].wait()
    own[3].wait()

    eye = iota((2 * CELLS, 2 * CELLS), 0) == iota((2 * CELLS, 2 * CELLS), 1)

    def forward(g):
        for w in (2 * g, 2 * g + 1):
            spread_relay("fields", 4, xbuf, w)
        for w in (2 * g, 2 * g + 1):
            spread_wait("fields", 4, xbuf, w)
        proj = jnp.zeros((2 * CELLS, 3 * AW), F32)
        for src in range(4):
            proj = proj + nt(xbuf[src, pl.ds(2 * g, 2)].reshape(2 * CELLS, SH), wt[:, src * SH:(src + 1) * SH])
        column = lab_col[pl.ds(pl.multiple_of(2 * g * CELLS, 128), 128), :]
        row = jnp.sum(jnp.where(eye, column, 0.0), axis=0, keepdims=True)
        same = row == column
        heads = range(HEADS)

        def slot(kind, h):
            at = kind * AW + h * HD
            return proj[:, at:at + HD]

        q = [slot(0, h) for h in heads]
        k = [slot(1, h) for h in heads]
        v = [slot(2, h).astype(BF) for h in heads]
        rq = [lax.rsqrt(jnp.sum(q[h] * q[h], axis=1, keepdims=True) + 1e-06) for h in heads]
        rk = [lax.rsqrt(jnp.sum(k[h] * k[h], axis=1, keepdims=True) + 1e-06) for h in heads]
        q_hat = [(q[h] * rq[h]).astype(BF) for h in heads]
        k_hat = [(k[h] * rk[h]).astype(BF) for h in heads]
        cosine = [nt(q_hat[h], k_hat[h]) for h in heads]
        power = [scales[:, h:h + 1] * (cosine[h] - 1.0) + (bsig[h] - 16.0) for h in heads]
        weight = [jnp.where(same, jnp.exp(power[h]), 0.0) for h in heads]
        total = [jnp.sum(weight[h], axis=1, keepdims=True) for h in heads]
        prob = [(weight[h] * (1.0 / total[h])).astype(BF) for h in heads]
        attended = [nn(prob[h], v[h]).astype(BF) for h in heads]
        for i in (0, 1):
            for h in heads:
                at = i * AW + h * HD
                abuf[t, g, :, at:at + HD] = attended[h][i * CELLS:(i + 1) * CELLS]
        for h in heads:
            qs[g, h] = q_hat[h]
            ks[g, h] = k_hat[h]
            vs[g, h] = v[h]
            probs[g, h] = prob[h]
            coss[g, h] = cosine[h]
            rqs[g, h] = rq[h]
            rks[g, h] = rk[h]
        spread_start("att", 2, abuf.at[t, g], abuf.at[t, g], g)

    gain = gain_ref[...].reshape(1, SH)
    shift = shift_ref[...].reshape(1, SH)
    lane = iota((2 * CELLS, 128), 1)

    def unpack(pair):
        return jnp.concatenate([pair[:, :AW], pair[:, AW:]], axis=0)

    def cells_of(buf, g):
        return buf[pl.ds(2 * g, 2)].reshape(2 * CELLS, SH).astype(F32)

    def mix(g):
        spread_relay("att", 2, abuf, g)
        spread_wait("att", 2, abuf, g)
        total = jnp.zeros((2 * CELLS, SH), F32)
        for d in range(4):
            total = total + nn(unpack(abuf[ring(t, -d, 4), g]), wcol[d])
        mixed[g] = total
        grad_norm = cells_of(cbuf, g) * gain
        packed = jnp.zeros((2 * CELLS, 128), F32)
        for i, v in enumerate((total, total * total, grad_norm, grad_norm * total)):
            packed = jnp.where(lane == i, jnp.sum(v, axis=1, keepdims=True), packed)
        stat_all[t, g] = jnp.transpose(packed)[0:8]
        mine = stat_all.at[t, g]
        for d in (1, 2, 3):
            send(mine, mine, SLOTS["stat"] + (d - 1) * 2 + g, tp_dev(d))

    def normalise(g):
        for d in (1, 2, 3):
            got(stat_all.at[ring(t, -d, 4), g], SLOTS["stat"] + (d - 1) * 2 + g)
        totals = stat_all[0, g] + stat_all[1, g] + stat_all[2, g] + stat_all[3, g]
        packed = jnp.transpose(jnp.concatenate([totals, jnp.zeros((120, 128), F32)], axis=0))
        mean = packed[:, 0:1] / CH
        variance = packed[:, 1:2] / CH - mean * mean
        inv_std = 1.0 / jnp.sqrt(variance + 1e-05)
        grad_mean = packed[:, 2:3] / CH
        cross_mean = inv_std * (packed[:, 3:4] - mean * packed[:, 2:3]) / CH
        normed = (mixed[g] - mean) * inv_std
        rows = cells_of(cbuf, g)
        grad = (inv_std * (rows * gain - grad_mean - normed * cross_mean)).astype(BF)
        gmix[g] = grad
        def term(dst):
            part = nt(grad, wcol[ring(t - dst, 0, 4)])
            return jnp.concatenate([part[:CELLS], part[CELLS:]], axis=1).astype(BF)

        sum_start("gatt", ga_send, ga_recv, ga_relay, g, term)
        base = xbuf[t, pl.ds(2 * g, 2)].reshape(2 * CELLS, SH).astype(F32)
        obuf[pl.ds(2 * g, 2)] = (base + (gain * normed + shift)).astype(BF).reshape(2, 2, 2, 16, SH)
        gacc[0:1, :] += jnp.sum(rows * normed, axis=0, keepdims=True)
        gacc[1:2, :] += jnp.sum(rows, axis=0, keepdims=True)

    def backward(g):
        total = sum_end("gatt", ga_send, ga_recv, g)
        grad_att = unpack(total.astype(BF))
        heads = range(HEADS)
        ga = [grad_att[:, h * HD:(h + 1) * HD] for h in heads]
        prob = [probs[g, h] for h in heads]
        q_hat = [qs[g, h] for h in heads]
        k_hat = [ks[g, h] for h in heads]
        grad_prob = [nt(ga[h], vs[g, h]) for h in heads]
        grads_v = [tn(prob[h], ga[h]) for h in heads]
        prob_f = [prob[h].astype(F32) for h in heads]
        inner = [jnp.sum(prob_f[h] * grad_prob[h], axis=1, keepdims=True) for h in heads]
        grad_logit = [prob_f[h] * (grad_prob[h] - inner[h]) for h in heads]
        grad_cos = [(grad_logit[h] * scales[:, h:h + 1]).astype(BF) for h in heads]
        gq = [nn(grad_cos[h], k_hat[h]) for h in heads]
        gk = [tn(grad_cos[h], q_hat[h]) for h in heads]
        for h in heads:
            tacc[h] += grad_logit[h]
            sacc[h] += grad_logit[h] * coss[g, h]
        q_float = [q_hat[h].astype(F32) for h in heads]
        k_float = [k_hat[h].astype(F32) for h in heads]
        q_in = [jnp.sum(q_float[h] * gq[h], axis=1, keepdims=True) for h in heads]
        k_in = [jnp.sum(k_float[h] * gk[h], axis=1, keepdims=True) for h in heads]
        grads_q = [(gq[h] - q_float[h] * q_in[h]) * rqs[g, h] for h in heads]
        grads_k = [(gk[h] - k_float[h] * k_in[h]) * rks[g, h] for h in heads]
        stacked = jnp.concatenate(grads_q + grads_k + grads_v, axis=1).astype(BF)
        def term(dst):
            return nn(stacked, wt[:, pl.ds(pl.multiple_of(dst * SH, 128), SH)]).astype(BF)

        sum_start("gsh", gs_send, gs_recv, gs_relay, g, term)

    def finish(g):
        total = sum_end("gsh", gs_send, gs_recv, g) + cells_of(cbuf, g)
        gobuf[pl.ds(2 * g, 2)] = total.astype(BF).reshape(2, 2, 2, 16, SH)

    def give_first(buf, out, base):
        out[1:3, 1:3] = buf[0]
        out[1:3, 3] = buf[1, :, 0]
        send(buf.at[1, :, 1], out.at[1:3, 0], base, (lat, lon_n, t))

    def give_second(buf, out, base):
        send(buf.at[2, 1], out.at[0, 1:3], base + 1, (lat_n, lon, t))
        send(buf.at[3, 0, 1], out.at[3, 0], base + 2, (lat, lon_n, t))
        send(buf.at[3, 1, 0], out.at[0, 3], base + 3, (lat_n, lon, t))
        send(buf.at[3, 1, 1], out.at[0, 0], base + 4, (lat_n, lon_n, t))
        out[3, 1:3] = buf[2, 0]
        out[3, 3] = buf[3, 0, 0]

    def back_parts(out):
        return [out.at[1:3, 0], out.at[0, 1:3], out.at[3, 0], out.at[0, 3], out.at[0, 0]]

    def weight_first():
        for group in range(4):
            wacc[group] = tn(unpack(abuf[group, 0]), gmix[0])

    def weight_start():
        for j in (0, 1):
            far = 2 * (1 - core) + j
            wc_send[j] = (wacc[far] + tn(unpack(abuf[far, 1]), gmix[1])).astype(BF)
        send(wc_send, wc_recv, SLOTS["w_core"], sib)
        for j in (0, 1):
            near = 2 * core + j
            wacc[near] = wacc[near] + tn(unpack(abuf[near, 1]), gmix[1])

    def rows_of(y, x):
        return pl.ds(pl.multiple_of(x * 48 + y * 16, 16), 16)

    def weight_plane():
        got(wc_recv, SLOTS["w_core"])
        for j in (0, 1):
            total = wacc[2 * core + j] + wc_recv[j].astype(F32)
            wacc[2 * core + j] = total
            wp_send[j] = total.astype(BF)
        for o in range(15):
            y, x = plane(o)

            @pl.when(y < 3)
            def _():
                send(wp_send.at[:, rows_of(y, x)], wp_recv.at[o], SLOTS["w_p"] + o, plane_dev(o))

    holder = t // 2 == core

    def weight_z():
        @pl.when(has_piece)
        def _():
            for o in range(15):
                got(wp_recv.at[o], SLOTS["w_p"] + o)
            for j in (0, 1):
                total = wacc[2 * core + j, rows_of(ly, lx), :]
                for o in range(15):
                    total = total + wp_recv[o, j].astype(F32)
                wp_sum[j] = total.astype(BF)
            for j in (0, 1):
                keeper = 2 * core + j
                for dz in range(4):
                    @pl.when((keeper != t) if dz == 0 else (keeper >= 0))
                    def _():
                        dev = (ring(zh, dz, 4) * 2 + core, lon, keeper)
                        send(wp_sum.at[j], bz.at[zh, t], SLOTS["w_z"] + zh * 4 + t, dev, SLOTS["w_zs"] + 4 * j + dz)

    def weight_back_plane():
        @pl.when(holder & has_piece)
        def _():
            bz[zh, t] = wp_sum[t % 2]
            for z in range(4):
                for src in range(4):
                    @pl.when((zh != z) | (t != src))
                    def _():
                        got(bz.at[z, src], SLOTS["w_z"] + z * 4 + src)

            for src in range(4):
                total = bz[0, src].astype(F32)
                for z in range(1, 4):
                    total = total + bz[z, src].astype(F32)
                out_w[rows_of(ly, lx), src * SH:(src + 1) * SH] = total.astype(BF)
            mine = out_w.at[rows_of(ly, lx)]
            for o in range(15):
                send(mine, mine, SLOTS["back_p"] + o, plane_dev(o))
            send(mine, mine, SLOTS["back_core"] + lx * 3 + ly, sib)

    def weight_back_core():
        @pl.when(holder)
        def _():
            for o in range(15):
                y, x = plane_from(o)

                @pl.when(y < 3)
                def _():
                    mine = out_w.at[rows_of(y, x)]
                    got(mine, SLOTS["back_p"] + o)
                    send(mine, mine, SLOTS["back_core"] + x * 3 + y, sib)

    def small_start():
        folded_t = [tacc[h, :CELLS, :CELLS] + tacc[h, CELLS:, CELLS:] for h in range(HEADS)]
        for c in range(NPAIR // 128):
            for h in range(HEADS):
                pair = [folded_t[h][2 * c + i:2 * c + i + 1, :] for i in (0, 1)]
                flat[h:h + 1, c * 128:(c + 1) * 128] = jnp.concatenate(pair, axis=1)
        spread = bsrow[0:HEADS, :]
        terms = flat[0:HEADS, :] * 16.0 * spread * (1.0 - spread)
        pad = jnp.zeros((8 - HEADS, NPAIR), F32)
        pieces = jnp.concatenate([v for p in split3(terms) for v in (p, pad)], axis=0).astype(BF)
        folded = nt(pieces, onehot[...])
        sm_p[lon] = folded[0:8] + folded[8:16] + folded[16:24]
        for h in range(HEADS):
            amount = jnp.sum(jnp.sum(sacc[h], axis=1, keepdims=True), axis=0, keepdims=True) * scales[:, h:h + 1]
            sm_p[lon, h:h + 1, TABLE - 1:TABLE] = amount
        sm_p[lon, 3:5, :] = gacc[0:2, 0:TABLE]
        sm_p[lon, 5:6, :] = jnp.concatenate([gacc[0:1, TABLE:SH], gacc[1:2, TABLE:SH]], axis=1)
        for o in range(15):
            send(sm_p.at[lon], sm_p.at[lon], SLOTS["s_p"] + o, plane_dev(o))

    def small_lat():
        for o in range(15):
            y, x = plane_from(o)
            got(sm_p.at[y * 4 + x], SLOTS["s_p"] + o)
        total = sm_p[0]
        for i in range(1, 16):
            total = total + sm_p[i]
        sm_l[lat] = total
        for d in range(1, 8):
            send(sm_l.at[lat], sm_l.at[lat], SLOTS["s_l"] + d - 1, (ring(lat, d, 8), lon, t))

    def small_end():
        for d in range(1, 8):
            got(sm_l.at[ring(lat, -d, 8)], SLOTS["s_l"] + d - 1)
        total = sm_l[0]
        for i in range(1, 8):
            total = total + sm_l[i]
        out_s[...] = jnp.zeros_like(out_s)
        out_s[0:2, 0:TABLE] = total[3:5]
        out_s[0:1, TABLE:SH] = total[5:6, 0:128]
        out_s[1:2, TABLE:SH] = total[5:6, 128:256]
        out_s[2:5, 0:TABLE] = total[0:3]

    def both(body):
        def step(g, carry):
            body(g)
            return carry

        lax.fori_loop(0, GROUPS, step, 0)

    both(forward)
    own[11].wait()
    for o in range(15):
        y, x = plane_from(o)

        @pl.when(y < 3)
        def _():
            got(piece(y, x), SLOTS["wcol_p"] + o)

    for i in (7, 8, 9, 10):
        own[i].wait()
    for i in range(5):
        got(halo_parts(cbuf)[i], SLOTS["halo_c"] + i)
    def drain_inputs():
        for base, parts in (("halo_f", halo_parts(x_own)), ("halo_c", halo_parts(cbuf))):
            for i in range(5):
                sent(parts[i], SLOTS[base] + i)
        for w in range(NWIN):
            spread_drain("fields", 4, xbuf.at[0, 0], w)

        @pl.when(has_piece)
        def _():
            for d in range(3):
                sent(wcol.at[0, 0:48, 0:128], SLOTS["wcol_z"] + d)
            for o in range(15):
                sent(wcol.at[1:4, 0:48, 0:128], SLOTS["wcol_p"] + o)

    def drain_middle():
        for g in range(GROUPS):
            spread_drain("att", 2, abuf.at[0, 0], g)
            for i in range(3):
                sent(stat_all.at[0, 0], SLOTS["stat"] + 2 * i + g)
                sent(ga_send.at[0, 0], SLOTS["gatt"] + 2 * i + g)
        sent(wc_send, SLOTS["w_core"])

    def drain_late():
        for i in range(5):
            sent(back_parts(out_f)[i], SLOTS["out_f"] + i)
        for o in range(15):
            sent(sm_p.at[0], SLOTS["s_p"] + o)

            @pl.when(plane(o)[0] < 3)
            def _():
                sent(wp_send.at[:, 0:16], SLOTS["w_p"] + o)

    def middle(g):
        mix(g)

        @pl.when(g == 1)
        def _():
            sum_relay("gatt", ga_send, ga_recv, ga_relay, 0)

        normalise(g)

    both(middle)
    weight_first()
    weight_start()
    sum_relay("gatt", ga_send, ga_recv, ga_relay, 1)
    drain_inputs()
    give_first(obuf, out_f, SLOTS["out_f"])
    give_second(obuf, out_f, SLOTS["out_f"])

    def last(g):
        @pl.when(g == 1)
        def _():
            weight_plane()
            sum_relay("gsh", gs_send, gs_recv, gs_relay, 0)

        backward(g)

    both(last)
    small_start()
    sum_relay("gsh", gs_send, gs_recv, gs_relay, 1)
    drain_middle()
    finish(0)
    give_first(gobuf, out_g, SLOTS["out_g"])
    weight_z()
    small_lat()
    drain_late()
    finish(1)
    give_second(gobuf, out_g, SLOTS["out_g"])
    weight_back_plane()
    small_end()
    weight_back_core()

    for i in range(5):
        got(back_parts(out_f)[i], SLOTS["out_f"] + i)
        got(back_parts(out_g)[i], SLOTS["out_g"] + i)

    for i in range(5):
        sent(back_parts(out_g)[i], SLOTS["out_g"] + i)
    for g in range(GROUPS):
        for i in range(3):
            sent(gs_send.at[0, 0], SLOTS["gsh"] + 2 * i + g)

    @pl.when(has_piece)
    def _():
        for d in range(3):
            for j in (0, 1):
                sent(wp_sum.at[j], SLOTS["w_zs"] + 4 * j + d + 1)
        for j in (0, 1):
            @pl.when(2 * core + j != t)
            def _():
                sent(wp_sum.at[j], SLOTS["w_zs"] + 4 * j)

    @pl.when(holder & has_piece)
    def _():
        for o in range(15):
            sent(out_w.at[0:16], SLOTS["back_p"] + o)
        sent(out_w.at[0:16], SLOTS["back_core"] + lx * 3 + ly)

    @pl.when(holder)
    def _():
        for o in range(15):
            y, x = plane_from(o)

            @pl.when(y < 3)
            def _():
                sent(out_w.at[0:16], SLOTS["back_core"] + x * 3 + y)

    for d in range(7):
        sent(sm_l.at[0], SLOTS["s_l"] + d)

    @pl.when(jnp.logical_not(holder))
    def _():
        for x in range(4):
            for y in range(3):
                got(out_w.at[x * 48 + y * 16:x * 48 + y * 16 + 16], SLOTS["back_core"] + x * 3 + y)


def per_device(
    fields, w_qkv, w_out, log_scale, bias_table, bias_index, mask_ids, norm_gain, norm_shift, cotangent
):
    rows = bias_table.shape[0]
    wt = w_qkv.transpose(1, 2, 0).reshape(3 * AW, CH)
    hbm = pl.BlockSpec(memory_space=pltpu.HBM)
    vmem = pl.BlockSpec(memory_space=pltpu.VMEM)
    scratch = [
        ((16, 16, SH), BF), ((16, 16, SH), BF), ((576, CH), BF), ((4, 4, 16, SH), BF), ((4, 4, 16, SH), BF), ((4, 4, 2, 2, 16, SH), BF), ((4, 2, 2, 16, SH), BF), ((4, AW, SH), BF),
        ((4, 2, CELLS, SH), BF), ((TABLE, NPAIR), BF), ((8, NPAIR), F32), ((8, NPAIR), F32), ((8, TABLE), F32),
        ((HEADS, 2 * CELLS, 2 * CELLS), F32), ((NWIN * CELLS, 1), F32),
        ((2, HEADS, 2 * CELLS, HD), BF), ((2, HEADS, 2 * CELLS, HD), BF), ((2, HEADS, 2 * CELLS, HD), BF),
        ((2, HEADS, 2 * CELLS, 2 * CELLS), BF), ((2, HEADS, 2 * CELLS, 2 * CELLS), F32),
        ((2, HEADS, 2 * CELLS, 1), F32), ((2, HEADS, 2 * CELLS, 1), F32),
        ((2, 2 * CELLS, SH), F32), ((4, 2, 8, 128), F32), ((2, 2 * CELLS, SH), BF),
        ((4, 2, CELLS, SH), BF), ((4, 2, CELLS, SH), BF), ((2, CELLS, SH), BF),
        ((4, 2, 2 * CELLS, SH), BF), ((4, 2, 2 * CELLS, SH), BF), ((2, 2 * CELLS, SH), BF),
        ((4, 2, 2, 16, SH), BF), ((4, 2, 2, 16, SH), BF),
        ((HEADS, 2 * CELLS, 2 * CELLS), F32), ((HEADS, 2 * CELLS, 2 * CELLS), F32), ((8, SH), F32), ((8, NPAIR), F32),
        ((2, AW, SH), BF), ((2, AW, SH), BF), ((4, AW, SH), F32),
        ((2, AW, SH), BF), ((15, 2, 16, SH), BF), ((2, 16, SH), BF), ((4, 4, 16, SH), BF),
        ((16, 8, TABLE), F32), ((8, 8, TABLE), F32),
    ]
    out_f, out_g, out_w, out_s = pl.pallas_call(
        whole_kernel,
        out_shape=(
            jax.ShapeDtypeStruct((4, 4, 16, SH), BF),
            jax.ShapeDtypeStruct((4, 4, 16, SH), BF),
            jax.ShapeDtypeStruct((AW, CH), BF),
            jax.ShapeDtypeStruct((8, SH), F32),
        ),
        in_specs=[hbm, hbm, hbm, hbm, vmem, vmem, vmem, vmem, vmem, vmem],
        out_specs=(vmem, vmem, vmem, vmem),
        scratch_shapes=[pltpu.VMEM(shape, kind) for shape, kind in scratch] + [
            pltpu.SemaphoreType.DMA((12,)),
            pltpu.SemaphoreType.DMA((COUNT,)),
            pltpu.SemaphoreType.DMA((COUNT,)),
        ],
        compiler_params=pltpu.CompilerParams(
            collective_id=0, has_side_effects=True, vmem_limit_bytes=60 * 1024 * 1024
        ),
        cost_estimate=pl.CostEstimate(flops=2_000_000_000, bytes_accessed=5_000_000, transcendentals=200_000),
    )(
        fields, cotangent, wt, w_out, log_scale.reshape(1, HEADS), bias_table.T, bias_index, mask_ids,
        norm_gain, norm_shift,
    )
    shapes = (
        (fields.shape, BF), (fields.shape, BF), ((AW, CH), BF), ((HEADS, rows), F32), ((HEADS,), F32),
        ((SH,), F32), ((SH,), F32),
    )
    block_out, grad_fields, grad_w_out, grad_table, grad_scale, grad_gain, grad_shift = pl.pallas_call(
        write_kernel,
        out_shape=tuple(jax.ShapeDtypeStruct(shape, kind) for shape, kind in shapes),
        in_specs=[vmem] * 4,
        out_specs=(vmem,) * 7,
        compiler_params=pltpu.CompilerParams(vmem_limit_bytes=60 * 1024 * 1024),
        cost_estimate=pl.CostEstimate(flops=1_000_000, bytes_accessed=2_000_000, transcendentals=0),
    )(out_f, out_g, out_w, out_s)
    return (block_out, grad_fields, grad_w_out, grad_table.T, grad_scale, grad_gain, grad_shift)


def solution(mesh):
    in_specs = (
        P("lat", "lon", "tp"), P(None, None, "tp"), P("tp", None), P("tp"), P(None, "tp"), P(),
        P("lat", "lon"), P("tp"), P("tp"), P("lat", "lon", "tp"),
    )
    out_specs = (
        P("lat", "lon", "tp"), P("lat", "lon", "tp"), P("tp", None), P(None, "tp"), P("tp"), P("tp"), P("tp"),
    )
    return jax.shard_map(per_device, mesh=mesh, in_specs=in_specs, out_specs=out_specs, check_vma=False)
```

```python
import jax
import jax.numpy as jnp
from jax import lax
from jax.experimental import pallas as pl
from jax.experimental.pallas import tpu as pltpu
from jax.sharding import PartitionSpec as P

MESH = pl.DeviceIdType.MESH
BF = jnp.bfloat16
F32 = jnp.float32

CH = 1536
SH = 384
HEADS = 3
HD = 64
AW = HEADS * HD
CELLS = 64
NWIN = 4
GROUPS = 2
WIN = 8
TABLE = 256
NPAIR = 4096

SLOTS = {}
COUNT = 0
for _name, _n in (
    ("halo_f", 5), ("halo_c", 5), ("fields", 16), ("wcol_z", 3), ("wcol_p", 15), ("att", 8), ("stat", 6),
    ("gatt", 8), ("gsh", 8), ("out_f", 5), ("out_g", 5), ("w_core", 1), ("w_p", 15), ("w_pair", 1), ("w_z", 8),
    ("w_zs", 4), ("back_p", 15), ("back_core", 12), ("s_p", 15), ("s_l", 3), ("s_far", 1),
):
    SLOTS[_name] = COUNT
    COUNT += _n

PLANE = [(dy, dx) for dy in range(4) for dx in range(4)][1:]


def nn(a, b):
    return lax.dot_general(a, b, (((1,), (0,)), ((), ())), preferred_element_type=F32)


def nt(a, b):
    return lax.dot_general(a, b, (((1,), (1,)), ((), ())), preferred_element_type=F32)


def tn(a, b):
    return lax.dot_general(a, b, (((0,), (0,)), ((), ())), preferred_element_type=F32)


def split3(value):
    high = value.astype(BF).astype(F32)
    middle = (value - high).astype(BF).astype(F32)
    return high, middle, value - high - middle


def swap_halves(first, second):
    low = lax.broadcasted_iota(jnp.int32, first.shape, 0) < 4
    return jnp.where(low, first, pltpu.roll(second, 4, 0)), jnp.where(low, pltpu.roll(first, 4, 0), second)


def cut_blocks(grid, blocks):
    for i in range(4):
        tiles = [[None, None] for _ in range(4)]
        for half in (0, 1):
            upper = grid[4 * i + 2 * half].astype(F32)
            lower = grid[4 * i + 2 * half + 1].astype(F32)
            for k in (0, 1):
                pair = swap_halves(upper[8 * k:8 * k + 8], lower[8 * k:8 * k + 8])
                tiles[2 * k][half], tiles[2 * k + 1][half] = pair
        for j in range(4):
            blocks[i, j] = jnp.concatenate(tiles[j], axis=0).astype(BF)


def join_blocks(blocks, grid):
    for i in range(4):
        for half in (0, 1):
            upper, lower = [], []
            for k in (0, 1):
                rows = slice(8 * half, 8 * half + 8)
                pair = swap_halves(blocks[i, 2 * k].astype(F32)[rows], blocks[i, 2 * k + 1].astype(F32)[rows])
                upper.append(pair[0])
                lower.append(pair[1])
            grid[4 * i + 2 * half] = jnp.concatenate(upper, axis=0).astype(BF)
            grid[4 * i + 2 * half + 1] = jnp.concatenate(lower, axis=0).astype(BF)


def write_kernel(blocks_f, blocks_g, weights, small, out_f, out_g, out_w, out_t, out_s, out_a, out_b):
    out_w[...] = weights[...]
    join_blocks(blocks_f, out_f)
    join_blocks(blocks_g, out_g)
    out_t[...] = small[2:2 + HEADS, 0:out_t.shape[1]]
    spare = small[2:2 + HEADS, TABLE - 1:TABLE]
    scales = jnp.transpose(jnp.concatenate([jnp.broadcast_to(spare, (HEADS, 128)), jnp.zeros((8 - HEADS, 128), F32)], axis=0))
    out_s[...] = scales[0:1, 0:HEADS].reshape(HEADS)
    out_a[...] = small[0]
    out_b[...] = small[1]


def whole_kernel(
    fields_hbm, cot_hbm, wt_hbm, wout, logs, table, index, mask, gain_ref, shift_ref,
    out_f, out_g, out_w, out_s,
    fields_grid, cot_grid, wt, fields, cot, xbuf, cbuf, wcol, abuf, onehot, bsrow, idx_row, tab_pad, bsig, lab_col, qs, ks, vs, probs, coss, rqs, rks,
    mixed, stat_all, gmix, ga_send, ga_recv, ga_relay, gs_send, gs_recv, gs_relay, obuf, gobuf, tacc, sacc, gacc, flat,
    wc_send, wc_recv, wacc, wp_send, wp_recv, wp_sum, wp_pair, wp_both, bz, sm_p, sm_l, sm_f, local_sem, ssem, rsem,
):
    lat = lax.axis_index("lat")
    lon = lax.axis_index("lon")
    t = lax.axis_index("tp")
    zh = lat // 2
    core = lat % 2
    ly = lon // 4
    lx = lon % 4

    def ring(value, by, count):
        return lax.rem(value + by + count, count)

    lat_p, lat_n = ring(lat, -1, 8), ring(lat, 1, 8)
    lon_p, lon_n = ring(lon, -1, 16), ring(lon, 1, 16)
    sib = (zh * 2 + (1 - core), lon, t)

    def tp_dev(d):
        return (lat, lon, ring(t, d, 4))

    def plane(o):
        return ring(ly, PLANE[o][0], 4), ring(lx, PLANE[o][1], 4)

    def plane_from(o):
        return ring(ly, -PLANE[o][0], 4), ring(lx, -PLANE[o][1], 4)

    def plane_dev(o):
        y, x = plane(o)
        return (lat, y * 4 + x, t)

    def z_dev(d):
        return (ring(zh, d, 4) * 2 + core, lon, t)

    def copy(src, dst, slot, dev, send_slot=None):
        return pltpu.make_async_remote_copy(
            src_ref=src, dst_ref=dst, send_sem=ssem.at[slot if send_slot is None else send_slot],
            recv_sem=rsem.at[slot], device_id=dev, device_id_type=MESH,
        )

    def send(src, dst, slot, dev, send_slot=None):
        copy(src, dst, slot, dev, send_slot).start()

    def got(dst, slot):
        copy(dst, dst, slot, sib).wait_recv()

    def sent(src, slot):
        copy(src, src, slot, sib).wait_send()

    own = []

    def keep(src, dst):
        own.append(pltpu.make_async_copy(src, dst, local_sem.at[len(own)]))
        own[-1].start()

    keep(fields_hbm, fields_grid)
    keep(cot_hbm, cot_grid)
    keep(wt_hbm, wt)

    z_pair = zh + 1 - 2 * (zh % 2)
    z_far = 3 - zh
    pair_devs = [sib, (z_pair * 2 + core, lon, t), (z_pair * 2 + (1 - core), lon, t)]

    partners = [plane_dev(o) for o in range(15)] + pair_devs
    partners += [(lat_p, lon, t), (lat_n, lon, t), (lat_p, lon_p, t), (lat_n, lon_n, t)]
    partners += [tp_dev(d) for d in (1, 2, 3)] + [(z_far * 2 + core, lon, ring(t, d, 4)) for d in range(4)]
    barrier = pltpu.get_barrier_semaphore()
    for dev in partners:
        pl.semaphore_signal(barrier, inc=1, device_id=dev, device_id_type=MESH)

    def keep_grid(grid, dst):
        keep(grid.at[1:3, 1:3], dst.at[0])
        keep(grid.at[1:3, 3], dst.at[1, :, 0])
        keep(grid.at[3, 1:3], dst.at[2, 0])
        keep(grid.at[3, 3], dst.at[3, 0, 0])

    x_own = xbuf.at[t]
    own[0].wait()
    cut_blocks(fields_grid, fields)
    keep_grid(fields, x_own)

    pl.semaphore_wait(barrier, len(partners))

    def halo(grid, dst, base):
        send(grid.at[1:3, 0], dst.at[1, :, 1], base, (lat, lon_p, t))
        send(grid.at[0, 1:3], dst.at[2, 1], base + 1, (lat_p, lon, t))
        send(grid.at[3, 0], dst.at[3, 0, 1], base + 2, (lat, lon_p, t))
        send(grid.at[0, 3], dst.at[3, 1, 0], base + 3, (lat_p, lon, t))
        send(grid.at[0, 0], dst.at[3, 1, 1], base + 4, (lat_p, lon_p, t))

    def halo_parts(dst):
        return [dst.at[1, :, 1], dst.at[2, 1], dst.at[3, 0, 1], dst.at[3, 1, 0], dst.at[3, 1, 1]]

    side = t // 2
    is_mid = (t == 1) | (t == 2)
    is_edge = jnp.logical_not(is_mid)
    partner = 2 * side + 1 - t % 2
    far_mid = 2 - side
    far_edge = 3 - 3 * side
    far_slot = jnp.where(is_mid, 1, 2)

    def on_line(where):
        return (lat, lon, where)

    def spread_start(name, n, src, dst, i):
        base = SLOTS[name] + i
        send(src, dst, base + n * far_slot, on_line(far_mid), base + n)

        @pl.when(is_mid)
        def _():
            send(src, dst, base + n, on_line(far_edge), base + 2 * n)

        send(src, dst, base, on_line(partner), base)

    def spread_relay(name, n, buf, i):
        base = SLOTS[name] + i

        @pl.when(is_mid)
        def _():
            chunk = buf.at[far_edge, i]
            got(chunk, base + 2 * n)
            send(chunk, chunk, base + 2 * n, on_line(partner), base + 3 * n)

    def spread_wait(name, n, buf, i):
        base = SLOTS[name] + i
        got(buf.at[partner, i], base)
        got(buf.at[far_mid, i], base + n)

        @pl.when(is_edge)
        def _():
            got(buf.at[far_edge, i], base + 2 * n)

    def spread_drain(name, n, chunk, i):
        base = SLOTS[name] + i
        sent(chunk, base)
        sent(chunk, base + n)

        @pl.when(is_mid)
        def _():
            sent(chunk, base + 2 * n)
            sent(chunk, base + 3 * n)

    def sum_start(name, part, recv, relay, g, term):
        base = SLOTS[name] + g
        part[far_edge, g] = term(far_edge)

        @pl.when(is_edge)
        def _():
            send(part.at[far_edge, g], relay.at[g], base + 6, on_line(partner), base + 4)

        part[far_mid, g] = term(far_mid)
        send(part.at[far_mid, g], recv.at[t, g], base + 2 * far_slot, on_line(far_mid), base + 2)
        part[partner, g] = term(partner)
        send(part.at[partner, g], recv.at[t, g], base, on_line(partner), base)
        part[t, g] = term(t)

    def sum_relay(name, part, recv, relay, g):
        base = SLOTS[name] + g

        @pl.when(is_mid)
        def _():
            got(relay.at[g], base + 6)
            part[far_edge, g] = (part[far_edge, g].astype(F32) + relay[g].astype(F32)).astype(BF)
            send(part.at[far_edge, g], recv.at[t, g], base + 2, on_line(far_edge), base + 4)

    def sum_end(name, part, recv, g):
        base = SLOTS[name] + g
        got(recv.at[partner, g], base)
        got(recv.at[far_mid, g], base + 2)

        @pl.when(is_mid)
        def _():
            got(recv.at[far_edge, g], base + 4)

        @pl.when(is_edge)
        def _():
            recv[far_edge, g] = jnp.zeros(recv.shape[2:], BF)

        total = part[t, g].astype(F32)
        for src in (partner, far_mid, far_edge):
            total = total + recv[src, g].astype(F32)
        return total

    def give_fields(w, src):
        spread_start("fields", 4, src, x_own.at[w], w)

    halo(fields, x_own, SLOTS["halo_f"])

    piece_rows = pl.ds(pl.multiple_of(lx * 48, 16), 48)
    has_piece = ly < 3

    def piece(y, x):
        rows = pl.ds(pl.multiple_of(x * 48, 16), 48)
        return wcol.at[1:4, rows, pl.ds(pl.multiple_of(y * 128, 128), 128)]

    @pl.when(has_piece)
    def _():
        for d in (1, 2, 3):
            cols = pl.ds(pl.multiple_of(ring(t, d, 4) * SH + ly * 128, 128), 128)
            here = pl.ds(pl.multiple_of(ly * 128, 128), 128)
            send(wout.at[piece_rows, cols], wcol.at[d, piece_rows, here], SLOTS["wcol_z"] + d - 1, tp_dev(d))

    give_fields(0, fields.at[1:3, 1:3])
    own[1].wait()
    cut_blocks(cot_grid, cot)
    keep_grid(cot, cbuf)
    keep(wout.at[:, pl.ds(pl.multiple_of(t * SH, 128), SH)], wcol.at[0])

    def place(n):
        a, b, c, d = (n >> 5) & 1, (n >> 4) & 1, (n >> 2) & 3, n & 3
        return 4 * a + c, 4 * b + d

    def iota(shape, dim):
        return lax.broadcasted_iota(jnp.int32, shape, dim)

    def hot(flag):
        return jnp.where(flag, 1.0, 0.0)

    row_of, col_of = place(iota((CELLS, CELLS), 0))
    order = hot(iota((CELLS, CELLS), 1) == row_of * WIN + col_of).astype(BF)
    swapped = nn(order, index[...].astype(F32).astype(BF)).astype(BF)
    idx = nt(swapped, order)
    for c in range(NPAIR // 128):
        idx_row[0:1, c * 128:(c + 1) * 128] = jnp.concatenate([idx[2 * c:2 * c + 1], idx[2 * c + 1:2 * c + 2]], axis=1)

    cell = iota((NWIN * CELLS, 16), 0)
    row_of, col_of = place(cell)
    row_of, col_of = row_of + WIN * (cell >> 7), col_of + WIN * ((cell >> 6) & 1)
    picked_rows = nn(hot(iota((NWIN * CELLS, 16), 1) == row_of).astype(BF), mask[...].astype(F32).astype(BF))
    labels = jnp.sum(hot(iota((NWIN * CELLS, 16), 1) == col_of) * picked_rows, axis=1, keepdims=True)
    lab_col[...] = labels + 4.0 * (iota((NWIN * CELLS, 1), 0) >> 6).astype(F32)

    own[4].wait()
    got(halo_parts(x_own)[0], SLOTS["halo_f"])
    give_fields(1, x_own.at[1])
    own[5].wait()
    got(halo_parts(x_own)[1], SLOTS["halo_f"] + 1)
    give_fields(2, x_own.at[2])
    own[6].wait()
    for part in (2, 3, 4):
        got(halo_parts(x_own)[part], SLOTS["halo_f"] + part)
    give_fields(3, x_own.at[3])

    @pl.when(has_piece)
    def _():
        for d in (1, 2, 3):
            here = pl.ds(pl.multiple_of(ly * 128, 128), 128)
            got(wcol.at[d, piece_rows, here], SLOTS["wcol_z"] + d - 1)
        for o in range(15):
            send(piece(ly, lx), piece(ly, lx), SLOTS["wcol_p"] + o, plane_dev(o))

    halo(cot, cbuf, SLOTS["halo_c"])

    tab_pad[...] = jnp.zeros_like(tab_pad)
    tab_pad[0:HEADS, 0:table.shape[1]] = table[...]
    tab = jnp.concatenate([*split3(tab_pad[...]), jnp.zeros((8, TABLE), F32)], axis=0).astype(BF)
    entry = iota((TABLE, 512), 0).astype(F32)
    for c in range(NPAIR // 512):
        span = slice(c * 512, (c + 1) * 512)
        picked = hot(entry == idx_row[0:1, span]).astype(BF)
        onehot[:, span] = picked
        parts = nn(tab, picked)
        bias = parts[0:8] + parts[8:16] + parts[16:24]
        sig = 1.0 / (1.0 + jnp.exp(-bias))
        bsrow[:, span] = sig
        for k in range(8):
            for h in range(HEADS):
                at = 8 * c + k
                pair = jnp.concatenate([16.0 * sig[h:h + 1, k * CELLS:(k + 1) * CELLS]] * 2, axis=1)
                bsig[h, at:at + 1, :] = pair
                bsig[h, CELLS + at:CELLS + at + 1, :] = pair
    tacc[...] = jnp.zeros_like(tacc)
    sacc[...] = jnp.zeros_like(sacc)
    gacc[...] = jnp.zeros_like(gacc)
    scales = jnp.exp(logs[...])

    own[2].wait()
    own[3].wait()

    eye = iota((2 * CELLS, 2 * CELLS), 0) == iota((2 * CELLS, 2 * CELLS), 1)

    def forward(g):
        for w in (2 * g, 2 * g + 1):
            spread_relay("fields", 4, xbuf, w)
        for w in (2 * g, 2 * g + 1):
            spread_wait("fields", 4, xbuf, w)
        proj = jnp.zeros((2 * CELLS, 3 * AW), F32)
        for src in range(4):
            proj = proj + nt(xbuf[src, pl.ds(2 * g, 2)].reshape(2 * CELLS, SH), wt[:, src * SH:(src + 1) * SH])
        column = lab_col[pl.ds(pl.multiple_of(2 * g * CELLS, 128), 128), :]
        row = jnp.sum(jnp.where(eye, column, 0.0), axis=0, keepdims=True)
        same = row == column
        heads = range(HEADS)

        def slot(kind, h):
            at = kind * AW + h * HD
            return proj[:, at:at + HD]

        q = [slot(0, h) for h in heads]
        k = [slot(1, h) for h in heads]
        v = [slot(2, h).astype(BF) for h in heads]
        rq = [lax.rsqrt(jnp.sum(q[h] * q[h], axis=1, keepdims=True) + 1e-06) for h in heads]
        rk = [lax.rsqrt(jnp.sum(k[h] * k[h], axis=1, keepdims=True) + 1e-06) for h in heads]
        q_hat = [(q[h] * rq[h]).astype(BF) for h in heads]
        k_hat = [(k[h] * rk[h]).astype(BF) for h in heads]
        cosine = [nt(q_hat[h], k_hat[h]) for h in heads]
        power = [scales[:, h:h + 1] * (cosine[h] - 1.0) + (bsig[h] - 16.0) for h in heads]
        weight = [jnp.where(same, jnp.exp(power[h]), 0.0) for h in heads]
        total = [jnp.sum(weight[h], axis=1, keepdims=True) for h in heads]
        prob = [(weight[h] * (1.0 / total[h])).astype(BF) for h in heads]
        attended = [nn(prob[h], v[h]).astype(BF) for h in heads]
        for i in (0, 1):
            for h in heads:
                at = i * AW + h * HD
                abuf[t, g, :, at:at + HD] = attended[h][i * CELLS:(i + 1) * CELLS]
        for h in heads:
            qs[g, h] = q_hat[h]
            ks[g, h] = k_hat[h]
            vs[g, h] = v[h]
            probs[g, h] = prob[h]
            coss[g, h] = cosine[h]
            rqs[g, h] = rq[h]
            rks[g, h] = rk[h]
        spread_start("att", 2, abuf.at[t, g], abuf.at[t, g], g)

    gain = gain_ref[...].reshape(1, SH)
    shift = shift_ref[...].reshape(1, SH)
    lane = iota((2 * CELLS, 128), 1)

    def unpack(pair):
        return jnp.concatenate([pair[:, :AW], pair[:, AW:]], axis=0)

    def cells_of(buf, g):
        return buf[pl.ds(2 * g, 2)].reshape(2 * CELLS, SH).astype(F32)

    def mix(g):
        spread_relay("att", 2, abuf, g)
        spread_wait("att", 2, abuf, g)
        total = jnp.zeros((2 * CELLS, SH), F32)
        for d in range(4):
            total = total + nn(unpack(abuf[ring(t, -d, 4), g]), wcol[d])
        mixed[g] = total
        grad_norm = cells_of(cbuf, g) * gain
        packed = jnp.zeros((2 * CELLS, 128), F32)
        for i, v in enumerate((total, total * total, grad_norm, grad_norm * total)):
            packed = jnp.where(lane == i, jnp.sum(v, axis=1, keepdims=True), packed)
        stat_all[t, g] = jnp.transpose(packed)[0:8]
        mine = stat_all.at[t, g]
        for d in (1, 2, 3):
            send(mine, mine, SLOTS["stat"] + (d - 1) * 2 + g, tp_dev(d))

    def normalise(g):
        for d in (1, 2, 3):
            got(stat_all.at[ring(t, -d, 4), g], SLOTS["stat"] + (d - 1) * 2 + g)
        totals = stat_all[0, g] + stat_all[1, g] + stat_all[2, g] + stat_all[3, g]
        packed = jnp.transpose(jnp.concatenate([totals, jnp.zeros((120, 128), F32)], axis=0))
        mean = packed[:, 0:1] / CH
        variance = packed[:, 1:2] / CH - mean * mean
        inv_std = 1.0 / jnp.sqrt(variance + 1e-05)
        grad_mean = packed[:, 2:3] / CH
        cross_mean = inv_std * (packed[:, 3:4] - mean * packed[:, 2:3]) / CH
        normed = (mixed[g] - mean) * inv_std
        rows = cells_of(cbuf, g)
        grad = (inv_std * (rows * gain - grad_mean - normed * cross_mean)).astype(BF)
        gmix[g] = grad
        def term(dst):
            part = nt(grad, wcol[ring(t - dst, 0, 4)])
            return jnp.concatenate([part[:CELLS], part[CELLS:]], axis=1).astype(BF)

        sum_start("gatt", ga_send, ga_recv, ga_relay, g, term)
        base = xbuf[t, pl.ds(2 * g, 2)].reshape(2 * CELLS, SH).astype(F32)
        obuf[pl.ds(2 * g, 2)] = (base + (gain * normed + shift)).astype(BF).reshape(2, 2, 2, 16, SH)
        gacc[0:1, :] += jnp.sum(rows * normed, axis=0, keepdims=True)
        gacc[1:2, :] += jnp.sum(rows, axis=0, keepdims=True)

    def backward(g):
        total = sum_end("gatt", ga_send, ga_recv, g)
        grad_att = unpack(total.astype(BF))
        heads = range(HEADS)
        ga = [grad_att[:, h * HD:(h + 1) * HD] for h in heads]
        prob = [probs[g, h] for h in heads]
        q_hat = [qs[g, h] for h in heads]
        k_hat = [ks[g, h] for h in heads]
        grad_prob = [nt(ga[h], vs[g, h]) for h in heads]
        grads_v = [tn(prob[h], ga[h]) for h in heads]
        prob_f = [prob[h].astype(F32) for h in heads]
        inner = [jnp.sum(prob_f[h] * grad_prob[h], axis=1, keepdims=True) for h in heads]
        grad_logit = [prob_f[h] * (grad_prob[h] - inner[h]) for h in heads]
        grad_cos = [(grad_logit[h] * scales[:, h:h + 1]).astype(BF) for h in heads]
        gq = [nn(grad_cos[h], k_hat[h]) for h in heads]
        gk = [tn(grad_cos[h], q_hat[h]) for h in heads]
        for h in heads:
            tacc[h] += grad_logit[h]
            sacc[h] += grad_logit[h] * coss[g, h]
        q_float = [q_hat[h].astype(F32) for h in heads]
        k_float = [k_hat[h].astype(F32) for h in heads]
        q_in = [jnp.sum(q_float[h] * gq[h], axis=1, keepdims=True) for h in heads]
        k_in = [jnp.sum(k_float[h] * gk[h], axis=1, keepdims=True) for h in heads]
        grads_q = [(gq[h] - q_float[h] * q_in[h]) * rqs[g, h] for h in heads]
        grads_k = [(gk[h] - k_float[h] * k_in[h]) * rks[g, h] for h in heads]
        stacked = jnp.concatenate(grads_q + grads_k + grads_v, axis=1).astype(BF)
        def term(dst):
            return nn(stacked, wt[:, pl.ds(pl.multiple_of(dst * SH, 128), SH)]).astype(BF)

        sum_start("gsh", gs_send, gs_recv, gs_relay, g, term)

    def finish(g):
        total = sum_end("gsh", gs_send, gs_recv, g) + cells_of(cbuf, g)
        gobuf[pl.ds(2 * g, 2)] = total.astype(BF).reshape(2, 2, 2, 16, SH)

    def give_first(buf, out, base):
        out[1:3, 1:3] = buf[0]
        out[1:3, 3] = buf[1, :, 0]
        send(buf.at[1, :, 1], out.at[1:3, 0], base, (lat, lon_n, t))

    def give_second(buf, out, base):
        send(buf.at[2, 1], out.at[0, 1:3], base + 1, (lat_n, lon, t))
        send(buf.at[3, 0, 1], out.at[3, 0], base + 2, (lat, lon_n, t))
        send(buf.at[3, 1, 0], out.at[0, 3], base + 3, (lat_n, lon, t))
        send(buf.at[3, 1, 1], out.at[0, 0], base + 4, (lat_n, lon_n, t))
        out[3, 1:3] = buf[2, 0]
        out[3, 3] = buf[3, 0, 0]

    def back_parts(out):
        return [out.at[1:3, 0], out.at[0, 1:3], out.at[3, 0], out.at[0, 3], out.at[0, 0]]

    def weight_first():
        for group in range(4):
            wacc[group] = tn(unpack(abuf[group, 0]), gmix[0])

    def weight_start():
        for j in (0, 1):
            far = 2 * (1 - core) + j
            wc_send[j] = (wacc[far] + tn(unpack(abuf[far, 1]), gmix[1])).astype(BF)
        send(wc_send, wc_recv, SLOTS["w_core"], sib)
        for j in (0, 1):
            near = 2 * core + j
            wacc[near] = wacc[near] + tn(unpack(abuf[near, 1]), gmix[1])

    def rows_of(y, x):
        return pl.ds(pl.multiple_of(x * 48 + y * 16, 16), 16)

    def weight_plane():
        got(wc_recv, SLOTS["w_core"])
        for j in (0, 1):
            total = wacc[2 * core + j] + wc_recv[j].astype(F32)
            wacc[2 * core + j] = total
            wp_send[j] = total.astype(BF)
        for o in range(15):
            y, x = plane(o)

            @pl.when(y < 3)
            def _():
                send(wp_send.at[:, rows_of(y, x)], wp_recv.at[o], SLOTS["w_p"] + o, plane_dev(o))

    holder = t // 2 == core

    def weight_z():
        @pl.when(has_piece)
        def _():
            for o in range(15):
                got(wp_recv.at[o], SLOTS["w_p"] + o)
            for j in (0, 1):
                total = wacc[2 * core + j, rows_of(ly, lx), :]
                for o in range(15):
                    total = total + wp_recv[o, j].astype(F32)
                wp_sum[j] = total.astype(BF)
            send(wp_sum, wp_pair, SLOTS["w_pair"], (z_pair * 2 + core, lon, t))

    def weight_far():
        @pl.when(has_piece)
        def _():
            got(wp_pair, SLOTS["w_pair"])
            wp_both[...] = (wp_sum[...].astype(F32) + wp_pair[...].astype(F32)).astype(BF)
            for j in (0, 1):
                keeper = 2 * core + j
                slot = SLOTS["w_z"] + (zh // 2) * 4 + t
                send(wp_both.at[j], bz.at[zh // 2, t], slot, (z_far * 2 + core, lon, keeper), SLOTS["w_zs"] + 2 * j)

                @pl.when(keeper != t)
                def _():
                    send(wp_both.at[j], bz.at[zh // 2, t], slot, (lat, lon, keeper), SLOTS["w_zs"] + 2 * j + 1)

    def weight_back_plane():
        @pl.when(holder & has_piece)
        def _():
            bz[zh // 2, t] = wp_both[t % 2]
            for z in range(2):
                for src in range(4):
                    @pl.when((zh // 2 != z) | (t != src))
                    def _():
                        got(bz.at[z, src], SLOTS["w_z"] + z * 4 + src)

            for src in range(4):
                total = bz[0, src].astype(F32) + bz[1, src].astype(F32)
                out_w[rows_of(ly, lx), src * SH:(src + 1) * SH] = total.astype(BF)
            mine = out_w.at[rows_of(ly, lx)]
            for o in range(15):
                send(mine, mine, SLOTS["back_p"] + o, plane_dev(o))
            send(mine, mine, SLOTS["back_core"] + lx * 3 + ly, sib)

    def weight_back_core():
        @pl.when(holder)
        def _():
            for o in range(15):
                y, x = plane_from(o)

                @pl.when(y < 3)
                def _():
                    mine = out_w.at[rows_of(y, x)]
                    got(mine, SLOTS["back_p"] + o)
                    send(mine, mine, SLOTS["back_core"] + x * 3 + y, sib)

    def small_start():
        folded_t = [tacc[h, :CELLS, :CELLS] + tacc[h, CELLS:, CELLS:] for h in range(HEADS)]
        for c in range(NPAIR // 128):
            for h in range(HEADS):
                pair = [folded_t[h][2 * c + i:2 * c + i + 1, :] for i in (0, 1)]
                flat[h:h + 1, c * 128:(c + 1) * 128] = jnp.concatenate(pair, axis=1)
        spread = bsrow[0:HEADS, :]
        terms = flat[0:HEADS, :] * 16.0 * spread * (1.0 - spread)
        pad = jnp.zeros((8 - HEADS, NPAIR), F32)
        pieces = jnp.concatenate([v for p in split3(terms) for v in (p, pad)], axis=0).astype(BF)
        folded = nt(pieces, onehot[...])
        sm_p[lon] = folded[0:8] + folded[8:16] + folded[16:24]
        for h in range(HEADS):
            amount = jnp.sum(jnp.sum(sacc[h], axis=1, keepdims=True), axis=0, keepdims=True) * scales[:, h:h + 1]
            sm_p[lon, h:h + 1, TABLE - 1:TABLE] = amount
        sm_p[lon, 3:5, :] = gacc[0:2, 0:TABLE]
        sm_p[lon, 5:6, :] = jnp.concatenate([gacc[0:1, TABLE:SH], gacc[1:2, TABLE:SH]], axis=1)
        for o in range(15):
            send(sm_p.at[lon], sm_p.at[lon], SLOTS["s_p"] + o, plane_dev(o))

    def small_lat():
        for o in range(15):
            y, x = plane_from(o)
            got(sm_p.at[y * 4 + x], SLOTS["s_p"] + o)
        total = sm_p[0]
        for i in range(1, 16):
            total = total + sm_p[i]
        sm_l[2 * (zh % 2) + core] = total
        mine = sm_l.at[2 * (zh % 2) + core]
        for i, dev in enumerate(pair_devs):
            send(mine, mine, SLOTS["s_l"] + i, dev)

    def small_far():
        for i, where in enumerate((2 * (zh % 2) + 1 - core, 2 * (1 - zh % 2) + core, 2 * (1 - zh % 2) + 1 - core)):
            got(sm_l.at[where], SLOTS["s_l"] + i)
        sm_f[0] = sm_l[0] + sm_l[1] + sm_l[2] + sm_l[3]
        send(sm_f.at[0], sm_f.at[1], SLOTS["s_far"], (z_far * 2 + core, lon, t))

    def small_end():
        got(sm_f.at[1], SLOTS["s_far"])
        total = sm_f[0] + sm_f[1]
        out_s[...] = jnp.zeros_like(out_s)
        out_s[0:2, 0:TABLE] = total[3:5]
        out_s[0:1, TABLE:SH] = total[5:6, 0:128]
        out_s[1:2, TABLE:SH] = total[5:6, 128:256]
        out_s[2:5, 0:TABLE] = total[0:3]

    def both(body):
        def step(g, carry):
            body(g)
            return carry

        lax.fori_loop(0, GROUPS, step, 0)

    both(forward)
    own[11].wait()
    for o in range(15):
        y, x = plane_from(o)

        @pl.when(y < 3)
        def _():
            got(piece(y, x), SLOTS["wcol_p"] + o)

    for i in (7, 8, 9, 10):
        own[i].wait()
    for i in range(5):
        got(halo_parts(cbuf)[i], SLOTS["halo_c"] + i)
    def drain_inputs():
        for base, parts in (("halo_f", halo_parts(x_own)), ("halo_c", halo_parts(cbuf))):
            for i in range(5):
                sent(parts[i], SLOTS[base] + i)
        for w in range(NWIN):
            spread_drain("fields", 4, xbuf.at[0, 0], w)

        @pl.when(has_piece)
        def _():
            for d in range(3):
                sent(wcol.at[0, 0:48, 0:128], SLOTS["wcol_z"] + d)
            for o in range(15):
                sent(wcol.at[1:4, 0:48, 0:128], SLOTS["wcol_p"] + o)

    def drain_middle():
        for g in range(GROUPS):
            spread_drain("att", 2, abuf.at[0, 0], g)
            for i in range(3):
                sent(stat_all.at[0, 0], SLOTS["stat"] + 2 * i + g)
                sent(ga_send.at[0, 0], SLOTS["gatt"] + 2 * i + g)
        sent(wc_send, SLOTS["w_core"])

    def drain_late():
        for i in range(5):
            sent(back_parts(out_f)[i], SLOTS["out_f"] + i)
        for o in range(15):
            sent(sm_p.at[0], SLOTS["s_p"] + o)

            @pl.when(plane(o)[0] < 3)
            def _():
                sent(wp_send.at[:, 0:16], SLOTS["w_p"] + o)

    def middle(g):
        mix(g)

        @pl.when(g == 1)
        def _():
            sum_relay("gatt", ga_send, ga_recv, ga_relay, 0)

        normalise(g)

    both(middle)
    weight_first()
    weight_start()
    sum_relay("gatt", ga_send, ga_recv, ga_relay, 1)
    drain_inputs()
    give_first(obuf, out_f, SLOTS["out_f"])
    give_second(obuf, out_f, SLOTS["out_f"])

    def last(g):
        @pl.when(g == 1)
        def _():
            weight_plane()
            sum_relay("gsh", gs_send, gs_recv, gs_relay, 0)

        backward(g)

    both(last)
    weight_z()
    small_start()
    sum_relay("gsh", gs_send, gs_recv, gs_relay, 1)
    weight_far()
    drain_middle()
    finish(0)
    give_first(gobuf, out_g, SLOTS["out_g"])
    small_lat()
    weight_back_plane()
    small_far()
    drain_late()
    finish(1)
    give_second(gobuf, out_g, SLOTS["out_g"])
    weight_back_core()
    small_end()

    for i in range(5):
        got(back_parts(out_f)[i], SLOTS["out_f"] + i)
        got(back_parts(out_g)[i], SLOTS["out_g"] + i)

    for i in range(5):
        sent(back_parts(out_g)[i], SLOTS["out_g"] + i)
    for g in range(GROUPS):
        for i in range(3):
            sent(gs_send.at[0, 0], SLOTS["gsh"] + 2 * i + g)

    @pl.when(has_piece)
    def _():
        sent(wp_sum, SLOTS["w_pair"])
        for j in (0, 1):
            sent(wp_both.at[j], SLOTS["w_zs"] + 2 * j)

            @pl.when(2 * core + j != t)
            def _():
                sent(wp_both.at[j], SLOTS["w_zs"] + 2 * j + 1)

    @pl.when(holder & has_piece)
    def _():
        for o in range(15):
            sent(out_w.at[0:16], SLOTS["back_p"] + o)
        sent(out_w.at[0:16], SLOTS["back_core"] + lx * 3 + ly)

    @pl.when(holder)
    def _():
        for o in range(15):
            y, x = plane_from(o)

            @pl.when(y < 3)
            def _():
                sent(out_w.at[0:16], SLOTS["back_core"] + x * 3 + y)

    for i in range(3):
        sent(sm_l.at[0], SLOTS["s_l"] + i)
    sent(sm_f.at[0], SLOTS["s_far"])

    @pl.when(jnp.logical_not(holder))
    def _():
        for x in range(4):
            for y in range(3):
                got(out_w.at[x * 48 + y * 16:x * 48 + y * 16 + 16], SLOTS["back_core"] + x * 3 + y)


def per_device(
    fields, w_qkv, w_out, log_scale, bias_table, bias_index, mask_ids, norm_gain, norm_shift, cotangent
):
    rows = bias_table.shape[0]
    wt = w_qkv.transpose(1, 2, 0).reshape(3 * AW, CH)
    hbm = pl.BlockSpec(memory_space=pltpu.HBM)
    vmem = pl.BlockSpec(memory_space=pltpu.VMEM)
    scratch = [
        ((16, 16, SH), BF), ((16, 16, SH), BF), ((576, CH), BF), ((4, 4, 16, SH), BF), ((4, 4, 16, SH), BF), ((4, 4, 2, 2, 16, SH), BF), ((4, 2, 2, 16, SH), BF), ((4, AW, SH), BF),
        ((4, 2, CELLS, SH), BF), ((TABLE, NPAIR), BF), ((8, NPAIR), F32), ((8, NPAIR), F32), ((8, TABLE), F32),
        ((HEADS, 2 * CELLS, 2 * CELLS), F32), ((NWIN * CELLS, 1), F32),
        ((2, HEADS, 2 * CELLS, HD), BF), ((2, HEADS, 2 * CELLS, HD), BF), ((2, HEADS, 2 * CELLS, HD), BF),
        ((2, HEADS, 2 * CELLS, 2 * CELLS), BF), ((2, HEADS, 2 * CELLS, 2 * CELLS), F32),
        ((2, HEADS, 2 * CELLS, 1), F32), ((2, HEADS, 2 * CELLS, 1), F32),
        ((2, 2 * CELLS, SH), F32), ((4, 2, 8, 128), F32), ((2, 2 * CELLS, SH), BF),
        ((4, 2, CELLS, SH), BF), ((4, 2, CELLS, SH), BF), ((2, CELLS, SH), BF),
        ((4, 2, 2 * CELLS, SH), BF), ((4, 2, 2 * CELLS, SH), BF), ((2, 2 * CELLS, SH), BF),
        ((4, 2, 2, 16, SH), BF), ((4, 2, 2, 16, SH), BF),
        ((HEADS, 2 * CELLS, 2 * CELLS), F32), ((HEADS, 2 * CELLS, 2 * CELLS), F32), ((8, SH), F32), ((8, NPAIR), F32),
        ((2, AW, SH), BF), ((2, AW, SH), BF), ((4, AW, SH), F32),
        ((2, AW, SH), BF), ((15, 2, 16, SH), BF), ((2, 16, SH), BF), ((2, 16, SH), BF), ((2, 16, SH), BF),
        ((2, 4, 16, SH), BF), ((16, 8, TABLE), F32), ((4, 8, TABLE), F32), ((2, 8, TABLE), F32),
    ]
    out_f, out_g, out_w, out_s = pl.pallas_call(
        whole_kernel,
        out_shape=(
            jax.ShapeDtypeStruct((4, 4, 16, SH), BF),
            jax.ShapeDtypeStruct((4, 4, 16, SH), BF),
            jax.ShapeDtypeStruct((AW, CH), BF),
            jax.ShapeDtypeStruct((8, SH), F32),
        ),
        in_specs=[hbm, hbm, hbm, hbm, vmem, vmem, vmem, vmem, vmem, vmem],
        out_specs=(vmem, vmem, vmem, vmem),
        scratch_shapes=[pltpu.VMEM(shape, kind) for shape, kind in scratch] + [
            pltpu.SemaphoreType.DMA((12,)),
            pltpu.SemaphoreType.DMA((COUNT,)),
            pltpu.SemaphoreType.DMA((COUNT,)),
        ],
        compiler_params=pltpu.CompilerParams(
            collective_id=0, has_side_effects=True, vmem_limit_bytes=60 * 1024 * 1024
        ),
        cost_estimate=pl.CostEstimate(flops=2_000_000_000, bytes_accessed=5_000_000, transcendentals=200_000),
    )(
        fields, cotangent, wt, w_out, log_scale.reshape(1, HEADS), bias_table.T, bias_index, mask_ids,
        norm_gain, norm_shift,
    )
    shapes = (
        (fields.shape, BF), (fields.shape, BF), ((AW, CH), BF), ((HEADS, rows), F32), ((HEADS,), F32),
        ((SH,), F32), ((SH,), F32),
    )
    block_out, grad_fields, grad_w_out, grad_table, grad_scale, grad_gain, grad_shift = pl.pallas_call(
        write_kernel,
        out_shape=tuple(jax.ShapeDtypeStruct(shape, kind) for shape, kind in shapes),
        in_specs=[vmem] * 4,
        out_specs=(vmem,) * 7,
        compiler_params=pltpu.CompilerParams(vmem_limit_bytes=60 * 1024 * 1024),
        cost_estimate=pl.CostEstimate(flops=1_000_000, bytes_accessed=2_000_000, transcendentals=0),
    )(out_f, out_g, out_w, out_s)
    return (block_out, grad_fields, grad_w_out, grad_table.T, grad_scale, grad_gain, grad_shift)


def solution(mesh):
    in_specs = (
        P("lat", "lon", "tp"), P(None, None, "tp"), P("tp", None), P("tp"), P(None, "tp"), P(),
        P("lat", "lon"), P("tp"), P("tp"), P("lat", "lon", "tp"),
    )
    out_specs = (
        P("lat", "lon", "tp"), P("lat", "lon", "tp"), P("tp", None), P(None, "tp"), P("tp"), P("tp"), P("tp"),
    )
    return jax.shard_map(per_device, mesh=mesh, in_specs=in_specs, out_specs=out_specs, check_vma=False)
```

```python
import jax
import jax.numpy as jnp
from jax import lax
from jax.experimental import pallas as pl
from jax.experimental.pallas import tpu as pltpu
from jax.sharding import PartitionSpec as P

MESH = pl.DeviceIdType.MESH
BF = jnp.bfloat16
F32 = jnp.float32

CH = 1536
SH = 384
HEADS = 3
HD = 64
AW = HEADS * HD
CELLS = 64
NWIN = 4
GROUPS = 2
WIN = 8
TABLE = 256
NPAIR = 4096

SLOTS = {}
COUNT = 0
for _name, _n in (
    ("halo_f", 5), ("halo_c", 5), ("fields", 16), ("wcol_z", 3), ("wcol_p", 15), ("att", 8), ("stat", 6),
    ("gatt", 8), ("gsh", 8), ("out_f", 5), ("out_g", 5), ("w_core", 1), ("w_p", 15), ("w_pair", 1), ("w_z", 8),
    ("w_zs", 4), ("back_p", 15), ("back_core", 12), ("s_p", 15), ("s_l", 3), ("s_far", 1),
):
    SLOTS[_name] = COUNT
    COUNT += _n

PLANE = [(dy, dx) for dy in range(4) for dx in range(4)][1:]


def nn(a, b):
    return lax.dot_general(a, b, (((1,), (0,)), ((), ())), preferred_element_type=F32)


def nt(a, b):
    return lax.dot_general(a, b, (((1,), (1,)), ((), ())), preferred_element_type=F32)


def tn(a, b):
    return lax.dot_general(a, b, (((0,), (0,)), ((), ())), preferred_element_type=F32)


def split3(value):
    high = value.astype(BF).astype(F32)
    middle = (value - high).astype(BF).astype(F32)
    return high, middle, value - high - middle


def swap_halves(first, second):
    low = lax.broadcasted_iota(jnp.int32, first.shape, 0) < 4
    return jnp.where(low, first, pltpu.roll(second, 4, 0)), jnp.where(low, pltpu.roll(first, 4, 0), second)


def cut_blocks(grid, blocks):
    for i in range(4):
        tiles = [[None, None] for _ in range(4)]
        for half in (0, 1):
            upper = grid[4 * i + 2 * half].astype(F32)
            lower = grid[4 * i + 2 * half + 1].astype(F32)
            for k in (0, 1):
                pair = swap_halves(upper[8 * k:8 * k + 8], lower[8 * k:8 * k + 8])
                tiles[2 * k][half], tiles[2 * k + 1][half] = pair
        for j in range(4):
            blocks[i, j] = jnp.concatenate(tiles[j], axis=0).astype(BF)


def join_blocks(blocks, grid):
    for i in range(4):
        for half in (0, 1):
            upper, lower = [], []
            for k in (0, 1):
                rows = slice(8 * half, 8 * half + 8)
                pair = swap_halves(blocks[i, 2 * k].astype(F32)[rows], blocks[i, 2 * k + 1].astype(F32)[rows])
                upper.append(pair[0])
                lower.append(pair[1])
            grid[4 * i + 2 * half] = jnp.concatenate(upper, axis=0).astype(BF)
            grid[4 * i + 2 * half + 1] = jnp.concatenate(lower, axis=0).astype(BF)


def write_kernel(blocks_f, blocks_g, weights, small, out_f, out_g, out_w, out_t, out_s, out_a, out_b):
    out_w[...] = weights[...]
    join_blocks(blocks_f, out_f)
    join_blocks(blocks_g, out_g)
    out_t[...] = small[2:2 + HEADS, 0:out_t.shape[1]]
    spare = small[2:2 + HEADS, TABLE - 1:TABLE]
    scales = jnp.transpose(jnp.concatenate([jnp.broadcast_to(spare, (HEADS, 128)), jnp.zeros((8 - HEADS, 128), F32)], axis=0))
    out_s[...] = scales[0:1, 0:HEADS].reshape(HEADS)
    out_a[...] = small[0]
    out_b[...] = small[1]


def whole_kernel(
    fields_hbm, cot_hbm, wt_hbm, wout, logs, table, index, mask, gain_ref, shift_ref,
    out_f, out_g, out_w, out_s,
    fields_grid, cot_grid, wt, fields, cot, xbuf, cbuf, wcol, abuf, onehot, bsrow, idx_row, tab_pad, bsig, lab_col, qs, ks, vs, probs, coss, rqs, rks,
    mixed, stat_all, gmix, ga_send, ga_recv, ga_relay, gs_send, gs_recv, gs_relay, obuf, gobuf, tacc, sacc, gacc, flat,
    wc_send, wc_recv, wacc, wp_send, wp_recv, wp_sum, wp_pair, wp_both, bz, sm_p, sm_l, sm_f, local_sem, ssem, rsem,
):
    lat = lax.axis_index("lat")
    lon = lax.axis_index("lon")
    t = lax.axis_index("tp")
    zh = lat // 2
    core = lat % 2
    ly = lon // 4
    lx = lon % 4

    def ring(value, by, count):
        return lax.rem(value + by + count, count)

    lat_p, lat_n = ring(lat, -1, 8), ring(lat, 1, 8)
    lon_p, lon_n = ring(lon, -1, 16), ring(lon, 1, 16)
    sib = (zh * 2 + (1 - core), lon, t)

    def tp_dev(d):
        return (lat, lon, ring(t, d, 4))

    def plane(o):
        return ring(ly, PLANE[o][0], 4), ring(lx, PLANE[o][1], 4)

    def plane_from(o):
        return ring(ly, -PLANE[o][0], 4), ring(lx, -PLANE[o][1], 4)

    def plane_dev(o):
        y, x = plane(o)
        return (lat, y * 4 + x, t)

    def z_dev(d):
        return (ring(zh, d, 4) * 2 + core, lon, t)

    def copy(src, dst, slot, dev, send_slot=None):
        return pltpu.make_async_remote_copy(
            src_ref=src, dst_ref=dst, send_sem=ssem.at[slot if send_slot is None else send_slot],
            recv_sem=rsem.at[slot], device_id=dev, device_id_type=MESH,
        )

    def send(src, dst, slot, dev, send_slot=None):
        copy(src, dst, slot, dev, send_slot).start()

    def got(dst, slot):
        copy(dst, dst, slot, sib).wait_recv()

    def sent(src, slot):
        copy(src, src, slot, sib).wait_send()

    own = []

    def keep(src, dst):
        own.append(pltpu.make_async_copy(src, dst, local_sem.at[len(own)]))
        own[-1].start()

    keep(fields_hbm, fields_grid)
    keep(cot_hbm, cot_grid)
    keep(wt_hbm, wt)

    z_pair = zh + 1 - 2 * (zh % 2)
    z_far = 3 - zh
    pair_devs = [sib, (z_pair * 2 + core, lon, t), (z_pair * 2 + (1 - core), lon, t)]

    partners = [plane_dev(o) for o in range(15)] + pair_devs
    partners += [(lat_p, lon, t), (lat_n, lon, t), (lat_p, lon_p, t), (lat_n, lon_n, t)]
    partners += [tp_dev(d) for d in (1, 2, 3)] + [(z_far * 2 + core, lon, ring(t, d, 4)) for d in range(4)]
    barrier = pltpu.get_barrier_semaphore()
    for dev in partners:
        pl.semaphore_signal(barrier, inc=1, device_id=dev, device_id_type=MESH)

    def keep_grid(grid, dst):
        keep(grid.at[1:3, 1:3], dst.at[0])
        keep(grid.at[1:3, 3], dst.at[1, :, 0])
        keep(grid.at[3, 1:3], dst.at[2, 0])
        keep(grid.at[3, 3], dst.at[3, 0, 0])

    x_own = xbuf.at[t]
    own[0].wait()
    cut_blocks(fields_grid, fields)
    keep_grid(fields, x_own)

    pl.semaphore_wait(barrier, len(partners))

    def halo_lon(grid, dst, base):
        send(grid.at[1:3, 0], dst.at[1, :, 1], base, (lat, lon_p, t))
        send(grid.at[3, 0], dst.at[3, 0, 1], base + 2, (lat, lon_p, t))

    def halo_lat(grid, dst, base):
        send(grid.at[0, 1:3], dst.at[2, 1], base + 1, (lat_p, lon, t))
        send(grid.at[0, 3], dst.at[3, 1, 0], base + 3, (lat_p, lon, t))
        send(grid.at[0, 0], dst.at[3, 1, 1], base + 4, (lat_p, lon_p, t))

    def halo_parts(dst):
        return [dst.at[1, :, 1], dst.at[2, 1], dst.at[3, 0, 1], dst.at[3, 1, 0], dst.at[3, 1, 1]]

    side = t // 2
    is_mid = (t == 1) | (t == 2)
    is_edge = jnp.logical_not(is_mid)
    partner = 2 * side + 1 - t % 2
    far_mid = 2 - side
    far_edge = 3 - 3 * side
    far_slot = jnp.where(is_mid, 1, 2)

    def on_line(where):
        return (lat, lon, where)

    def spread_start(name, n, src, dst, i):
        base = SLOTS[name] + i
        send(src, dst, base + n * far_slot, on_line(far_mid), base + n)

        @pl.when(is_mid)
        def _():
            send(src, dst, base + n, on_line(far_edge), base + 2 * n)

        send(src, dst, base, on_line(partner), base)

    def spread_relay(name, n, buf, i):
        base = SLOTS[name] + i

        @pl.when(is_mid)
        def _():
            chunk = buf.at[far_edge, i]
            got(chunk, base + 2 * n)
            send(chunk, chunk, base + 2 * n, on_line(partner), base + 3 * n)

    def spread_wait(name, n, buf, i):
        base = SLOTS[name] + i
        got(buf.at[partner, i], base)
        got(buf.at[far_mid, i], base + n)

        @pl.when(is_edge)
        def _():
            got(buf.at[far_edge, i], base + 2 * n)

    def spread_drain(name, n, chunk, i):
        base = SLOTS[name] + i
        sent(chunk, base)
        sent(chunk, base + n)

        @pl.when(is_mid)
        def _():
            sent(chunk, base + 2 * n)
            sent(chunk, base + 3 * n)

    def sum_start(name, part, recv, relay, g, term):
        base = SLOTS[name] + g
        part[far_edge, g] = term(far_edge)

        @pl.when(is_edge)
        def _():
            send(part.at[far_edge, g], relay.at[g], base + 6, on_line(partner), base + 4)

        part[far_mid, g] = term(far_mid)
        send(part.at[far_mid, g], recv.at[t, g], base + 2 * far_slot, on_line(far_mid), base + 2)
        part[partner, g] = term(partner)
        send(part.at[partner, g], recv.at[t, g], base, on_line(partner), base)
        part[t, g] = term(t)

    def sum_relay(name, part, recv, relay, g):
        base = SLOTS[name] + g

        @pl.when(is_mid)
        def _():
            got(relay.at[g], base + 6)
            part[far_edge, g] = (part[far_edge, g].astype(F32) + relay[g].astype(F32)).astype(BF)
            send(part.at[far_edge, g], recv.at[t, g], base + 2, on_line(far_edge), base + 4)

    def sum_end(name, part, recv, g):
        base = SLOTS[name] + g
        got(recv.at[partner, g], base)
        got(recv.at[far_mid, g], base + 2)

        @pl.when(is_mid)
        def _():
            got(recv.at[far_edge, g], base + 4)

        @pl.when(is_edge)
        def _():
            recv[far_edge, g] = jnp.zeros(recv.shape[2:], BF)

        total = part[t, g].astype(F32)
        for src in (partner, far_mid, far_edge):
            total = total + recv[src, g].astype(F32)
        return total

    def give_fields(w, src):
        spread_start("fields", 4, src, x_own.at[w], w)

    halo_lat(fields, x_own, SLOTS["halo_f"])
    halo_lon(fields, x_own, SLOTS["halo_f"])

    piece_rows = pl.ds(pl.multiple_of(lx * 48, 16), 48)
    has_piece = ly < 3

    def piece(y, x):
        rows = pl.ds(pl.multiple_of(x * 48, 16), 48)
        return wcol.at[1:4, rows, pl.ds(pl.multiple_of(y * 128, 128), 128)]

    @pl.when(has_piece)
    def _():
        for d in (1, 2, 3):
            cols = pl.ds(pl.multiple_of(ring(t, d, 4) * SH + ly * 128, 128), 128)
            here = pl.ds(pl.multiple_of(ly * 128, 128), 128)
            send(wout.at[piece_rows, cols], wcol.at[d, piece_rows, here], SLOTS["wcol_z"] + d - 1, tp_dev(d))

    give_fields(0, fields.at[1:3, 1:3])
    own[1].wait()
    cut_blocks(cot_grid, cot)
    keep_grid(cot, cbuf)
    keep(wout.at[:, pl.ds(pl.multiple_of(t * SH, 128), SH)], wcol.at[0])

    def place(n):
        a, b, c, d = (n >> 5) & 1, (n >> 4) & 1, (n >> 2) & 3, n & 3
        return 4 * a + c, 4 * b + d

    def iota(shape, dim):
        return lax.broadcasted_iota(jnp.int32, shape, dim)

    def hot(flag):
        return jnp.where(flag, 1.0, 0.0)

    row_of, col_of = place(iota((CELLS, CELLS), 0))
    order = hot(iota((CELLS, CELLS), 1) == row_of * WIN + col_of).astype(BF)
    swapped = nn(order, index[...].astype(F32).astype(BF)).astype(BF)
    idx = nt(swapped, order)
    for c in range(NPAIR // 128):
        idx_row[0:1, c * 128:(c + 1) * 128] = jnp.concatenate([idx[2 * c:2 * c + 1], idx[2 * c + 1:2 * c + 2]], axis=1)

    cell = iota((NWIN * CELLS, 16), 0)
    row_of, col_of = place(cell)
    row_of, col_of = row_of + WIN * (cell >> 7), col_of + WIN * ((cell >> 6) & 1)
    picked_rows = nn(hot(iota((NWIN * CELLS, 16), 1) == row_of).astype(BF), mask[...].astype(F32).astype(BF))
    labels = jnp.sum(hot(iota((NWIN * CELLS, 16), 1) == col_of) * picked_rows, axis=1, keepdims=True)
    lab_col[...] = labels + 4.0 * (iota((NWIN * CELLS, 1), 0) >> 6).astype(F32)

    own[4].wait()
    got(halo_parts(x_own)[0], SLOTS["halo_f"])
    give_fields(1, x_own.at[1])
    own[5].wait()
    got(halo_parts(x_own)[1], SLOTS["halo_f"] + 1)
    give_fields(2, x_own.at[2])
    own[6].wait()
    for part in (2, 3, 4):
        got(halo_parts(x_own)[part], SLOTS["halo_f"] + part)
    give_fields(3, x_own.at[3])

    @pl.when(has_piece)
    def _():
        for d in (1, 2, 3):
            here = pl.ds(pl.multiple_of(ly * 128, 128), 128)
            got(wcol.at[d, piece_rows, here], SLOTS["wcol_z"] + d - 1)
        for o in range(15):
            send(piece(ly, lx), piece(ly, lx), SLOTS["wcol_p"] + o, plane_dev(o))

    halo_lon(cot, cbuf, SLOTS["halo_c"])

    tab_pad[...] = jnp.zeros_like(tab_pad)
    tab_pad[0:HEADS, 0:table.shape[1]] = table[...]
    tab = jnp.concatenate([*split3(tab_pad[...]), jnp.zeros((8, TABLE), F32)], axis=0).astype(BF)
    entry = iota((TABLE, 512), 0).astype(F32)
    for c in range(NPAIR // 512):
        span = slice(c * 512, (c + 1) * 512)
        picked = hot(entry == idx_row[0:1, span]).astype(BF)
        onehot[:, span] = picked
        parts = nn(tab, picked)
        bias = parts[0:8] + parts[8:16] + parts[16:24]
        sig = 1.0 / (1.0 + jnp.exp(-bias))
        bsrow[:, span] = sig
        for k in range(8):
            for h in range(HEADS):
                at = 8 * c + k
                pair = jnp.concatenate([16.0 * sig[h:h + 1, k * CELLS:(k + 1) * CELLS]] * 2, axis=1)
                bsig[h, at:at + 1, :] = pair
                bsig[h, CELLS + at:CELLS + at + 1, :] = pair
    tacc[...] = jnp.zeros_like(tacc)
    sacc[...] = jnp.zeros_like(sacc)
    gacc[...] = jnp.zeros_like(gacc)
    scales = jnp.exp(logs[...])

    own[2].wait()
    own[3].wait()

    eye = iota((2 * CELLS, 2 * CELLS), 0) == iota((2 * CELLS, 2 * CELLS), 1)

    def forward(g):
        @pl.when(g == 0)
        def _():
            spread_relay("fields", 4, xbuf, 0)
            spread_relay("fields", 4, xbuf, 1)

        @pl.when(g == 1)
        def _():
            spread_relay("fields", 4, xbuf, 3)

        for w in (2 * g, 2 * g + 1):
            spread_wait("fields", 4, xbuf, w)
        proj = jnp.zeros((2 * CELLS, 3 * AW), F32)
        for src in range(4):
            proj = proj + nt(xbuf[src, pl.ds(2 * g, 2)].reshape(2 * CELLS, SH), wt[:, src * SH:(src + 1) * SH])

        @pl.when(g == 0)
        def _():
            spread_relay("fields", 4, xbuf, 2)

        column = lab_col[pl.ds(pl.multiple_of(2 * g * CELLS, 128), 128), :]
        row = jnp.sum(jnp.where(eye, column, 0.0), axis=0, keepdims=True)
        same = row == column
        heads = range(HEADS)

        def slot(kind, h):
            at = kind * AW + h * HD
            return proj[:, at:at + HD]

        q = [slot(0, h) for h in heads]
        k = [slot(1, h) for h in heads]
        v = [slot(2, h).astype(BF) for h in heads]
        rq = [lax.rsqrt(jnp.sum(q[h] * q[h], axis=1, keepdims=True) + 1e-06) for h in heads]
        rk = [lax.rsqrt(jnp.sum(k[h] * k[h], axis=1, keepdims=True) + 1e-06) for h in heads]
        q_hat = [(q[h] * rq[h]).astype(BF) for h in heads]
        k_hat = [(k[h] * rk[h]).astype(BF) for h in heads]
        cosine = [nt(q_hat[h], k_hat[h]) for h in heads]
        power = [scales[:, h:h + 1] * (cosine[h] - 1.0) + (bsig[h] - 16.0) for h in heads]
        weight = [jnp.where(same, jnp.exp(power[h]), 0.0) for h in heads]
        total = [jnp.sum(weight[h], axis=1, keepdims=True) for h in heads]
        prob = [(weight[h] * (1.0 / total[h])).astype(BF) for h in heads]
        attended = [nn(prob[h], v[h]).astype(BF) for h in heads]
        for i in (0, 1):
            for h in heads:
                at = i * AW + h * HD
                abuf[t, g, :, at:at + HD] = attended[h][i * CELLS:(i + 1) * CELLS]
        for h in heads:
            qs[g, h] = q_hat[h]
            ks[g, h] = k_hat[h]
            vs[g, h] = v[h]
            probs[g, h] = prob[h]
            coss[g, h] = cosine[h]
            rqs[g, h] = rq[h]
            rks[g, h] = rk[h]
        spread_start("att", 2, abuf.at[t, g], abuf.at[t, g], g)

    gain = gain_ref[...].reshape(1, SH)
    shift = shift_ref[...].reshape(1, SH)
    lane = iota((2 * CELLS, 128), 1)

    def unpack(pair):
        return jnp.concatenate([pair[:, :AW], pair[:, AW:]], axis=0)

    def cells_of(buf, g):
        return buf[pl.ds(2 * g, 2)].reshape(2 * CELLS, SH).astype(F32)

    def mix(g):
        spread_relay("att", 2, abuf, g)
        spread_wait("att", 2, abuf, g)
        total = jnp.zeros((2 * CELLS, SH), F32)
        for d in range(4):
            total = total + nn(unpack(abuf[ring(t, -d, 4), g]), wcol[d])
        mixed[g] = total
        grad_norm = cells_of(cbuf, g) * gain
        packed = jnp.zeros((2 * CELLS, 128), F32)
        for i, v in enumerate((total, total * total, grad_norm, grad_norm * total)):
            packed = jnp.where(lane == i, jnp.sum(v, axis=1, keepdims=True), packed)
        stat_all[t, g] = jnp.transpose(packed)[0:8]
        mine = stat_all.at[t, g]
        for d in (1, 2, 3):
            send(mine, mine, SLOTS["stat"] + (d - 1) * 2 + g, tp_dev(d))

    def normalise(g):
        for d in (1, 2, 3):
            got(stat_all.at[ring(t, -d, 4), g], SLOTS["stat"] + (d - 1) * 2 + g)
        totals = stat_all[0, g] + stat_all[1, g] + stat_all[2, g] + stat_all[3, g]
        packed = jnp.transpose(jnp.concatenate([totals, jnp.zeros((120, 128), F32)], axis=0))
        mean = packed[:, 0:1] / CH
        variance = packed[:, 1:2] / CH - mean * mean
        inv_std = 1.0 / jnp.sqrt(variance + 1e-05)
        grad_mean = packed[:, 2:3] / CH
        cross_mean = inv_std * (packed[:, 3:4] - mean * packed[:, 2:3]) / CH
        normed = (mixed[g] - mean) * inv_std
        rows = cells_of(cbuf, g)
        grad = (inv_std * (rows * gain - grad_mean - normed * cross_mean)).astype(BF)
        gmix[g] = grad
        def term(dst):
            part = nt(grad, wcol[ring(t - dst, 0, 4)])
            return jnp.concatenate([part[:CELLS], part[CELLS:]], axis=1).astype(BF)

        sum_start("gatt", ga_send, ga_recv, ga_relay, g, term)
        base = xbuf[t, pl.ds(2 * g, 2)].reshape(2 * CELLS, SH).astype(F32)
        obuf[pl.ds(2 * g, 2)] = (base + (gain * normed + shift)).astype(BF).reshape(2, 2, 2, 16, SH)
        gacc[0:1, :] += jnp.sum(rows * normed, axis=0, keepdims=True)
        gacc[1:2, :] += jnp.sum(rows, axis=0, keepdims=True)

    def backward(g):
        total = sum_end("gatt", ga_send, ga_recv, g)
        grad_att = unpack(total.astype(BF))
        heads = range(HEADS)
        ga = [grad_att[:, h * HD:(h + 1) * HD] for h in heads]
        prob = [probs[g, h] for h in heads]
        q_hat = [qs[g, h] for h in heads]
        k_hat = [ks[g, h] for h in heads]
        grad_prob = [nt(ga[h], vs[g, h]) for h in heads]
        grads_v = [tn(prob[h], ga[h]) for h in heads]
        prob_f = [prob[h].astype(F32) for h in heads]
        inner = [jnp.sum(prob_f[h] * grad_prob[h], axis=1, keepdims=True) for h in heads]
        grad_logit = [prob_f[h] * (grad_prob[h] - inner[h]) for h in heads]
        grad_cos = [(grad_logit[h] * scales[:, h:h + 1]).astype(BF) for h in heads]
        gq = [nn(grad_cos[h], k_hat[h]) for h in heads]
        gk = [tn(grad_cos[h], q_hat[h]) for h in heads]
        for h in heads:
            tacc[h] += grad_logit[h]
            sacc[h] += grad_logit[h] * coss[g, h]
        q_float = [q_hat[h].astype(F32) for h in heads]
        k_float = [k_hat[h].astype(F32) for h in heads]
        q_in = [jnp.sum(q_float[h] * gq[h], axis=1, keepdims=True) for h in heads]
        k_in = [jnp.sum(k_float[h] * gk[h], axis=1, keepdims=True) for h in heads]
        grads_q = [(gq[h] - q_float[h] * q_in[h]) * rqs[g, h] for h in heads]
        grads_k = [(gk[h] - k_float[h] * k_in[h]) * rks[g, h] for h in heads]
        stacked = jnp.concatenate(grads_q + grads_k + grads_v, axis=1).astype(BF)
        def term(dst):
            return nn(stacked, wt[:, pl.ds(pl.multiple_of(dst * SH, 128), SH)]).astype(BF)

        sum_start("gsh", gs_send, gs_recv, gs_relay, g, term)

    def finish(g):
        total = sum_end("gsh", gs_send, gs_recv, g) + cells_of(cbuf, g)
        gobuf[pl.ds(2 * g, 2)] = total.astype(BF).reshape(2, 2, 2, 16, SH)

    def give_first(buf, out, base):
        out[1:3, 1:3] = buf[0]
        out[1:3, 3] = buf[1, :, 0]
        send(buf.at[1, :, 1], out.at[1:3, 0], base, (lat, lon_n, t))

    def give_second(buf, out, base):
        send(buf.at[2, 1], out.at[0, 1:3], base + 1, (lat_n, lon, t))
        send(buf.at[3, 0, 1], out.at[3, 0], base + 2, (lat, lon_n, t))
        send(buf.at[3, 1, 0], out.at[0, 3], base + 3, (lat_n, lon, t))
        send(buf.at[3, 1, 1], out.at[0, 0], base + 4, (lat_n, lon_n, t))
        out[3, 1:3] = buf[2, 0]
        out[3, 3] = buf[3, 0, 0]

    def back_parts(out):
        return [out.at[1:3, 0], out.at[0, 1:3], out.at[3, 0], out.at[0, 3], out.at[0, 0]]

    def weight_first():
        for group in range(4):
            wacc[group] = tn(unpack(abuf[group, 0]), gmix[0])

    def weight_start():
        for j in (0, 1):
            far = 2 * (1 - core) + j
            wc_send[j] = (wacc[far] + tn(unpack(abuf[far, 1]), gmix[1])).astype(BF)
        send(wc_send, wc_recv, SLOTS["w_core"], sib)
        for j in (0, 1):
            near = 2 * core + j
            wacc[near] = wacc[near] + tn(unpack(abuf[near, 1]), gmix[1])

    def rows_of(y, x):
        return pl.ds(pl.multiple_of(x * 48 + y * 16, 16), 16)

    def weight_plane():
        got(wc_recv, SLOTS["w_core"])
        for j in (0, 1):
            total = wacc[2 * core + j] + wc_recv[j].astype(F32)
            wacc[2 * core + j] = total
            wp_send[j] = total.astype(BF)
        for o in range(15):
            y, x = plane(o)

            @pl.when(y < 3)
            def _():
                send(wp_send.at[:, rows_of(y, x)], wp_recv.at[o], SLOTS["w_p"] + o, plane_dev(o))

    holder = t // 2 == core

    def weight_z():
        @pl.when(has_piece)
        def _():
            for o in range(15):
                got(wp_recv.at[o], SLOTS["w_p"] + o)
            for j in (0, 1):
                total = wacc[2 * core + j, rows_of(ly, lx), :]
                for o in range(15):
                    total = total + wp_recv[o, j].astype(F32)
                wp_sum[j] = total.astype(BF)
            send(wp_sum, wp_pair, SLOTS["w_pair"], (z_pair * 2 + core, lon, t))

    def weight_far():
        @pl.when(has_piece)
        def _():
            got(wp_pair, SLOTS["w_pair"])
            wp_both[...] = (wp_sum[...].astype(F32) + wp_pair[...].astype(F32)).astype(BF)
            for j in (0, 1):
                keeper = 2 * core + j
                slot = SLOTS["w_z"] + (zh // 2) * 4 + t
                send(wp_both.at[j], bz.at[zh // 2, t], slot, (z_far * 2 + core, lon, keeper), SLOTS["w_zs"] + 2 * j)

                @pl.when(keeper != t)
                def _():
                    send(wp_both.at[j], bz.at[zh // 2, t], slot, (lat, lon, keeper), SLOTS["w_zs"] + 2 * j + 1)

    def weight_back_plane():
        @pl.when(holder & has_piece)
        def _():
            bz[zh // 2, t] = wp_both[t % 2]
            for z in range(2):
                for src in range(4):
                    @pl.when((zh // 2 != z) | (t != src))
                    def _():
                        got(bz.at[z, src], SLOTS["w_z"] + z * 4 + src)

            for src in range(4):
                total = bz[0, src].astype(F32) + bz[1, src].astype(F32)
                out_w[rows_of(ly, lx), src * SH:(src + 1) * SH] = total.astype(BF)
            mine = out_w.at[rows_of(ly, lx)]
            for o in range(15):
                send(mine, mine, SLOTS["back_p"] + o, plane_dev(o))
            send(mine, mine, SLOTS["back_core"] + lx * 3 + ly, sib)

    def weight_back_core():
        @pl.when(holder)
        def _():
            for o in range(15):
                y, x = plane_from(o)

                @pl.when(y < 3)
                def _():
                    mine = out_w.at[rows_of(y, x)]
                    got(mine, SLOTS["back_p"] + o)
                    send(mine, mine, SLOTS["back_core"] + x * 3 + y, sib)

    def small_start():
        folded_t = [tacc[h, :CELLS, :CELLS] + tacc[h, CELLS:, CELLS:] for h in range(HEADS)]
        for c in range(NPAIR // 128):
            for h in range(HEADS):
                pair = [folded_t[h][2 * c + i:2 * c + i + 1, :] for i in (0, 1)]
                flat[h:h + 1, c * 128:(c + 1) * 128] = jnp.concatenate(pair, axis=1)
        spread = bsrow[0:HEADS, :]
        terms = flat[0:HEADS, :] * 16.0 * spread * (1.0 - spread)
        pad = jnp.zeros((8 - HEADS, NPAIR), F32)
        pieces = jnp.concatenate([v for p in split3(terms) for v in (p, pad)], axis=0).astype(BF)
        folded = nt(pieces, onehot[...])
        sm_p[lon] = folded[0:8] + folded[8:16] + folded[16:24]
        for h in range(HEADS):
            amount = jnp.sum(jnp.sum(sacc[h], axis=1, keepdims=True), axis=0, keepdims=True) * scales[:, h:h + 1]
            sm_p[lon, h:h + 1, TABLE - 1:TABLE] = amount
        sm_p[lon, 3:5, :] = gacc[0:2, 0:TABLE]
        sm_p[lon, 5:6, :] = jnp.concatenate([gacc[0:1, TABLE:SH], gacc[1:2, TABLE:SH]], axis=1)
        for o in range(15):
            send(sm_p.at[lon], sm_p.at[lon], SLOTS["s_p"] + o, plane_dev(o))

    def small_lat():
        for o in range(15):
            y, x = plane_from(o)
            got(sm_p.at[y * 4 + x], SLOTS["s_p"] + o)
        total = sm_p[0]
        for i in range(1, 16):
            total = total + sm_p[i]
        sm_l[2 * (zh % 2) + core] = total
        mine = sm_l.at[2 * (zh % 2) + core]
        for i, dev in enumerate(pair_devs):
            send(mine, mine, SLOTS["s_l"] + i, dev)

    def small_far():
        for i, where in enumerate((2 * (zh % 2) + 1 - core, 2 * (1 - zh % 2) + core, 2 * (1 - zh % 2) + 1 - core)):
            got(sm_l.at[where], SLOTS["s_l"] + i)
        sm_f[0] = sm_l[0] + sm_l[1] + sm_l[2] + sm_l[3]
        send(sm_f.at[0], sm_f.at[1], SLOTS["s_far"], (z_far * 2 + core, lon, t))

    def small_end():
        got(sm_f.at[1], SLOTS["s_far"])
        total = sm_f[0] + sm_f[1]
        out_s[...] = jnp.zeros_like(out_s)
        out_s[0:2, 0:TABLE] = total[3:5]
        out_s[0:1, TABLE:SH] = total[5:6, 0:128]
        out_s[1:2, TABLE:SH] = total[5:6, 128:256]
        out_s[2:5, 0:TABLE] = total[0:3]

    def both(body):
        def step(g, carry):
            body(g)
            return carry

        lax.fori_loop(0, GROUPS, step, 0)

    def first(g):
        forward(g)

        @pl.when(g == 0)
        def _():
            halo_lat(cot, cbuf, SLOTS["halo_c"])

    both(first)
    own[11].wait()
    for o in range(15):
        y, x = plane_from(o)

        @pl.when(y < 3)
        def _():
            got(piece(y, x), SLOTS["wcol_p"] + o)

    for i in (7, 8, 9, 10):
        own[i].wait()
    got(halo_parts(cbuf)[0], SLOTS["halo_c"])

    def drain_inputs():
        for base, parts in (("halo_f", halo_parts(x_own)), ("halo_c", halo_parts(cbuf))):
            for i in range(5):
                sent(parts[i], SLOTS[base] + i)
        for w in range(NWIN):
            spread_drain("fields", 4, xbuf.at[0, 0], w)

        @pl.when(has_piece)
        def _():
            for d in range(3):
                sent(wcol.at[0, 0:48, 0:128], SLOTS["wcol_z"] + d)
            for o in range(15):
                sent(wcol.at[1:4, 0:48, 0:128], SLOTS["wcol_p"] + o)

    def drain_middle():
        for g in range(GROUPS):
            spread_drain("att", 2, abuf.at[0, 0], g)
            for i in range(3):
                sent(stat_all.at[0, 0], SLOTS["stat"] + 2 * i + g)
                sent(ga_send.at[0, 0], SLOTS["gatt"] + 2 * i + g)
        sent(wc_send, SLOTS["w_core"])

    def drain_late():
        for i in range(5):
            sent(back_parts(out_f)[i], SLOTS["out_f"] + i)
        for o in range(15):
            sent(sm_p.at[0], SLOTS["s_p"] + o)

            @pl.when(plane(o)[0] < 3)
            def _():
                sent(wp_send.at[:, 0:16], SLOTS["w_p"] + o)

    def middle(g):
        @pl.when(g == 1)
        def _():
            for i in range(1, 5):
                got(halo_parts(cbuf)[i], SLOTS["halo_c"] + i)

        mix(g)

        @pl.when(g == 1)
        def _():
            sum_relay("gatt", ga_send, ga_recv, ga_relay, 0)
            weight_first()

        normalise(g)

    both(middle)
    weight_start()
    sum_relay("gatt", ga_send, ga_recv, ga_relay, 1)

    def last(g):
        @pl.when(g == 1)
        def _():
            weight_plane()
            sum_relay("gsh", gs_send, gs_recv, gs_relay, 0)
            give_first(obuf, out_f, SLOTS["out_f"])
            give_second(obuf, out_f, SLOTS["out_f"])

        backward(g)

    both(last)
    weight_z()
    sum_relay("gsh", gs_send, gs_recv, gs_relay, 1)
    small_start()
    weight_far()
    drain_inputs()
    drain_middle()
    finish(0)
    give_first(gobuf, out_g, SLOTS["out_g"])
    small_lat()
    weight_back_plane()
    small_far()
    drain_late()
    finish(1)
    give_second(gobuf, out_g, SLOTS["out_g"])
    weight_back_core()
    small_end()

    for i in range(5):
        got(back_parts(out_f)[i], SLOTS["out_f"] + i)
        got(back_parts(out_g)[i], SLOTS["out_g"] + i)

    for i in range(5):
        sent(back_parts(out_g)[i], SLOTS["out_g"] + i)
    for g in range(GROUPS):
        for i in range(3):
            sent(gs_send.at[0, 0], SLOTS["gsh"] + 2 * i + g)

    @pl.when(has_piece)
    def _():
        sent(wp_sum, SLOTS["w_pair"])
        for j in (0, 1):
            sent(wp_both.at[j], SLOTS["w_zs"] + 2 * j)

            @pl.when(2 * core + j != t)
            def _():
                sent(wp_both.at[j], SLOTS["w_zs"] + 2 * j + 1)

    @pl.when(holder & has_piece)
    def _():
        for o in range(15):
            sent(out_w.at[0:16], SLOTS["back_p"] + o)
        sent(out_w.at[0:16], SLOTS["back_core"] + lx * 3 + ly)

    @pl.when(holder)
    def _():
        for o in range(15):
            y, x = plane_from(o)

            @pl.when(y < 3)
            def _():
                sent(out_w.at[0:16], SLOTS["back_core"] + x * 3 + y)

    for i in range(3):
        sent(sm_l.at[0], SLOTS["s_l"] + i)
    sent(sm_f.at[0], SLOTS["s_far"])

    @pl.when(jnp.logical_not(holder))
    def _():
        for x in range(4):
            for y in range(3):
                got(out_w.at[x * 48 + y * 16:x * 48 + y * 16 + 16], SLOTS["back_core"] + x * 3 + y)


def per_device(
    fields, w_qkv, w_out, log_scale, bias_table, bias_index, mask_ids, norm_gain, norm_shift, cotangent
):
    rows = bias_table.shape[0]
    wt = w_qkv.transpose(1, 2, 0).reshape(3 * AW, CH)
    hbm = pl.BlockSpec(memory_space=pltpu.HBM)
    vmem = pl.BlockSpec(memory_space=pltpu.VMEM)
    scratch = [
        ((16, 16, SH), BF), ((16, 16, SH), BF), ((576, CH), BF), ((4, 4, 16, SH), BF), ((4, 4, 16, SH), BF), ((4, 4, 2, 2, 16, SH), BF), ((4, 2, 2, 16, SH), BF), ((4, AW, SH), BF),
        ((4, 2, CELLS, SH), BF), ((TABLE, NPAIR), BF), ((8, NPAIR), F32), ((8, NPAIR), F32), ((8, TABLE), F32),
        ((HEADS, 2 * CELLS, 2 * CELLS), F32), ((NWIN * CELLS, 1), F32),
        ((2, HEADS, 2 * CELLS, HD), BF), ((2, HEADS, 2 * CELLS, HD), BF), ((2, HEADS, 2 * CELLS, HD), BF),
        ((2, HEADS, 2 * CELLS, 2 * CELLS), BF), ((2, HEADS, 2 * CELLS, 2 * CELLS), F32),
        ((2, HEADS, 2 * CELLS, 1), F32), ((2, HEADS, 2 * CELLS, 1), F32),
        ((2, 2 * CELLS, SH), F32), ((4, 2, 8, 128), F32), ((2, 2 * CELLS, SH), BF),
        ((4, 2, CELLS, SH), BF), ((4, 2, CELLS, SH), BF), ((2, CELLS, SH), BF),
        ((4, 2, 2 * CELLS, SH), BF), ((4, 2, 2 * CELLS, SH), BF), ((2, 2 * CELLS, SH), BF),
        ((4, 2, 2, 16, SH), BF), ((4, 2, 2, 16, SH), BF),
        ((HEADS, 2 * CELLS, 2 * CELLS), F32), ((HEADS, 2 * CELLS, 2 * CELLS), F32), ((8, SH), F32), ((8, NPAIR), F32),
        ((2, AW, SH), BF), ((2, AW, SH), BF), ((4, AW, SH), F32),
        ((2, AW, SH), BF), ((15, 2, 16, SH), BF), ((2, 16, SH), BF), ((2, 16, SH), BF), ((2, 16, SH), BF),
        ((2, 4, 16, SH), BF), ((16, 8, TABLE), F32), ((4, 8, TABLE), F32), ((2, 8, TABLE), F32),
    ]
    out_f, out_g, out_w, out_s = pl.pallas_call(
        whole_kernel,
        out_shape=(
            jax.ShapeDtypeStruct((4, 4, 16, SH), BF),
            jax.ShapeDtypeStruct((4, 4, 16, SH), BF),
            jax.ShapeDtypeStruct((AW, CH), BF),
            jax.ShapeDtypeStruct((8, SH), F32),
        ),
        in_specs=[hbm, hbm, hbm, hbm, vmem, vmem, vmem, vmem, vmem, vmem],
        out_specs=(vmem, vmem, vmem, vmem),
        scratch_shapes=[pltpu.VMEM(shape, kind) for shape, kind in scratch] + [
            pltpu.SemaphoreType.DMA((12,)),
            pltpu.SemaphoreType.DMA((COUNT,)),
            pltpu.SemaphoreType.DMA((COUNT,)),
        ],
        compiler_params=pltpu.CompilerParams(
            collective_id=0, has_side_effects=True, vmem_limit_bytes=60 * 1024 * 1024
        ),
        cost_estimate=pl.CostEstimate(flops=2_000_000_000, bytes_accessed=5_000_000, transcendentals=200_000),
    )(
        fields, cotangent, wt, w_out, log_scale.reshape(1, HEADS), bias_table.T, bias_index, mask_ids,
        norm_gain, norm_shift,
    )
    shapes = (
        (fields.shape, BF), (fields.shape, BF), ((AW, CH), BF), ((HEADS, rows), F32), ((HEADS,), F32),
        ((SH,), F32), ((SH,), F32),
    )
    block_out, grad_fields, grad_w_out, grad_table, grad_scale, grad_gain, grad_shift = pl.pallas_call(
        write_kernel,
        out_shape=tuple(jax.ShapeDtypeStruct(shape, kind) for shape, kind in shapes),
        in_specs=[vmem] * 4,
        out_specs=(vmem,) * 7,
        compiler_params=pltpu.CompilerParams(vmem_limit_bytes=60 * 1024 * 1024),
        cost_estimate=pl.CostEstimate(flops=1_000_000, bytes_accessed=2_000_000, transcendentals=0),
    )(out_f, out_g, out_w, out_s)
    return (block_out, grad_fields, grad_w_out, grad_table.T, grad_scale, grad_gain, grad_shift)


def solution(mesh):
    in_specs = (
        P("lat", "lon", "tp"), P(None, None, "tp"), P("tp", None), P("tp"), P(None, "tp"), P(),
        P("lat", "lon"), P("tp"), P("tp"), P("lat", "lon", "tp"),
    )
    out_specs = (
        P("lat", "lon", "tp"), P("lat", "lon", "tp"), P("tp", None), P(None, "tp"), P("tp"), P("tp"), P("tp"),
    )
    return jax.shard_map(per_device, mesh=mesh, in_specs=in_specs, out_specs=out_specs, check_vma=False)
```

```python
import jax
import jax.numpy as jnp
from jax import lax
from jax.experimental import pallas as pl
from jax.experimental.pallas import tpu as pltpu
from jax.sharding import PartitionSpec as P

MESH = pl.DeviceIdType.MESH
BF = jnp.bfloat16
F32 = jnp.float32

CH = 1536
SH = 384
HEADS = 3
HD = 64
AW = HEADS * HD
CELLS = 64
NWIN = 4
GROUPS = 2
WIN = 8
TABLE = 256
NPAIR = 4096

SLOTS = {}
COUNT = 0
for _name, _n in (
    ("halo_f", 5), ("halo_c", 5), ("fields", 16), ("wcol_z", 3), ("wcol_p", 15), ("att", 8), ("stat", 6),
    ("gatt", 8), ("gsh", 8), ("out_f", 5), ("out_g", 5), ("w_core", 1), ("w_p", 15), ("w_pair", 1), ("w_z", 8),
    ("w_zs", 4), ("back_p", 15), ("back_core", 12), ("s_p", 15), ("s_l", 3), ("s_far", 1),
):
    SLOTS[_name] = COUNT
    COUNT += _n

PLANE = [(dy, dx) for dy in range(4) for dx in range(4)][1:]


def nn(a, b):
    return lax.dot_general(a, b, (((1,), (0,)), ((), ())), preferred_element_type=F32)


def nt(a, b):
    return lax.dot_general(a, b, (((1,), (1,)), ((), ())), preferred_element_type=F32)


def tn(a, b):
    return lax.dot_general(a, b, (((0,), (0,)), ((), ())), preferred_element_type=F32)


def split3(value):
    high = value.astype(BF).astype(F32)
    middle = (value - high).astype(BF).astype(F32)
    return high, middle, value - high - middle


def swap_halves(first, second):
    low = lax.broadcasted_iota(jnp.int32, first.shape, 0) < 4
    return jnp.where(low, first, pltpu.roll(second, 4, 0)), jnp.where(low, pltpu.roll(first, 4, 0), second)


def cut_blocks(grid, blocks):
    for i in range(4):
        tiles = [[None, None] for _ in range(4)]
        for half in (0, 1):
            upper = grid[4 * i + 2 * half].astype(F32)
            lower = grid[4 * i + 2 * half + 1].astype(F32)
            for k in (0, 1):
                pair = swap_halves(upper[8 * k:8 * k + 8], lower[8 * k:8 * k + 8])
                tiles[2 * k][half], tiles[2 * k + 1][half] = pair
        for j in range(4):
            blocks[i, j] = jnp.concatenate(tiles[j], axis=0).astype(BF)


def join_blocks(blocks, grid):
    for i in range(4):
        for half in (0, 1):
            upper, lower = [], []
            for k in (0, 1):
                rows = slice(8 * half, 8 * half + 8)
                pair = swap_halves(blocks[i, 2 * k].astype(F32)[rows], blocks[i, 2 * k + 1].astype(F32)[rows])
                upper.append(pair[0])
                lower.append(pair[1])
            grid[4 * i + 2 * half] = jnp.concatenate(upper, axis=0).astype(BF)
            grid[4 * i + 2 * half + 1] = jnp.concatenate(lower, axis=0).astype(BF)


def write_kernel(blocks_f, blocks_g, weights, small, out_f, out_g, out_w, out_t, out_s, out_a, out_b):
    out_w[...] = weights[...]
    join_blocks(blocks_f, out_f)
    join_blocks(blocks_g, out_g)
    out_t[...] = small[2:2 + HEADS, 0:out_t.shape[1]]
    spare = small[2:2 + HEADS, TABLE - 1:TABLE]
    scales = jnp.transpose(jnp.concatenate([jnp.broadcast_to(spare, (HEADS, 128)), jnp.zeros((8 - HEADS, 128), F32)], axis=0))
    out_s[...] = scales[0:1, 0:HEADS].reshape(HEADS)
    out_a[...] = small[0]
    out_b[...] = small[1]


def whole_kernel(
    fields_hbm, cot_hbm, wt_hbm, wout, logs, table, index, mask, gain_ref, shift_ref,
    out_f, out_g, out_w, out_s,
    fields_grid, cot_grid, wt, fields, cot, xbuf, cbuf, wcol, abuf, onehot, bsrow, idx_row, tab_pad, bsig, lab_col, qs, ks, vs, probs, coss, rqs, rks,
    mixed, stat_all, gmix, ga_send, ga_recv, ga_relay, gs_send, gs_recv, gs_relay, obuf, gobuf, tacc, sacc, gacc, flat,
    wc_send, wc_recv, wacc, wp_send, wp_recv, wp_sum, wp_pair, wp_both, bz, sm_p, sm_l, sm_f, local_sem, ssem, rsem,
):
    lat = lax.axis_index("lat")
    lon = lax.axis_index("lon")
    t = lax.axis_index("tp")
    zh = lat // 2
    core = lat % 2
    ly = lon // 4
    lx = lon % 4

    def ring(value, by, count):
        return lax.rem(value + by + count, count)

    lat_p, lat_n = ring(lat, -1, 8), ring(lat, 1, 8)
    lon_p, lon_n = ring(lon, -1, 16), ring(lon, 1, 16)
    sib = (zh * 2 + (1 - core), lon, t)

    def tp_dev(d):
        return (lat, lon, ring(t, d, 4))

    def plane(o):
        return ring(ly, PLANE[o][0], 4), ring(lx, PLANE[o][1], 4)

    def plane_from(o):
        return ring(ly, -PLANE[o][0], 4), ring(lx, -PLANE[o][1], 4)

    def plane_dev(o):
        y, x = plane(o)
        return (lat, y * 4 + x, t)

    def z_dev(d):
        return (ring(zh, d, 4) * 2 + core, lon, t)

    def copy(src, dst, slot, dev, send_slot=None):
        return pltpu.make_async_remote_copy(
            src_ref=src, dst_ref=dst, send_sem=ssem.at[slot if send_slot is None else send_slot],
            recv_sem=rsem.at[slot], device_id=dev, device_id_type=MESH,
        )

    def send(src, dst, slot, dev, send_slot=None):
        copy(src, dst, slot, dev, send_slot).start()

    def got(dst, slot):
        copy(dst, dst, slot, sib).wait_recv()

    def sent(src, slot):
        copy(src, src, slot, sib).wait_send()

    own = []

    def keep(src, dst):
        own.append(pltpu.make_async_copy(src, dst, local_sem.at[len(own)]))
        own[-1].start()

    keep(fields_hbm, fields_grid)
    keep(cot_hbm, cot_grid)
    keep(wt_hbm, wt)

    z_pair = zh + 1 - 2 * (zh % 2)
    z_far = 3 - zh
    pair_devs = [sib, (z_pair * 2 + core, lon, t), (z_pair * 2 + (1 - core), lon, t)]

    partners = [plane_dev(o) for o in range(15)] + pair_devs
    partners += [(lat_p, lon, t), (lat_n, lon, t), (lat_p, lon_p, t), (lat_n, lon_n, t)]
    partners += [tp_dev(d) for d in (1, 2, 3)] + [(z_far * 2 + core, lon, ring(t, d, 4)) for d in range(4)]
    barrier = pltpu.get_barrier_semaphore()
    for dev in partners:
        pl.semaphore_signal(barrier, inc=1, device_id=dev, device_id_type=MESH)

    def keep_grid(grid, dst):
        keep(grid.at[1:3, 1:3], dst.at[0])
        keep(grid.at[1:3, 3], dst.at[1, :, 0])
        keep(grid.at[3, 1:3], dst.at[2, 0])
        keep(grid.at[3, 3], dst.at[3, 0, 0])

    x_own = xbuf.at[t]
    own[0].wait()
    cut_blocks(fields_grid, fields)
    keep_grid(fields, x_own)

    pl.semaphore_wait(barrier, len(partners))

    def halo_lon(grid, dst, base):
        send(grid.at[1:3, 0], dst.at[1, :, 1], base, (lat, lon_p, t))
        send(grid.at[3, 0], dst.at[3, 0, 1], base + 2, (lat, lon_p, t))

    def halo_lat(grid, dst, base):
        send(grid.at[0, 1:3], dst.at[2, 1], base + 1, (lat_p, lon, t))
        send(grid.at[0, 3], dst.at[3, 1, 0], base + 3, (lat_p, lon, t))
        send(grid.at[0, 0], dst.at[3, 1, 1], base + 4, (lat_p, lon_p, t))

    def halo_parts(dst):
        return [dst.at[1, :, 1], dst.at[2, 1], dst.at[3, 0, 1], dst.at[3, 1, 0], dst.at[3, 1, 1]]

    side = t // 2
    is_mid = (t == 1) | (t == 2)
    is_edge = jnp.logical_not(is_mid)
    partner = 2 * side + 1 - t % 2
    far_mid = 2 - side
    far_edge = 3 - 3 * side
    far_slot = jnp.where(is_mid, 1, 2)

    def on_line(where):
        return (lat, lon, where)

    def spread_start(name, n, src, dst, i):
        base = SLOTS[name] + i
        send(src, dst, base + n * far_slot, on_line(far_mid), base + n)

        @pl.when(is_mid)
        def _():
            send(src, dst, base + n, on_line(far_edge), base + 2 * n)

        send(src, dst, base, on_line(partner), base)

    def spread_relay(name, n, buf, i):
        base = SLOTS[name] + i

        @pl.when(is_mid)
        def _():
            chunk = buf.at[far_edge, i]
            got(chunk, base + 2 * n)
            send(chunk, chunk, base + 2 * n, on_line(partner), base + 3 * n)

    def spread_wait(name, n, buf, i):
        base = SLOTS[name] + i
        got(buf.at[partner, i], base)
        got(buf.at[far_mid, i], base + n)

        @pl.when(is_edge)
        def _():
            got(buf.at[far_edge, i], base + 2 * n)

    def spread_drain(name, n, chunk, i):
        base = SLOTS[name] + i
        sent(chunk, base)
        sent(chunk, base + n)

        @pl.when(is_mid)
        def _():
            sent(chunk, base + 2 * n)
            sent(chunk, base + 3 * n)

    def sum_start(name, part, recv, relay, g, term):
        base = SLOTS[name] + g
        part[far_edge, g] = term(far_edge)

        @pl.when(is_edge)
        def _():
            send(part.at[far_edge, g], relay.at[g], base + 6, on_line(partner), base + 4)

        part[far_mid, g] = term(far_mid)
        send(part.at[far_mid, g], recv.at[t, g], base + 2 * far_slot, on_line(far_mid), base + 2)
        part[partner, g] = term(partner)
        send(part.at[partner, g], recv.at[t, g], base, on_line(partner), base)
        part[t, g] = term(t)

    def sum_relay(name, part, recv, relay, g):
        base = SLOTS[name] + g

        @pl.when(is_mid)
        def _():
            got(relay.at[g], base + 6)
            part[far_edge, g] = (part[far_edge, g].astype(F32) + relay[g].astype(F32)).astype(BF)
            send(part.at[far_edge, g], recv.at[t, g], base + 2, on_line(far_edge), base + 4)

    def sum_end(name, part, recv, g):
        base = SLOTS[name] + g
        got(recv.at[partner, g], base)
        got(recv.at[far_mid, g], base + 2)

        @pl.when(is_mid)
        def _():
            got(recv.at[far_edge, g], base + 4)

        @pl.when(is_edge)
        def _():
            recv[far_edge, g] = jnp.zeros(recv.shape[2:], BF)

        total = part[t, g].astype(F32)
        for src in (partner, far_mid, far_edge):
            total = total + recv[src, g].astype(F32)
        return total

    def give_fields(w, src):
        spread_start("fields", 4, src, x_own.at[w], w)

    halo_lat(fields, x_own, SLOTS["halo_f"])
    halo_lon(fields, x_own, SLOTS["halo_f"])

    piece_rows = pl.ds(pl.multiple_of(lx * 48, 16), 48)
    has_piece = ly < 3

    def piece(y, x):
        rows = pl.ds(pl.multiple_of(x * 48, 16), 48)
        return wcol.at[1:4, rows, pl.ds(pl.multiple_of(y * 128, 128), 128)]

    @pl.when(has_piece)
    def _():
        for d in (1, 2, 3):
            cols = pl.ds(pl.multiple_of(ring(t, d, 4) * SH + ly * 128, 128), 128)
            here = pl.ds(pl.multiple_of(ly * 128, 128), 128)
            send(wout.at[piece_rows, cols], wcol.at[d, piece_rows, here], SLOTS["wcol_z"] + d - 1, tp_dev(d))

    give_fields(0, fields.at[1:3, 1:3])
    own[1].wait()
    cut_blocks(cot_grid, cot)
    keep_grid(cot, cbuf)
    keep(wout.at[:, pl.ds(pl.multiple_of(t * SH, 128), SH)], wcol.at[0])

    def place(n):
        a, b, c, d = (n >> 5) & 1, (n >> 4) & 1, (n >> 2) & 3, n & 3
        return 4 * a + c, 4 * b + d

    def iota(shape, dim):
        return lax.broadcasted_iota(jnp.int32, shape, dim)

    def hot(flag):
        return jnp.where(flag, 1.0, 0.0)

    row_of, col_of = place(iota((CELLS, CELLS), 0))
    order = hot(iota((CELLS, CELLS), 1) == row_of * WIN + col_of).astype(BF)
    swapped = nn(order, index[...].astype(F32).astype(BF)).astype(BF)
    idx = nt(swapped, order)
    for c in range(NPAIR // 128):
        idx_row[0:1, c * 128:(c + 1) * 128] = jnp.concatenate([idx[2 * c:2 * c + 1], idx[2 * c + 1:2 * c + 2]], axis=1)

    cell = iota((NWIN * CELLS, 16), 0)
    row_of, col_of = place(cell)
    row_of, col_of = row_of + WIN * (cell >> 7), col_of + WIN * ((cell >> 6) & 1)
    picked_rows = nn(hot(iota((NWIN * CELLS, 16), 1) == row_of).astype(BF), mask[...].astype(F32).astype(BF))
    labels = jnp.sum(hot(iota((NWIN * CELLS, 16), 1) == col_of) * picked_rows, axis=1, keepdims=True)
    lab_col[...] = labels + 4.0 * (iota((NWIN * CELLS, 1), 0) >> 6).astype(F32)

    own[4].wait()
    got(halo_parts(x_own)[0], SLOTS["halo_f"])
    give_fields(1, x_own.at[1])
    own[5].wait()
    got(halo_parts(x_own)[1], SLOTS["halo_f"] + 1)
    give_fields(2, x_own.at[2])
    own[6].wait()
    for part in (2, 3, 4):
        got(halo_parts(x_own)[part], SLOTS["halo_f"] + part)
    give_fields(3, x_own.at[3])

    @pl.when(has_piece)
    def _():
        for d in (1, 2, 3):
            here = pl.ds(pl.multiple_of(ly * 128, 128), 128)
            got(wcol.at[d, piece_rows, here], SLOTS["wcol_z"] + d - 1)
        for o in range(15):
            send(piece(ly, lx), piece(ly, lx), SLOTS["wcol_p"] + o, plane_dev(o))

    halo_lon(cot, cbuf, SLOTS["halo_c"])

    spread_relay("fields", 4, xbuf, 0)

    tab_pad[...] = jnp.zeros_like(tab_pad)
    tab_pad[0:HEADS, 0:table.shape[1]] = table[...]
    tab = jnp.concatenate([*split3(tab_pad[...]), jnp.zeros((8, TABLE), F32)], axis=0).astype(BF)
    entry = iota((TABLE, 512), 0).astype(F32)
    for c in range(NPAIR // 512):
        span = slice(c * 512, (c + 1) * 512)
        picked = hot(entry == idx_row[0:1, span]).astype(BF)
        onehot[:, span] = picked
        parts = nn(tab, picked)
        bias = parts[0:8] + parts[8:16] + parts[16:24]
        sig = 1.0 / (1.0 + jnp.exp(-bias))
        bsrow[:, span] = sig
        for k in range(8):
            for h in range(HEADS):
                at = 8 * c + k
                pair = jnp.concatenate([16.0 * sig[h:h + 1, k * CELLS:(k + 1) * CELLS]] * 2, axis=1)
                bsig[h, at:at + 1, :] = pair
                bsig[h, CELLS + at:CELLS + at + 1, :] = pair
    spread_relay("fields", 4, xbuf, 1)
    tacc[...] = jnp.zeros_like(tacc)
    sacc[...] = jnp.zeros_like(sacc)
    gacc[...] = jnp.zeros_like(gacc)
    scales = jnp.exp(logs[...])

    own[2].wait()
    own[3].wait()

    eye = iota((2 * CELLS, 2 * CELLS), 0) == iota((2 * CELLS, 2 * CELLS), 1)

    def forward(g):
        @pl.when(g == 1)
        def _():
            spread_relay("fields", 4, xbuf, 3)

        for w in (2 * g, 2 * g + 1):
            spread_wait("fields", 4, xbuf, w)
        proj = jnp.zeros((2 * CELLS, 3 * AW), F32)
        for src in range(4):
            proj = proj + nt(xbuf[src, pl.ds(2 * g, 2)].reshape(2 * CELLS, SH), wt[:, src * SH:(src + 1) * SH])

        @pl.when(g == 0)
        def _():
            spread_relay("fields", 4, xbuf, 2)

        column = lab_col[pl.ds(pl.multiple_of(2 * g * CELLS, 128), 128), :]
        row = jnp.sum(jnp.where(eye, column, 0.0), axis=0, keepdims=True)
        same = row == column
        heads = range(HEADS)

        def slot(kind, h):
            at = kind * AW + h * HD
            return proj[:, at:at + HD]

        q = [slot(0, h) for h in heads]
        k = [slot(1, h) for h in heads]
        v = [slot(2, h).astype(BF) for h in heads]
        rq = [lax.rsqrt(jnp.sum(q[h] * q[h], axis=1, keepdims=True) + 1e-06) for h in heads]
        rk = [lax.rsqrt(jnp.sum(k[h] * k[h], axis=1, keepdims=True) + 1e-06) for h in heads]
        q_hat = [(q[h] * rq[h]).astype(BF) for h in heads]
        k_hat = [(k[h] * rk[h]).astype(BF) for h in heads]
        cosine = [nt(q_hat[h], k_hat[h]) for h in heads]
        power = [scales[:, h:h + 1] * (cosine[h] - 1.0) + (bsig[h] - 16.0) for h in heads]
        weight = [jnp.where(same, jnp.exp(power[h]), 0.0) for h in heads]
        total = [jnp.sum(weight[h], axis=1, keepdims=True) for h in heads]
        prob = [(weight[h] * (1.0 / total[h])).astype(BF) for h in heads]
        attended = [nn(prob[h], v[h]).astype(BF) for h in heads]
        for i in (0, 1):
            for h in heads:
                at = i * AW + h * HD
                abuf[t, g, :, at:at + HD] = attended[h][i * CELLS:(i + 1) * CELLS]
        for h in heads:
            qs[g, h] = q_hat[h]
            ks[g, h] = k_hat[h]
            vs[g, h] = v[h]
            probs[g, h] = prob[h]
            coss[g, h] = cosine[h]
            rqs[g, h] = rq[h]
            rks[g, h] = rk[h]
        spread_start("att", 2, abuf.at[t, g], abuf.at[t, g], g)

    gain = gain_ref[...].reshape(1, SH)
    shift = shift_ref[...].reshape(1, SH)
    lane = iota((2 * CELLS, 128), 1)

    def unpack(pair):
        return jnp.concatenate([pair[:, :AW], pair[:, AW:]], axis=0)

    def cells_of(buf, g):
        return buf[pl.ds(2 * g, 2)].reshape(2 * CELLS, SH).astype(F32)

    def mix(g):
        spread_wait("att", 2, abuf, g)
        total = jnp.zeros((2 * CELLS, SH), F32)
        for d in range(4):
            total = total + nn(unpack(abuf[ring(t, -d, 4), g]), wcol[d])
        mixed[g] = total
        grad_norm = cells_of(cbuf, g) * gain
        packed = jnp.zeros((2 * CELLS, 128), F32)
        for i, v in enumerate((total, total * total, grad_norm, grad_norm * total)):
            packed = jnp.where(lane == i, jnp.sum(v, axis=1, keepdims=True), packed)
        stat_all[t, g] = jnp.transpose(packed)[0:8]
        mine = stat_all.at[t, g]
        for d in (1, 2, 3):
            send(mine, mine, SLOTS["stat"] + (d - 1) * 2 + g, tp_dev(d))

    def normalise(g):
        for d in (1, 2, 3):
            got(stat_all.at[ring(t, -d, 4), g], SLOTS["stat"] + (d - 1) * 2 + g)
        totals = stat_all[0, g] + stat_all[1, g] + stat_all[2, g] + stat_all[3, g]
        packed = jnp.transpose(jnp.concatenate([totals, jnp.zeros((120, 128), F32)], axis=0))
        mean = packed[:, 0:1] / CH
        variance = packed[:, 1:2] / CH - mean * mean
        inv_std = 1.0 / jnp.sqrt(variance + 1e-05)
        grad_mean = packed[:, 2:3] / CH
        cross_mean = inv_std * (packed[:, 3:4] - mean * packed[:, 2:3]) / CH
        normed = (mixed[g] - mean) * inv_std
        rows = cells_of(cbuf, g)
        grad = (inv_std * (rows * gain - grad_mean - normed * cross_mean)).astype(BF)
        gmix[g] = grad
        def term(dst):
            part = nt(grad, wcol[ring(t - dst, 0, 4)])
            return jnp.concatenate([part[:CELLS], part[CELLS:]], axis=1).astype(BF)

        sum_start("gatt", ga_send, ga_recv, ga_relay, g, term)
        base = xbuf[t, pl.ds(2 * g, 2)].reshape(2 * CELLS, SH).astype(F32)
        obuf[pl.ds(2 * g, 2)] = (base + (gain * normed + shift)).astype(BF).reshape(2, 2, 2, 16, SH)
        gacc[0:1, :] += jnp.sum(rows * normed, axis=0, keepdims=True)
        gacc[1:2, :] += jnp.sum(rows, axis=0, keepdims=True)

    def backward(g):
        total = sum_end("gatt", ga_send, ga_recv, g)
        grad_att = unpack(total.astype(BF))
        heads = range(HEADS)
        ga = [grad_att[:, h * HD:(h + 1) * HD] for h in heads]
        prob = [probs[g, h] for h in heads]
        q_hat = [qs[g, h] for h in heads]
        k_hat = [ks[g, h] for h in heads]
        grad_prob = [nt(ga[h], vs[g, h]) for h in heads]
        grads_v = [tn(prob[h], ga[h]) for h in heads]
        prob_f = [prob[h].astype(F32) for h in heads]
        inner = [jnp.sum(prob_f[h] * grad_prob[h], axis=1, keepdims=True) for h in heads]
        grad_logit = [prob_f[h] * (grad_prob[h] - inner[h]) for h in heads]
        grad_cos = [(grad_logit[h] * scales[:, h:h + 1]).astype(BF) for h in heads]
        gq = [nn(grad_cos[h], k_hat[h]) for h in heads]
        gk = [tn(grad_cos[h], q_hat[h]) for h in heads]
        for h in heads:
            tacc[h] += grad_logit[h]
            sacc[h] += grad_logit[h] * coss[g, h]
        q_float = [q_hat[h].astype(F32) for h in heads]
        k_float = [k_hat[h].astype(F32) for h in heads]
        q_in = [jnp.sum(q_float[h] * gq[h], axis=1, keepdims=True) for h in heads]
        k_in = [jnp.sum(k_float[h] * gk[h], axis=1, keepdims=True) for h in heads]
        grads_q = [(gq[h] - q_float[h] * q_in[h]) * rqs[g, h] for h in heads]
        grads_k = [(gk[h] - k_float[h] * k_in[h]) * rks[g, h] for h in heads]
        stacked = jnp.concatenate(grads_q + grads_k + grads_v, axis=1).astype(BF)
        def term(dst):
            return nn(stacked, wt[:, pl.ds(pl.multiple_of(dst * SH, 128), SH)]).astype(BF)

        sum_start("gsh", gs_send, gs_recv, gs_relay, g, term)

    def finish(g):
        total = sum_end("gsh", gs_send, gs_recv, g) + cells_of(cbuf, g)
        gobuf[pl.ds(2 * g, 2)] = total.astype(BF).reshape(2, 2, 2, 16, SH)

    def give_first(buf, out, base):
        out[1:3, 1:3] = buf[0]
        out[1:3, 3] = buf[1, :, 0]
        send(buf.at[1, :, 1], out.at[1:3, 0], base, (lat, lon_n, t))

    def give_second(buf, out, base):
        send(buf.at[2, 1], out.at[0, 1:3], base + 1, (lat_n, lon, t))
        send(buf.at[3, 0, 1], out.at[3, 0], base + 2, (lat, lon_n, t))
        send(buf.at[3, 1, 0], out.at[0, 3], base + 3, (lat_n, lon, t))
        send(buf.at[3, 1, 1], out.at[0, 0], base + 4, (lat_n, lon_n, t))
        out[3, 1:3] = buf[2, 0]
        out[3, 3] = buf[3, 0, 0]

    def back_parts(out):
        return [out.at[1:3, 0], out.at[0, 1:3], out.at[3, 0], out.at[0, 3], out.at[0, 0]]

    def weight_first():
        for group in range(4):
            wacc[group] = tn(unpack(abuf[group, 0]), gmix[0])

    def weight_start():
        for j in (0, 1):
            far = 2 * (1 - core) + j
            wc_send[j] = (wacc[far] + tn(unpack(abuf[far, 1]), gmix[1])).astype(BF)
        send(wc_send, wc_recv, SLOTS["w_core"], sib)
        for j in (0, 1):
            near = 2 * core + j
            wacc[near] = wacc[near] + tn(unpack(abuf[near, 1]), gmix[1])

    def rows_of(y, x):
        return pl.ds(pl.multiple_of(x * 48 + y * 16, 16), 16)

    def weight_plane():
        got(wc_recv, SLOTS["w_core"])
        for j in (0, 1):
            total = wacc[2 * core + j] + wc_recv[j].astype(F32)
            wacc[2 * core + j] = total
            wp_send[j] = total.astype(BF)
        for o in range(15):
            y, x = plane(o)

            @pl.when(y < 3)
            def _():
                send(wp_send.at[:, rows_of(y, x)], wp_recv.at[o], SLOTS["w_p"] + o, plane_dev(o))

    holder = t // 2 == core

    def weight_z():
        @pl.when(has_piece)
        def _():
            for o in range(15):
                got(wp_recv.at[o], SLOTS["w_p"] + o)
            for j in (0, 1):
                total = wacc[2 * core + j, rows_of(ly, lx), :]
                for o in range(15):
                    total = total + wp_recv[o, j].astype(F32)
                wp_sum[j] = total.astype(BF)
            send(wp_sum, wp_pair, SLOTS["w_pair"], (z_pair * 2 + core, lon, t))

    def weight_far():
        @pl.when(has_piece)
        def _():
            got(wp_pair, SLOTS["w_pair"])
            wp_both[...] = (wp_sum[...].astype(F32) + wp_pair[...].astype(F32)).astype(BF)
            for j in (0, 1):
                keeper = 2 * core + j
                slot = SLOTS["w_z"] + (zh // 2) * 4 + t
                send(wp_both.at[j], bz.at[zh // 2, t], slot, (z_far * 2 + core, lon, keeper), SLOTS["w_zs"] + 2 * j)

                @pl.when(keeper != t)
                def _():
                    send(wp_both.at[j], bz.at[zh // 2, t], slot, (lat, lon, keeper), SLOTS["w_zs"] + 2 * j + 1)

    def weight_back_plane():
        @pl.when(holder & has_piece)
        def _():
            bz[zh // 2, t] = wp_both[t % 2]
            for z in range(2):
                for src in range(4):
                    @pl.when((zh // 2 != z) | (t != src))
                    def _():
                        got(bz.at[z, src], SLOTS["w_z"] + z * 4 + src)

            for src in range(4):
                total = bz[0, src].astype(F32) + bz[1, src].astype(F32)
                out_w[rows_of(ly, lx), src * SH:(src + 1) * SH] = total.astype(BF)
            mine = out_w.at[rows_of(ly, lx)]
            for o in range(15):
                send(mine, mine, SLOTS["back_p"] + o, plane_dev(o))
            send(mine, mine, SLOTS["back_core"] + lx * 3 + ly, sib)

    def weight_back_core():
        @pl.when(holder)
        def _():
            for o in range(15):
                y, x = plane_from(o)

                @pl.when(y < 3)
                def _():
                    mine = out_w.at[rows_of(y, x)]
                    got(mine, SLOTS["back_p"] + o)
                    send(mine, mine, SLOTS["back_core"] + x * 3 + y, sib)

    def small_start():
        folded_t = [tacc[h, :CELLS, :CELLS] + tacc[h, CELLS:, CELLS:] for h in range(HEADS)]
        for c in range(NPAIR // 128):
            for h in range(HEADS):
                pair = [folded_t[h][2 * c + i:2 * c + i + 1, :] for i in (0, 1)]
                flat[h:h + 1, c * 128:(c + 1) * 128] = jnp.concatenate(pair, axis=1)
        spread = bsrow[0:HEADS, :]
        terms = flat[0:HEADS, :] * 16.0 * spread * (1.0 - spread)
        pad = jnp.zeros((8 - HEADS, NPAIR), F32)
        pieces = jnp.concatenate([v for p in split3(terms) for v in (p, pad)], axis=0).astype(BF)
        folded = nt(pieces, onehot[...])
        sm_p[lon] = folded[0:8] + folded[8:16] + folded[16:24]
        for h in range(HEADS):
            amount = jnp.sum(jnp.sum(sacc[h], axis=1, keepdims=True), axis=0, keepdims=True) * scales[:, h:h + 1]
            sm_p[lon, h:h + 1, TABLE - 1:TABLE] = amount
        sm_p[lon, 3:5, :] = gacc[0:2, 0:TABLE]
        sm_p[lon, 5:6, :] = jnp.concatenate([gacc[0:1, TABLE:SH], gacc[1:2, TABLE:SH]], axis=1)
        for o in range(15):
            send(sm_p.at[lon], sm_p.at[lon], SLOTS["s_p"] + o, plane_dev(o))

    def small_lat():
        for o in range(15):
            y, x = plane_from(o)
            got(sm_p.at[y * 4 + x], SLOTS["s_p"] + o)
        total = sm_p[0]
        for i in range(1, 16):
            total = total + sm_p[i]
        sm_l[2 * (zh % 2) + core] = total
        mine = sm_l.at[2 * (zh % 2) + core]
        for i, dev in enumerate(pair_devs):
            send(mine, mine, SLOTS["s_l"] + i, dev)

    def small_far():
        for i, where in enumerate((2 * (zh % 2) + 1 - core, 2 * (1 - zh % 2) + core, 2 * (1 - zh % 2) + 1 - core)):
            got(sm_l.at[where], SLOTS["s_l"] + i)
        sm_f[0] = sm_l[0] + sm_l[1] + sm_l[2] + sm_l[3]
        send(sm_f.at[0], sm_f.at[1], SLOTS["s_far"], (z_far * 2 + core, lon, t))

    def small_end():
        got(sm_f.at[1], SLOTS["s_far"])
        total = sm_f[0] + sm_f[1]
        out_s[...] = jnp.zeros_like(out_s)
        out_s[0:2, 0:TABLE] = total[3:5]
        out_s[0:1, TABLE:SH] = total[5:6, 0:128]
        out_s[1:2, TABLE:SH] = total[5:6, 128:256]
        out_s[2:5, 0:TABLE] = total[0:3]

    def both(body):
        def step(g, carry):
            body(g)
            return carry

        lax.fori_loop(0, GROUPS, step, 0)

    def first(g):
        forward(g)

        @pl.when(g == 0)
        def _():
            halo_lat(cot, cbuf, SLOTS["halo_c"])

    both(first)
    own[11].wait()
    for o in range(15):
        y, x = plane_from(o)

        @pl.when(y < 3)
        def _():
            got(piece(y, x), SLOTS["wcol_p"] + o)

    for i in (7, 8, 9, 10):
        own[i].wait()
    got(halo_parts(cbuf)[0], SLOTS["halo_c"])

    def drain_inputs():
        for base, parts in (("halo_f", halo_parts(x_own)), ("halo_c", halo_parts(cbuf))):
            for i in range(5):
                sent(parts[i], SLOTS[base] + i)
        for w in range(NWIN):
            spread_drain("fields", 4, xbuf.at[0, 0], w)

        @pl.when(has_piece)
        def _():
            for d in range(3):
                sent(wcol.at[0, 0:48, 0:128], SLOTS["wcol_z"] + d)
            for o in range(15):
                sent(wcol.at[1:4, 0:48, 0:128], SLOTS["wcol_p"] + o)

    def drain_middle():
        for g in range(GROUPS):
            spread_drain("att", 2, abuf.at[0, 0], g)
            for i in range(3):
                sent(stat_all.at[0, 0], SLOTS["stat"] + 2 * i + g)
                sent(ga_send.at[0, 0], SLOTS["gatt"] + 2 * i + g)
        sent(wc_send, SLOTS["w_core"])

    def drain_late():
        for i in range(5):
            sent(back_parts(out_f)[i], SLOTS["out_f"] + i)
        for o in range(15):
            sent(sm_p.at[0], SLOTS["s_p"] + o)

            @pl.when(plane(o)[0] < 3)
            def _():
                sent(wp_send.at[:, 0:16], SLOTS["w_p"] + o)

    def middle(g):
        @pl.when(g == 1)
        def _():
            for i in range(1, 5):
                got(halo_parts(cbuf)[i], SLOTS["halo_c"] + i)

        @pl.when(g == 0)
        def _():
            spread_relay("att", 2, abuf, 0)

        mix(g)

        @pl.when(g == 0)
        def _():
            spread_relay("att", 2, abuf, 1)

        @pl.when(g == 1)
        def _():
            sum_relay("gatt", ga_send, ga_recv, ga_relay, 0)
            weight_first()

        normalise(g)

    both(middle)
    weight_start()
    sum_relay("gatt", ga_send, ga_recv, ga_relay, 1)

    def last(g):
        @pl.when(g == 1)
        def _():
            weight_plane()
            sum_relay("gsh", gs_send, gs_recv, gs_relay, 0)
            give_first(obuf, out_f, SLOTS["out_f"])
            give_second(obuf, out_f, SLOTS["out_f"])

        backward(g)

    both(last)
    weight_z()
    sum_relay("gsh", gs_send, gs_recv, gs_relay, 1)
    small_start()
    weight_far()
    drain_inputs()
    drain_middle()
    finish(0)
    give_first(gobuf, out_g, SLOTS["out_g"])
    small_lat()
    weight_back_plane()
    small_far()
    drain_late()
    finish(1)
    give_second(gobuf, out_g, SLOTS["out_g"])
    weight_back_core()
    small_end()

    for i in range(5):
        got(back_parts(out_f)[i], SLOTS["out_f"] + i)
        got(back_parts(out_g)[i], SLOTS["out_g"] + i)

    for i in range(5):
        sent(back_parts(out_g)[i], SLOTS["out_g"] + i)
    for g in range(GROUPS):
        for i in range(3):
            sent(gs_send.at[0, 0], SLOTS["gsh"] + 2 * i + g)

    @pl.when(has_piece)
    def _():
        sent(wp_sum, SLOTS["w_pair"])
        for j in (0, 1):
            sent(wp_both.at[j], SLOTS["w_zs"] + 2 * j)

            @pl.when(2 * core + j != t)
            def _():
                sent(wp_both.at[j], SLOTS["w_zs"] + 2 * j + 1)

    @pl.when(holder & has_piece)
    def _():
        for o in range(15):
            sent(out_w.at[0:16], SLOTS["back_p"] + o)
        sent(out_w.at[0:16], SLOTS["back_core"] + lx * 3 + ly)

    @pl.when(holder)
    def _():
        for o in range(15):
            y, x = plane_from(o)

            @pl.when(y < 3)
            def _():
                sent(out_w.at[0:16], SLOTS["back_core"] + x * 3 + y)

    for i in range(3):
        sent(sm_l.at[0], SLOTS["s_l"] + i)
    sent(sm_f.at[0], SLOTS["s_far"])

    @pl.when(jnp.logical_not(holder))
    def _():
        for x in range(4):
            for y in range(3):
                got(out_w.at[x * 48 + y * 16:x * 48 + y * 16 + 16], SLOTS["back_core"] + x * 3 + y)


def per_device(
    fields, w_qkv, w_out, log_scale, bias_table, bias_index, mask_ids, norm_gain, norm_shift, cotangent
):
    rows = bias_table.shape[0]
    wt = w_qkv.transpose(1, 2, 0).reshape(3 * AW, CH)
    hbm = pl.BlockSpec(memory_space=pltpu.HBM)
    vmem = pl.BlockSpec(memory_space=pltpu.VMEM)
    scratch = [
        ((16, 16, SH), BF), ((16, 16, SH), BF), ((576, CH), BF), ((4, 4, 16, SH), BF), ((4, 4, 16, SH), BF), ((4, 4, 2, 2, 16, SH), BF), ((4, 2, 2, 16, SH), BF), ((4, AW, SH), BF),
        ((4, 2, CELLS, SH), BF), ((TABLE, NPAIR), BF), ((8, NPAIR), F32), ((8, NPAIR), F32), ((8, TABLE), F32),
        ((HEADS, 2 * CELLS, 2 * CELLS), F32), ((NWIN * CELLS, 1), F32),
        ((2, HEADS, 2 * CELLS, HD), BF), ((2, HEADS, 2 * CELLS, HD), BF), ((2, HEADS, 2 * CELLS, HD), BF),
        ((2, HEADS, 2 * CELLS, 2 * CELLS), BF), ((2, HEADS, 2 * CELLS, 2 * CELLS), F32),
        ((2, HEADS, 2 * CELLS, 1), F32), ((2, HEADS, 2 * CELLS, 1), F32),
        ((2, 2 * CELLS, SH), F32), ((4, 2, 8, 128), F32), ((2, 2 * CELLS, SH), BF),
        ((4, 2, CELLS, SH), BF), ((4, 2, CELLS, SH), BF), ((2, CELLS, SH), BF),
        ((4, 2, 2 * CELLS, SH), BF), ((4, 2, 2 * CELLS, SH), BF), ((2, 2 * CELLS, SH), BF),
        ((4, 2, 2, 16, SH), BF), ((4, 2, 2, 16, SH), BF),
        ((HEADS, 2 * CELLS, 2 * CELLS), F32), ((HEADS, 2 * CELLS, 2 * CELLS), F32), ((8, SH), F32), ((8, NPAIR), F32),
        ((2, AW, SH), BF), ((2, AW, SH), BF), ((4, AW, SH), F32),
        ((2, AW, SH), BF), ((15, 2, 16, SH), BF), ((2, 16, SH), BF), ((2, 16, SH), BF), ((2, 16, SH), BF),
        ((2, 4, 16, SH), BF), ((16, 8, TABLE), F32), ((4, 8, TABLE), F32), ((2, 8, TABLE), F32),
    ]
    out_f, out_g, out_w, out_s = pl.pallas_call(
        whole_kernel,
        out_shape=(
            jax.ShapeDtypeStruct((4, 4, 16, SH), BF),
            jax.ShapeDtypeStruct((4, 4, 16, SH), BF),
            jax.ShapeDtypeStruct((AW, CH), BF),
            jax.ShapeDtypeStruct((8, SH), F32),
        ),
        in_specs=[hbm, hbm, hbm, hbm, vmem, vmem, vmem, vmem, vmem, vmem],
        out_specs=(vmem, vmem, vmem, vmem),
        scratch_shapes=[pltpu.VMEM(shape, kind) for shape, kind in scratch] + [
            pltpu.SemaphoreType.DMA((12,)),
            pltpu.SemaphoreType.DMA((COUNT,)),
            pltpu.SemaphoreType.DMA((COUNT,)),
        ],
        compiler_params=pltpu.CompilerParams(
            collective_id=0, has_side_effects=True, vmem_limit_bytes=60 * 1024 * 1024
        ),
        cost_estimate=pl.CostEstimate(flops=2_000_000_000, bytes_accessed=5_000_000, transcendentals=200_000),
    )(
        fields, cotangent, wt, w_out, log_scale.reshape(1, HEADS), bias_table.T, bias_index, mask_ids,
        norm_gain, norm_shift,
    )
    shapes = (
        (fields.shape, BF), (fields.shape, BF), ((AW, CH), BF), ((HEADS, rows), F32), ((HEADS,), F32),
        ((SH,), F32), ((SH,), F32),
    )
    block_out, grad_fields, grad_w_out, grad_table, grad_scale, grad_gain, grad_shift = pl.pallas_call(
        write_kernel,
        out_shape=tuple(jax.ShapeDtypeStruct(shape, kind) for shape, kind in shapes),
        in_specs=[vmem] * 4,
        out_specs=(vmem,) * 7,
        compiler_params=pltpu.CompilerParams(vmem_limit_bytes=60 * 1024 * 1024),
        cost_estimate=pl.CostEstimate(flops=1_000_000, bytes_accessed=2_000_000, transcendentals=0),
    )(out_f, out_g, out_w, out_s)
    return (block_out, grad_fields, grad_w_out, grad_table.T, grad_scale, grad_gain, grad_shift)


def solution(mesh):
    in_specs = (
        P("lat", "lon", "tp"), P(None, None, "tp"), P("tp", None), P("tp"), P(None, "tp"), P(),
        P("lat", "lon"), P("tp"), P("tp"), P("lat", "lon", "tp"),
    )
    out_specs = (
        P("lat", "lon", "tp"), P("lat", "lon", "tp"), P("tp", None), P(None, "tp"), P("tp"), P("tp"), P("tp"),
    )
    return jax.shard_map(per_device, mesh=mesh, in_specs=in_specs, out_specs=out_specs, check_vma=False)
```

```python
import jax
import jax.numpy as jnp
from jax import lax
from jax.experimental import pallas as pl
from jax.experimental.pallas import tpu as pltpu
from jax.sharding import PartitionSpec as P

MESH = pl.DeviceIdType.MESH
BF = jnp.bfloat16
F32 = jnp.float32

CH = 1536
SH = 384
HEADS = 3
HD = 64
AW = HEADS * HD
CELLS = 64
NWIN = 4
GROUPS = 2
WIN = 8
TABLE = 256
NPAIR = 4096

SLOTS = {}
COUNT = 0
for _name, _n in (
    ("halo_f", 5), ("halo_c", 5), ("fields", 16), ("wcol_z", 3), ("wcol_p", 15), ("att", 8), ("stat", 6),
    ("gatt", 8), ("gsh", 8), ("out_f", 5), ("out_g", 5), ("w_core", 1), ("w_p", 15), ("w_pair", 1), ("w_z", 8),
    ("w_zs", 4), ("back_p", 15), ("back_core", 12), ("s_p", 15), ("s_l", 3), ("s_far", 1),
):
    SLOTS[_name] = COUNT
    COUNT += _n

PLANE = [(dy, dx) for dy in range(4) for dx in range(4)][1:]


def nn(a, b):
    return lax.dot_general(a, b, (((1,), (0,)), ((), ())), preferred_element_type=F32)


def nt(a, b):
    return lax.dot_general(a, b, (((1,), (1,)), ((), ())), preferred_element_type=F32)


def tn(a, b):
    return lax.dot_general(a, b, (((0,), (0,)), ((), ())), preferred_element_type=F32)


def split3(value):
    high = value.astype(BF).astype(F32)
    middle = (value - high).astype(BF).astype(F32)
    return high, middle, value - high - middle


def swap_halves(first, second):
    low = lax.broadcasted_iota(jnp.int32, first.shape, 0) < 4
    return jnp.where(low, first, pltpu.roll(second, 4, 0)), jnp.where(low, pltpu.roll(first, 4, 0), second)


def cut_blocks(grid, blocks):
    for i in range(4):
        tiles = [[None, None] for _ in range(4)]
        for half in (0, 1):
            upper = grid[4 * i + 2 * half].astype(F32)
            lower = grid[4 * i + 2 * half + 1].astype(F32)
            for k in (0, 1):
                pair = swap_halves(upper[8 * k:8 * k + 8], lower[8 * k:8 * k + 8])
                tiles[2 * k][half], tiles[2 * k + 1][half] = pair
        for j in range(4):
            blocks[i, j] = jnp.concatenate(tiles[j], axis=0).astype(BF)


def join_blocks(blocks, grid):
    for i in range(4):
        for half in (0, 1):
            upper, lower = [], []
            for k in (0, 1):
                rows = slice(8 * half, 8 * half + 8)
                pair = swap_halves(blocks[i, 2 * k].astype(F32)[rows], blocks[i, 2 * k + 1].astype(F32)[rows])
                upper.append(pair[0])
                lower.append(pair[1])
            grid[4 * i + 2 * half] = jnp.concatenate(upper, axis=0).astype(BF)
            grid[4 * i + 2 * half + 1] = jnp.concatenate(lower, axis=0).astype(BF)


def write_kernel(blocks_f, blocks_g, weights, small, out_f, out_g, out_w, out_t, out_s, out_a, out_b):
    out_w[...] = weights[...]
    join_blocks(blocks_f, out_f)
    join_blocks(blocks_g, out_g)
    out_t[...] = small[2:2 + HEADS, 0:out_t.shape[1]]
    spare = small[2:2 + HEADS, TABLE - 1:TABLE]
    scales = jnp.transpose(jnp.concatenate([jnp.broadcast_to(spare, (HEADS, 128)), jnp.zeros((8 - HEADS, 128), F32)], axis=0))
    out_s[...] = scales[0:1, 0:HEADS].reshape(HEADS)
    out_a[...] = small[0]
    out_b[...] = small[1]


def whole_kernel(
    fields_hbm, cot_hbm, wt_hbm, wout, logs, table, index, mask, gain_ref, shift_ref,
    out_f, out_g, out_w, out_s,
    fields_grid, cot_grid, wt, fields, cot, xbuf, cbuf, wcol, abuf, onehot, bsrow, idx_row, tab_pad, bsig, lab_col, qs, ks, vs, probs, coss, rqs, rks,
    mixed, stat_all, gmix, ga_send, ga_recv, ga_relay, gs_send, gs_recv, gs_relay, obuf, gobuf, tacc, sacc, gacc, flat,
    wc_send, wc_recv, wacc, wp_send, wp_recv, wp_sum, wp_pair, wp_both, bz, sm_p, sm_l, sm_f, local_sem, ssem, rsem,
):
    lat = lax.axis_index("lat")
    lon = lax.axis_index("lon")
    t = lax.axis_index("tp")
    zh = lat // 2
    core = lat % 2
    ly = lon // 4
    lx = lon % 4

    def ring(value, by, count):
        return lax.rem(value + by + count, count)

    lat_p, lat_n = ring(lat, -1, 8), ring(lat, 1, 8)
    lon_p, lon_n = ring(lon, -1, 16), ring(lon, 1, 16)
    sib = (zh * 2 + (1 - core), lon, t)

    def tp_dev(d):
        return (lat, lon, ring(t, d, 4))

    def plane(o):
        return ring(ly, PLANE[o][0], 4), ring(lx, PLANE[o][1], 4)

    def plane_from(o):
        return ring(ly, -PLANE[o][0], 4), ring(lx, -PLANE[o][1], 4)

    def plane_dev(o):
        y, x = plane(o)
        return (lat, y * 4 + x, t)

    def z_dev(d):
        return (ring(zh, d, 4) * 2 + core, lon, t)

    def copy(src, dst, slot, dev, send_slot=None):
        return pltpu.make_async_remote_copy(
            src_ref=src, dst_ref=dst, send_sem=ssem.at[slot if send_slot is None else send_slot],
            recv_sem=rsem.at[slot], device_id=dev, device_id_type=MESH,
        )

    def send(src, dst, slot, dev, send_slot=None):
        copy(src, dst, slot, dev, send_slot).start()

    def got(dst, slot):
        copy(dst, dst, slot, sib).wait_recv()

    def sent(src, slot):
        copy(src, src, slot, sib).wait_send()

    own = []

    def keep(src, dst):
        own.append(pltpu.make_async_copy(src, dst, local_sem.at[len(own)]))
        own[-1].start()

    keep(fields_hbm, fields_grid)
    keep(cot_hbm, cot_grid)
    keep(wt_hbm, wt)

    z_pair = zh + 1 - 2 * (zh % 2)
    z_far = 3 - zh
    pair_devs = [sib, (z_pair * 2 + core, lon, t), (z_pair * 2 + (1 - core), lon, t)]

    partners = [plane_dev(o) for o in range(15)] + pair_devs
    partners += [(lat_p, lon, t), (lat_n, lon, t), (lat_p, lon_p, t), (lat_n, lon_n, t)]
    partners += [tp_dev(d) for d in (1, 2, 3)] + [(z_far * 2 + core, lon, ring(t, d, 4)) for d in range(4)]
    barrier = pltpu.get_barrier_semaphore()
    for dev in partners:
        pl.semaphore_signal(barrier, inc=1, device_id=dev, device_id_type=MESH)

    def keep_grid(grid, dst):
        keep(grid.at[1:3, 1:3], dst.at[0])
        keep(grid.at[1:3, 3], dst.at[1, :, 0])
        keep(grid.at[3, 1:3], dst.at[2, 0])
        keep(grid.at[3, 3], dst.at[3, 0, 0])

    x_own = xbuf.at[t]
    own[0].wait()
    cut_blocks(fields_grid, fields)
    keep_grid(fields, x_own)

    pl.semaphore_wait(barrier, len(partners))

    def halo_lon(grid, dst, base):
        send(grid.at[1:3, 0], dst.at[1, :, 1], base, (lat, lon_p, t))
        send(grid.at[3, 0], dst.at[3, 0, 1], base + 2, (lat, lon_p, t))

    def halo_lat(grid, dst, base):
        send(grid.at[0, 1:3], dst.at[2, 1], base + 1, (lat_p, lon, t))
        send(grid.at[0, 3], dst.at[3, 1, 0], base + 3, (lat_p, lon, t))
        send(grid.at[0, 0], dst.at[3, 1, 1], base + 4, (lat_p, lon_p, t))

    def halo_parts(dst):
        return [dst.at[1, :, 1], dst.at[2, 1], dst.at[3, 0, 1], dst.at[3, 1, 0], dst.at[3, 1, 1]]

    side = t // 2
    is_mid = (t == 1) | (t == 2)
    is_edge = jnp.logical_not(is_mid)
    partner = 2 * side + 1 - t % 2
    far_mid = 2 - side
    far_edge = 3 - 3 * side
    far_slot = jnp.where(is_mid, 1, 2)

    def on_line(where):
        return (lat, lon, where)

    def spread_start(name, n, src, dst, i):
        base = SLOTS[name] + i
        send(src, dst, base + n * far_slot, on_line(far_mid), base + n)

        @pl.when(is_mid)
        def _():
            send(src, dst, base + n, on_line(far_edge), base + 2 * n)

        send(src, dst, base, on_line(partner), base)

    def spread_relay(name, n, buf, i):
        base = SLOTS[name] + i

        @pl.when(is_mid)
        def _():
            chunk = buf.at[far_edge, i]
            got(chunk, base + 2 * n)
            send(chunk, chunk, base + 2 * n, on_line(partner), base + 3 * n)

    due = (t, partner, far_mid, far_edge)

    def spread_wait(name, n, buf, i, step):
        base = SLOTS[name] + i
        if step == 1:
            got(buf.at[partner, i], base)
        if step == 2:
            got(buf.at[far_mid, i], base + n)
        if step == 3:
            @pl.when(is_edge)
            def _():
                got(buf.at[far_edge, i], base + 2 * n)

    def spread_drain(name, n, chunk, i):
        base = SLOTS[name] + i
        sent(chunk, base)
        sent(chunk, base + n)

        @pl.when(is_mid)
        def _():
            sent(chunk, base + 2 * n)
            sent(chunk, base + 3 * n)

    def sum_start(name, part, recv, relay, g, term):
        base = SLOTS[name] + g
        part[far_edge, g] = term(far_edge)

        @pl.when(is_edge)
        def _():
            send(part.at[far_edge, g], relay.at[g], base + 6, on_line(partner), base + 4)

        part[far_mid, g] = term(far_mid)
        send(part.at[far_mid, g], recv.at[t, g], base + 2 * far_slot, on_line(far_mid), base + 2)
        part[partner, g] = term(partner)
        send(part.at[partner, g], recv.at[t, g], base, on_line(partner), base)
        part[t, g] = term(t)

    def sum_relay(name, part, recv, relay, g):
        base = SLOTS[name] + g

        @pl.when(is_mid)
        def _():
            got(relay.at[g], base + 6)
            part[far_edge, g] = (part[far_edge, g].astype(F32) + relay[g].astype(F32)).astype(BF)
            send(part.at[far_edge, g], recv.at[t, g], base + 2, on_line(far_edge), base + 4)

    def sum_end(name, part, recv, g):
        base = SLOTS[name] + g
        got(recv.at[partner, g], base)
        got(recv.at[far_mid, g], base + 2)

        @pl.when(is_mid)
        def _():
            got(recv.at[far_edge, g], base + 4)

        @pl.when(is_edge)
        def _():
            recv[far_edge, g] = jnp.zeros(recv.shape[2:], BF)

        total = part[t, g].astype(F32)
        for src in (partner, far_mid, far_edge):
            total = total + recv[src, g].astype(F32)
        return total

    def give_fields(w, src):
        spread_start("fields", 4, src, x_own.at[w], w)

    halo_lat(fields, x_own, SLOTS["halo_f"])
    halo_lon(fields, x_own, SLOTS["halo_f"])

    piece_rows = pl.ds(pl.multiple_of(lx * 48, 16), 48)
    has_piece = ly < 3

    def piece(y, x):
        rows = pl.ds(pl.multiple_of(x * 48, 16), 48)
        return wcol.at[1:4, rows, pl.ds(pl.multiple_of(y * 128, 128), 128)]

    @pl.when(has_piece)
    def _():
        for d in (1, 2, 3):
            cols = pl.ds(pl.multiple_of(ring(t, d, 4) * SH + ly * 128, 128), 128)
            here = pl.ds(pl.multiple_of(ly * 128, 128), 128)
            send(wout.at[piece_rows, cols], wcol.at[d, piece_rows, here], SLOTS["wcol_z"] + d - 1, tp_dev(d))

    give_fields(0, fields.at[1:3, 1:3])
    own[1].wait()
    cut_blocks(cot_grid, cot)
    keep_grid(cot, cbuf)
    keep(wout.at[:, pl.ds(pl.multiple_of(t * SH, 128), SH)], wcol.at[0])

    def place(n):
        a, b, c, d = (n >> 5) & 1, (n >> 4) & 1, (n >> 2) & 3, n & 3
        return 4 * a + c, 4 * b + d

    def iota(shape, dim):
        return lax.broadcasted_iota(jnp.int32, shape, dim)

    def hot(flag):
        return jnp.where(flag, 1.0, 0.0)

    row_of, col_of = place(iota((CELLS, CELLS), 0))
    order = hot(iota((CELLS, CELLS), 1) == row_of * WIN + col_of).astype(BF)
    swapped = nn(order, index[...].astype(F32).astype(BF)).astype(BF)
    idx = nt(swapped, order)
    for c in range(NPAIR // 128):
        idx_row[0:1, c * 128:(c + 1) * 128] = jnp.concatenate([idx[2 * c:2 * c + 1], idx[2 * c + 1:2 * c + 2]], axis=1)

    cell = iota((NWIN * CELLS, 16), 0)
    row_of, col_of = place(cell)
    row_of, col_of = row_of + WIN * (cell >> 7), col_of + WIN * ((cell >> 6) & 1)
    picked_rows = nn(hot(iota((NWIN * CELLS, 16), 1) == row_of).astype(BF), mask[...].astype(F32).astype(BF))
    labels = jnp.sum(hot(iota((NWIN * CELLS, 16), 1) == col_of) * picked_rows, axis=1, keepdims=True)
    lab_col[...] = labels + 4.0 * (iota((NWIN * CELLS, 1), 0) >> 6).astype(F32)

    own[4].wait()
    got(halo_parts(x_own)[0], SLOTS["halo_f"])
    give_fields(1, x_own.at[1])
    own[5].wait()
    got(halo_parts(x_own)[1], SLOTS["halo_f"] + 1)
    give_fields(2, x_own.at[2])
    own[6].wait()
    for part in (2, 3, 4):
        got(halo_parts(x_own)[part], SLOTS["halo_f"] + part)
    give_fields(3, x_own.at[3])

    @pl.when(has_piece)
    def _():
        for d in (1, 2, 3):
            here = pl.ds(pl.multiple_of(ly * 128, 128), 128)
            got(wcol.at[d, piece_rows, here], SLOTS["wcol_z"] + d - 1)
        for o in range(15):
            send(piece(ly, lx), piece(ly, lx), SLOTS["wcol_p"] + o, plane_dev(o))

    halo_lon(cot, cbuf, SLOTS["halo_c"])

    spread_relay("fields", 4, xbuf, 0)

    tab_pad[...] = jnp.zeros_like(tab_pad)
    tab_pad[0:HEADS, 0:table.shape[1]] = table[...]
    tab = jnp.concatenate([*split3(tab_pad[...]), jnp.zeros((8, TABLE), F32)], axis=0).astype(BF)
    entry = iota((TABLE, 512), 0).astype(F32)
    for c in range(NPAIR // 512):
        span = slice(c * 512, (c + 1) * 512)
        picked = hot(entry == idx_row[0:1, span]).astype(BF)
        onehot[:, span] = picked
        parts = nn(tab, picked)
        bias = parts[0:8] + parts[8:16] + parts[16:24]
        sig = 1.0 / (1.0 + jnp.exp(-bias))
        bsrow[:, span] = sig
        for k in range(8):
            for h in range(HEADS):
                at = 8 * c + k
                pair = jnp.concatenate([16.0 * sig[h:h + 1, k * CELLS:(k + 1) * CELLS]] * 2, axis=1)
                bsig[h, at:at + 1, :] = pair
                bsig[h, CELLS + at:CELLS + at + 1, :] = pair
    spread_relay("fields", 4, xbuf, 1)
    tacc[...] = jnp.zeros_like(tacc)
    sacc[...] = jnp.zeros_like(sacc)
    gacc[...] = jnp.zeros_like(gacc)
    scales = jnp.exp(logs[...])

    own[2].wait()
    own[3].wait()

    eye = iota((2 * CELLS, 2 * CELLS), 0) == iota((2 * CELLS, 2 * CELLS), 1)

    def forward(g):
        @pl.when(g == 1)
        def _():
            spread_relay("fields", 4, xbuf, 3)

        proj = jnp.zeros((2 * CELLS, 3 * AW), F32)
        for step, src in enumerate(due):
            for w in (2 * g, 2 * g + 1):
                spread_wait("fields", 4, xbuf, w, step)
            cols = pl.ds(pl.multiple_of(src * SH, 128), SH)
            proj = proj + nt(xbuf[src, pl.ds(2 * g, 2)].reshape(2 * CELLS, SH), wt[:, cols])

        @pl.when(g == 0)
        def _():
            spread_relay("fields", 4, xbuf, 2)

        column = lab_col[pl.ds(pl.multiple_of(2 * g * CELLS, 128), 128), :]
        row = jnp.sum(jnp.where(eye, column, 0.0), axis=0, keepdims=True)
        same = row == column
        heads = range(HEADS)

        def slot(kind, h):
            at = kind * AW + h * HD
            return proj[:, at:at + HD]

        q = [slot(0, h) for h in heads]
        k = [slot(1, h) for h in heads]
        v = [slot(2, h).astype(BF) for h in heads]
        rq = [lax.rsqrt(jnp.sum(q[h] * q[h], axis=1, keepdims=True) + 1e-06) for h in heads]
        rk = [lax.rsqrt(jnp.sum(k[h] * k[h], axis=1, keepdims=True) + 1e-06) for h in heads]
        q_hat = [(q[h] * rq[h]).astype(BF) for h in heads]
        k_hat = [(k[h] * rk[h]).astype(BF) for h in heads]
        cosine = [nt(q_hat[h], k_hat[h]) for h in heads]
        power = [scales[:, h:h + 1] * (cosine[h] - 1.0) + (bsig[h] - 16.0) for h in heads]
        weight = [jnp.where(same, jnp.exp(power[h]), 0.0) for h in heads]
        total = [jnp.sum(weight[h], axis=1, keepdims=True) for h in heads]
        prob = [(weight[h] * (1.0 / total[h])).astype(BF) for h in heads]
        attended = [nn(prob[h], v[h]).astype(BF) for h in heads]
        for i in (0, 1):
            for h in heads:
                at = i * AW + h * HD
                abuf[t, g, :, at:at + HD] = attended[h][i * CELLS:(i + 1) * CELLS]
        for h in heads:
            qs[g, h] = q_hat[h]
            ks[g, h] = k_hat[h]
            vs[g, h] = v[h]
            probs[g, h] = prob[h]
            coss[g, h] = cosine[h]
            rqs[g, h] = rq[h]
            rks[g, h] = rk[h]
        spread_start("att", 2, abuf.at[t, g], abuf.at[t, g], g)

    gain = gain_ref[...].reshape(1, SH)
    shift = shift_ref[...].reshape(1, SH)
    lane = iota((2 * CELLS, 128), 1)

    def unpack(pair):
        return jnp.concatenate([pair[:, :AW], pair[:, AW:]], axis=0)

    def cells_of(buf, g):
        return buf[pl.ds(2 * g, 2)].reshape(2 * CELLS, SH).astype(F32)

    def mix(g):
        total = jnp.zeros((2 * CELLS, SH), F32)
        for step, src in enumerate(due):
            spread_wait("att", 2, abuf, g, step)
            total = total + nn(unpack(abuf[src, g]), wcol[ring(t - src, 0, 4)])
        mixed[g] = total
        grad_norm = cells_of(cbuf, g) * gain
        packed = jnp.zeros((2 * CELLS, 128), F32)
        for i, v in enumerate((total, total * total, grad_norm, grad_norm * total)):
            packed = jnp.where(lane == i, jnp.sum(v, axis=1, keepdims=True), packed)
        stat_all[t, g] = jnp.transpose(packed)[0:8]
        mine = stat_all.at[t, g]
        for d in (1, 2, 3):
            send(mine, mine, SLOTS["stat"] + (d - 1) * 2 + g, tp_dev(d))

    def normalise(g):
        for d in (1, 2, 3):
            got(stat_all.at[ring(t, -d, 4), g], SLOTS["stat"] + (d - 1) * 2 + g)
        totals = stat_all[0, g] + stat_all[1, g] + stat_all[2, g] + stat_all[3, g]
        packed = jnp.transpose(jnp.concatenate([totals, jnp.zeros((120, 128), F32)], axis=0))
        mean = packed[:, 0:1] / CH
        variance = packed[:, 1:2] / CH - mean * mean
        inv_std = 1.0 / jnp.sqrt(variance + 1e-05)
        grad_mean = packed[:, 2:3] / CH
        cross_mean = inv_std * (packed[:, 3:4] - mean * packed[:, 2:3]) / CH
        normed = (mixed[g] - mean) * inv_std
        rows = cells_of(cbuf, g)
        grad = (inv_std * (rows * gain - grad_mean - normed * cross_mean)).astype(BF)
        gmix[g] = grad
        def term(dst):
            part = nt(grad, wcol[ring(t - dst, 0, 4)])
            return jnp.concatenate([part[:CELLS], part[CELLS:]], axis=1).astype(BF)

        sum_start("gatt", ga_send, ga_recv, ga_relay, g, term)
        base = xbuf[t, pl.ds(2 * g, 2)].reshape(2 * CELLS, SH).astype(F32)
        obuf[pl.ds(2 * g, 2)] = (base + (gain * normed + shift)).astype(BF).reshape(2, 2, 2, 16, SH)
        gacc[0:1, :] += jnp.sum(rows * normed, axis=0, keepdims=True)
        gacc[1:2, :] += jnp.sum(rows, axis=0, keepdims=True)

    def backward(g):
        total = sum_end("gatt", ga_send, ga_recv, g)
        grad_att = unpack(total.astype(BF))
        heads = range(HEADS)
        ga = [grad_att[:, h * HD:(h + 1) * HD] for h in heads]
        prob = [probs[g, h] for h in heads]
        q_hat = [qs[g, h] for h in heads]
        k_hat = [ks[g, h] for h in heads]
        grad_prob = [nt(ga[h], vs[g, h]) for h in heads]
        grads_v = [tn(prob[h], ga[h]) for h in heads]
        prob_f = [prob[h].astype(F32) for h in heads]
        inner = [jnp.sum(prob_f[h] * grad_prob[h], axis=1, keepdims=True) for h in heads]
        grad_logit = [prob_f[h] * (grad_prob[h] - inner[h]) for h in heads]
        grad_cos = [(grad_logit[h] * scales[:, h:h + 1]).astype(BF) for h in heads]
        gq = [nn(grad_cos[h], k_hat[h]) for h in heads]
        gk = [tn(grad_cos[h], q_hat[h]) for h in heads]
        for h in heads:
            tacc[h] += grad_logit[h]
            sacc[h] += grad_logit[h] * coss[g, h]
        q_float = [q_hat[h].astype(F32) for h in heads]
        k_float = [k_hat[h].astype(F32) for h in heads]
        q_in = [jnp.sum(q_float[h] * gq[h], axis=1, keepdims=True) for h in heads]
        k_in = [jnp.sum(k_float[h] * gk[h], axis=1, keepdims=True) for h in heads]
        grads_q = [(gq[h] - q_float[h] * q_in[h]) * rqs[g, h] for h in heads]
        grads_k = [(gk[h] - k_float[h] * k_in[h]) * rks[g, h] for h in heads]
        stacked = jnp.concatenate(grads_q + grads_k + grads_v, axis=1).astype(BF)
        def term(dst):
            return nn(stacked, wt[:, pl.ds(pl.multiple_of(dst * SH, 128), SH)]).astype(BF)

        sum_start("gsh", gs_send, gs_recv, gs_relay, g, term)

    def finish(g):
        total = sum_end("gsh", gs_send, gs_recv, g) + cells_of(cbuf, g)
        gobuf[pl.ds(2 * g, 2)] = total.astype(BF).reshape(2, 2, 2, 16, SH)

    def give_first(buf, out, base):
        out[1:3, 1:3] = buf[0]
        out[1:3, 3] = buf[1, :, 0]
        send(buf.at[1, :, 1], out.at[1:3, 0], base, (lat, lon_n, t))

    def give_second(buf, out, base):
        send(buf.at[2, 1], out.at[0, 1:3], base + 1, (lat_n, lon, t))
        send(buf.at[3, 0, 1], out.at[3, 0], base + 2, (lat, lon_n, t))
        send(buf.at[3, 1, 0], out.at[0, 3], base + 3, (lat_n, lon, t))
        send(buf.at[3, 1, 1], out.at[0, 0], base + 4, (lat_n, lon_n, t))
        out[3, 1:3] = buf[2, 0]
        out[3, 3] = buf[3, 0, 0]

    def back_parts(out):
        return [out.at[1:3, 0], out.at[0, 1:3], out.at[3, 0], out.at[0, 3], out.at[0, 0]]

    def weight_first():
        for group in range(4):
            wacc[group] = tn(unpack(abuf[group, 0]), gmix[0])

    def weight_start():
        for j in (0, 1):
            far = 2 * (1 - core) + j
            wc_send[j] = (wacc[far] + tn(unpack(abuf[far, 1]), gmix[1])).astype(BF)
        send(wc_send, wc_recv, SLOTS["w_core"], sib)
        for j in (0, 1):
            near = 2 * core + j
            wacc[near] = wacc[near] + tn(unpack(abuf[near, 1]), gmix[1])

    def rows_of(y, x):
        return pl.ds(pl.multiple_of(x * 48 + y * 16, 16), 16)

    def weight_plane():
        got(wc_recv, SLOTS["w_core"])
        for j in (0, 1):
            total = wacc[2 * core + j] + wc_recv[j].astype(F32)
            wacc[2 * core + j] = total
            wp_send[j] = total.astype(BF)
        for o in range(15):
            y, x = plane(o)

            @pl.when(y < 3)
            def _():
                send(wp_send.at[:, rows_of(y, x)], wp_recv.at[o], SLOTS["w_p"] + o, plane_dev(o))

    holder = t // 2 == core

    def weight_z():
        @pl.when(has_piece)
        def _():
            for o in range(15):
                got(wp_recv.at[o], SLOTS["w_p"] + o)
            for j in (0, 1):
                total = wacc[2 * core + j, rows_of(ly, lx), :]
                for o in range(15):
                    total = total + wp_recv[o, j].astype(F32)
                wp_sum[j] = total.astype(BF)
            send(wp_sum, wp_pair, SLOTS["w_pair"], (z_pair * 2 + core, lon, t))

    def weight_far():
        @pl.when(has_piece)
        def _():
            got(wp_pair, SLOTS["w_pair"])
            wp_both[...] = (wp_sum[...].astype(F32) + wp_pair[...].astype(F32)).astype(BF)
            for j in (0, 1):
                keeper = 2 * core + j
                slot = SLOTS["w_z"] + (zh // 2) * 4 + t
                send(wp_both.at[j], bz.at[zh // 2, t], slot, (z_far * 2 + core, lon, keeper), SLOTS["w_zs"] + 2 * j)

                @pl.when(keeper != t)
                def _():
                    send(wp_both.at[j], bz.at[zh // 2, t], slot, (lat, lon, keeper), SLOTS["w_zs"] + 2 * j + 1)

    def weight_back_plane():
        @pl.when(holder & has_piece)
        def _():
            bz[zh // 2, t] = wp_both[t % 2]
            for z in range(2):
                for src in range(4):
                    @pl.when((zh // 2 != z) | (t != src))
                    def _():
                        got(bz.at[z, src], SLOTS["w_z"] + z * 4 + src)

            for src in range(4):
                total = bz[0, src].astype(F32) + bz[1, src].astype(F32)
                out_w[rows_of(ly, lx), src * SH:(src + 1) * SH] = total.astype(BF)
            mine = out_w.at[rows_of(ly, lx)]
            for o in range(15):
                send(mine, mine, SLOTS["back_p"] + o, plane_dev(o))
            send(mine, mine, SLOTS["back_core"] + lx * 3 + ly, sib)

    def weight_back_core():
        @pl.when(holder)
        def _():
            for o in range(15):
                y, x = plane_from(o)

                @pl.when(y < 3)
                def _():
                    mine = out_w.at[rows_of(y, x)]
                    got(mine, SLOTS["back_p"] + o)
                    send(mine, mine, SLOTS["back_core"] + x * 3 + y, sib)

    def small_start():
        folded_t = [tacc[h, :CELLS, :CELLS] + tacc[h, CELLS:, CELLS:] for h in range(HEADS)]
        for c in range(NPAIR // 128):
            for h in range(HEADS):
                pair = [folded_t[h][2 * c + i:2 * c + i + 1, :] for i in (0, 1)]
                flat[h:h + 1, c * 128:(c + 1) * 128] = jnp.concatenate(pair, axis=1)
        spread = bsrow[0:HEADS, :]
        terms = flat[0:HEADS, :] * 16.0 * spread * (1.0 - spread)
        pad = jnp.zeros((8 - HEADS, NPAIR), F32)
        pieces = jnp.concatenate([v for p in split3(terms) for v in (p, pad)], axis=0).astype(BF)
        folded = nt(pieces, onehot[...])
        sm_p[lon] = folded[0:8] + folded[8:16] + folded[16:24]
        for h in range(HEADS):
            amount = jnp.sum(jnp.sum(sacc[h], axis=1, keepdims=True), axis=0, keepdims=True) * scales[:, h:h + 1]
            sm_p[lon, h:h + 1, TABLE - 1:TABLE] = amount
        sm_p[lon, 3:5, :] = gacc[0:2, 0:TABLE]
        sm_p[lon, 5:6, :] = jnp.concatenate([gacc[0:1, TABLE:SH], gacc[1:2, TABLE:SH]], axis=1)
        for o in range(15):
            send(sm_p.at[lon], sm_p.at[lon], SLOTS["s_p"] + o, plane_dev(o))

    def small_lat():
        for o in range(15):
            y, x = plane_from(o)
            got(sm_p.at[y * 4 + x], SLOTS["s_p"] + o)
        total = sm_p[0]
        for i in range(1, 16):
            total = total + sm_p[i]
        sm_l[2 * (zh % 2) + core] = total
        mine = sm_l.at[2 * (zh % 2) + core]
        for i, dev in enumerate(pair_devs):
            send(mine, mine, SLOTS["s_l"] + i, dev)

    def small_far():
        for i, where in enumerate((2 * (zh % 2) + 1 - core, 2 * (1 - zh % 2) + core, 2 * (1 - zh % 2) + 1 - core)):
            got(sm_l.at[where], SLOTS["s_l"] + i)
        sm_f[0] = sm_l[0] + sm_l[1] + sm_l[2] + sm_l[3]
        send(sm_f.at[0], sm_f.at[1], SLOTS["s_far"], (z_far * 2 + core, lon, t))

    def small_end():
        got(sm_f.at[1], SLOTS["s_far"])
        total = sm_f[0] + sm_f[1]
        out_s[...] = jnp.zeros_like(out_s)
        out_s[0:2, 0:TABLE] = total[3:5]
        out_s[0:1, TABLE:SH] = total[5:6, 0:128]
        out_s[1:2, TABLE:SH] = total[5:6, 128:256]
        out_s[2:5, 0:TABLE] = total[0:3]

    def both(body):
        def step(g, carry):
            body(g)
            return carry

        lax.fori_loop(0, GROUPS, step, 0)

    def first(g):
        forward(g)

        @pl.when(g == 0)
        def _():
            halo_lat(cot, cbuf, SLOTS["halo_c"])

    both(first)
    own[11].wait()
    for o in range(15):
        y, x = plane_from(o)

        @pl.when(y < 3)
        def _():
            got(piece(y, x), SLOTS["wcol_p"] + o)

    for i in (7, 8, 9, 10):
        own[i].wait()
    got(halo_parts(cbuf)[0], SLOTS["halo_c"])

    def drain_inputs():
        for base, parts in (("halo_f", halo_parts(x_own)), ("halo_c", halo_parts(cbuf))):
            for i in range(5):
                sent(parts[i], SLOTS[base] + i)
        for w in range(NWIN):
            spread_drain("fields", 4, xbuf.at[0, 0], w)

        @pl.when(has_piece)
        def _():
            for d in range(3):
                sent(wcol.at[0, 0:48, 0:128], SLOTS["wcol_z"] + d)
            for o in range(15):
                sent(wcol.at[1:4, 0:48, 0:128], SLOTS["wcol_p"] + o)

    def drain_middle():
        for g in range(GROUPS):
            spread_drain("att", 2, abuf.at[0, 0], g)
            for i in range(3):
                sent(stat_all.at[0, 0], SLOTS["stat"] + 2 * i + g)
                sent(ga_send.at[0, 0], SLOTS["gatt"] + 2 * i + g)
        sent(wc_send, SLOTS["w_core"])

    def drain_late():
        for i in range(5):
            sent(back_parts(out_f)[i], SLOTS["out_f"] + i)
        for o in range(15):
            sent(sm_p.at[0], SLOTS["s_p"] + o)

            @pl.when(plane(o)[0] < 3)
            def _():
                sent(wp_send.at[:, 0:16], SLOTS["w_p"] + o)

    def middle(g):
        @pl.when(g == 1)
        def _():
            for i in range(1, 5):
                got(halo_parts(cbuf)[i], SLOTS["halo_c"] + i)

        @pl.when(g == 0)
        def _():
            spread_relay("att", 2, abuf, 0)

        mix(g)

        @pl.when(g == 0)
        def _():
            spread_relay("att", 2, abuf, 1)

        @pl.when(g == 1)
        def _():
            sum_relay("gatt", ga_send, ga_recv, ga_relay, 0)
            weight_first()

        normalise(g)

    both(middle)
    weight_start()
    sum_relay("gatt", ga_send, ga_recv, ga_relay, 1)

    def last(g):
        @pl.when(g == 1)
        def _():
            weight_plane()
            sum_relay("gsh", gs_send, gs_recv, gs_relay, 0)
            give_first(obuf, out_f, SLOTS["out_f"])
            give_second(obuf, out_f, SLOTS["out_f"])

        backward(g)

    both(last)
    weight_z()
    sum_relay("gsh", gs_send, gs_recv, gs_relay, 1)
    small_start()
    weight_far()
    drain_inputs()
    drain_middle()
    finish(0)
    give_first(gobuf, out_g, SLOTS["out_g"])
    small_lat()
    weight_back_plane()
    small_far()
    drain_late()
    finish(1)
    give_second(gobuf, out_g, SLOTS["out_g"])
    weight_back_core()
    small_end()

    for i in range(5):
        got(back_parts(out_f)[i], SLOTS["out_f"] + i)
        got(back_parts(out_g)[i], SLOTS["out_g"] + i)

    for i in range(5):
        sent(back_parts(out_g)[i], SLOTS["out_g"] + i)
    for g in range(GROUPS):
        for i in range(3):
            sent(gs_send.at[0, 0], SLOTS["gsh"] + 2 * i + g)

    @pl.when(has_piece)
    def _():
        sent(wp_sum, SLOTS["w_pair"])
        for j in (0, 1):
            sent(wp_both.at[j], SLOTS["w_zs"] + 2 * j)

            @pl.when(2 * core + j != t)
            def _():
                sent(wp_both.at[j], SLOTS["w_zs"] + 2 * j + 1)

    @pl.when(holder & has_piece)
    def _():
        for o in range(15):
            sent(out_w.at[0:16], SLOTS["back_p"] + o)
        sent(out_w.at[0:16], SLOTS["back_core"] + lx * 3 + ly)

    @pl.when(holder)
    def _():
        for o in range(15):
            y, x = plane_from(o)

            @pl.when(y < 3)
            def _():
                sent(out_w.at[0:16], SLOTS["back_core"] + x * 3 + y)

    for i in range(3):
        sent(sm_l.at[0], SLOTS["s_l"] + i)
    sent(sm_f.at[0], SLOTS["s_far"])

    @pl.when(jnp.logical_not(holder))
    def _():
        for x in range(4):
            for y in range(3):
                got(out_w.at[x * 48 + y * 16:x * 48 + y * 16 + 16], SLOTS["back_core"] + x * 3 + y)


def per_device(
    fields, w_qkv, w_out, log_scale, bias_table, bias_index, mask_ids, norm_gain, norm_shift, cotangent
):
    rows = bias_table.shape[0]
    wt = w_qkv.transpose(1, 2, 0).reshape(3 * AW, CH)
    hbm = pl.BlockSpec(memory_space=pltpu.HBM)
    vmem = pl.BlockSpec(memory_space=pltpu.VMEM)
    scratch = [
        ((16, 16, SH), BF), ((16, 16, SH), BF), ((576, CH), BF), ((4, 4, 16, SH), BF), ((4, 4, 16, SH), BF), ((4, 4, 2, 2, 16, SH), BF), ((4, 2, 2, 16, SH), BF), ((4, AW, SH), BF),
        ((4, 2, CELLS, SH), BF), ((TABLE, NPAIR), BF), ((8, NPAIR), F32), ((8, NPAIR), F32), ((8, TABLE), F32),
        ((HEADS, 2 * CELLS, 2 * CELLS), F32), ((NWIN * CELLS, 1), F32),
        ((2, HEADS, 2 * CELLS, HD), BF), ((2, HEADS, 2 * CELLS, HD), BF), ((2, HEADS, 2 * CELLS, HD), BF),
        ((2, HEADS, 2 * CELLS, 2 * CELLS), BF), ((2, HEADS, 2 * CELLS, 2 * CELLS), F32),
        ((2, HEADS, 2 * CELLS, 1), F32), ((2, HEADS, 2 * CELLS, 1), F32),
        ((2, 2 * CELLS, SH), F32), ((4, 2, 8, 128), F32), ((2, 2 * CELLS, SH), BF),
        ((4, 2, CELLS, SH), BF), ((4, 2, CELLS, SH), BF), ((2, CELLS, SH), BF),
        ((4, 2, 2 * CELLS, SH), BF), ((4, 2, 2 * CELLS, SH), BF), ((2, 2 * CELLS, SH), BF),
        ((4, 2, 2, 16, SH), BF), ((4, 2, 2, 16, SH), BF),
        ((HEADS, 2 * CELLS, 2 * CELLS), F32), ((HEADS, 2 * CELLS, 2 * CELLS), F32), ((8, SH), F32), ((8, NPAIR), F32),
        ((2, AW, SH), BF), ((2, AW, SH), BF), ((4, AW, SH), F32),
        ((2, AW, SH), BF), ((15, 2, 16, SH), BF), ((2, 16, SH), BF), ((2, 16, SH), BF), ((2, 16, SH), BF),
        ((2, 4, 16, SH), BF), ((16, 8, TABLE), F32), ((4, 8, TABLE), F32), ((2, 8, TABLE), F32),
    ]
    out_f, out_g, out_w, out_s = pl.pallas_call(
        whole_kernel,
        out_shape=(
            jax.ShapeDtypeStruct((4, 4, 16, SH), BF),
            jax.ShapeDtypeStruct((4, 4, 16, SH), BF),
            jax.ShapeDtypeStruct((AW, CH), BF),
            jax.ShapeDtypeStruct((8, SH), F32),
        ),
        in_specs=[hbm, hbm, hbm, hbm, vmem, vmem, vmem, vmem, vmem, vmem],
        out_specs=(vmem, vmem, vmem, vmem),
        scratch_shapes=[pltpu.VMEM(shape, kind) for shape, kind in scratch] + [
            pltpu.SemaphoreType.DMA((12,)),
            pltpu.SemaphoreType.DMA((COUNT,)),
            pltpu.SemaphoreType.DMA((COUNT,)),
        ],
        compiler_params=pltpu.CompilerParams(
            collective_id=0, has_side_effects=True, vmem_limit_bytes=60 * 1024 * 1024
        ),
        cost_estimate=pl.CostEstimate(flops=2_000_000_000, bytes_accessed=5_000_000, transcendentals=200_000),
    )(
        fields, cotangent, wt, w_out, log_scale.reshape(1, HEADS), bias_table.T, bias_index, mask_ids,
        norm_gain, norm_shift,
    )
    shapes = (
        (fields.shape, BF), (fields.shape, BF), ((AW, CH), BF), ((HEADS, rows), F32), ((HEADS,), F32),
        ((SH,), F32), ((SH,), F32),
    )
    block_out, grad_fields, grad_w_out, grad_table, grad_scale, grad_gain, grad_shift = pl.pallas_call(
        write_kernel,
        out_shape=tuple(jax.ShapeDtypeStruct(shape, kind) for shape, kind in shapes),
        in_specs=[vmem] * 4,
        out_specs=(vmem,) * 7,
        compiler_params=pltpu.CompilerParams(vmem_limit_bytes=60 * 1024 * 1024),
        cost_estimate=pl.CostEstimate(flops=1_000_000, bytes_accessed=2_000_000, transcendentals=0),
    )(out_f, out_g, out_w, out_s)
    return (block_out, grad_fields, grad_w_out, grad_table.T, grad_scale, grad_gain, grad_shift)


def solution(mesh):
    in_specs = (
        P("lat", "lon", "tp"), P(None, None, "tp"), P("tp", None), P("tp"), P(None, "tp"), P(),
        P("lat", "lon"), P("tp"), P("tp"), P("lat", "lon", "tp"),
    )
    out_specs = (
        P("lat", "lon", "tp"), P("lat", "lon", "tp"), P("tp", None), P(None, "tp"), P("tp"), P("tp"), P("tp"),
    )
    return jax.shard_map(per_device, mesh=mesh, in_specs=in_specs, out_specs=out_specs, check_vma=False)
```

```python
import jax
import jax.numpy as jnp
from jax import lax
from jax.experimental import pallas as pl
from jax.experimental.pallas import tpu as pltpu
from jax.sharding import PartitionSpec as P

MESH = pl.DeviceIdType.MESH
BF = jnp.bfloat16
F32 = jnp.float32

CH = 1536
SH = 384
HEADS = 3
HD = 64
AW = HEADS * HD
CELLS = 64
NWIN = 4
GROUPS = 2
WIN = 8
TABLE = 256
NPAIR = 4096

SLOTS = {}
COUNT = 0
for _name, _n in (
    ("halo_f", 5), ("halo_c", 5), ("fields", 16), ("wcol_z", 3), ("wcol_p", 15), ("att", 8), ("stat", 6),
    ("gatt", 8), ("gsh", 8), ("out_f", 5), ("out_g", 5), ("w_core", 1), ("w_p", 15), ("w_pair", 1), ("w_z", 8),
    ("w_zs", 4), ("back_p", 15), ("back_core", 12), ("s_p", 15), ("s_l", 3), ("s_far", 1),
):
    SLOTS[_name] = COUNT
    COUNT += _n

PLANE = [(dy, dx) for dy in range(4) for dx in range(4)][1:]


def nn(a, b):
    return lax.dot_general(a, b, (((1,), (0,)), ((), ())), preferred_element_type=F32)


def nt(a, b):
    return lax.dot_general(a, b, (((1,), (1,)), ((), ())), preferred_element_type=F32)


def tn(a, b):
    return lax.dot_general(a, b, (((0,), (0,)), ((), ())), preferred_element_type=F32)


def split3(value):
    high = value.astype(BF).astype(F32)
    middle = (value - high).astype(BF).astype(F32)
    return high, middle, value - high - middle


def swap_halves(first, second):
    low = lax.broadcasted_iota(jnp.int32, first.shape, 0) < 4
    return jnp.where(low, first, pltpu.roll(second, 4, 0)), jnp.where(low, pltpu.roll(first, 4, 0), second)


def cut_blocks(grid, blocks):
    for i in range(4):
        tiles = [[None, None] for _ in range(4)]
        for half in (0, 1):
            upper = grid[4 * i + 2 * half].astype(F32)
            lower = grid[4 * i + 2 * half + 1].astype(F32)
            for k in (0, 1):
                pair = swap_halves(upper[8 * k:8 * k + 8], lower[8 * k:8 * k + 8])
                tiles[2 * k][half], tiles[2 * k + 1][half] = pair
        for j in range(4):
            blocks[i, j] = jnp.concatenate(tiles[j], axis=0).astype(BF)


def join_blocks(blocks, grid):
    for i in range(4):
        for half in (0, 1):
            upper, lower = [], []
            for k in (0, 1):
                rows = slice(8 * half, 8 * half + 8)
                pair = swap_halves(blocks[i, 2 * k].astype(F32)[rows], blocks[i, 2 * k + 1].astype(F32)[rows])
                upper.append(pair[0])
                lower.append(pair[1])
            grid[4 * i + 2 * half] = jnp.concatenate(upper, axis=0).astype(BF)
            grid[4 * i + 2 * half + 1] = jnp.concatenate(lower, axis=0).astype(BF)


def write_kernel(blocks_f, blocks_g, weights, small, out_f, out_g, out_w, out_t, out_s, out_a, out_b):
    out_w[...] = weights[...]
    join_blocks(blocks_f, out_f)
    join_blocks(blocks_g, out_g)
    out_t[...] = small[2:2 + HEADS, 0:out_t.shape[1]]
    spare = small[2:2 + HEADS, TABLE - 1:TABLE]
    scales = jnp.transpose(jnp.concatenate([jnp.broadcast_to(spare, (HEADS, 128)), jnp.zeros((8 - HEADS, 128), F32)], axis=0))
    out_s[...] = scales[0:1, 0:HEADS].reshape(HEADS)
    out_a[...] = small[0]
    out_b[...] = small[1]


def whole_kernel(
    fields_hbm, cot_hbm, wt_hbm, wout, logs, table, index, mask, gain_ref, shift_ref,
    out_f, out_g, out_w, out_s,
    fields_grid, cot_grid, wt, fields, cot, xbuf, cbuf, wcol, abuf, onehot, bsrow, idx_row, tab_pad, bsig, lab_col, qs, ks, vs, probs, coss, rqs, rks,
    mixed, stat_all, gmix, ga_send, ga_recv, ga_relay, gs_send, gs_recv, gs_relay, obuf, gobuf, tacc, sacc, gacc, flat,
    wc_send, wc_recv, wacc, wp_send, wp_recv, wp_sum, wp_pair, wp_both, bz, sm_p, sm_l, sm_f, local_sem, ssem, rsem,
):
    lat = lax.axis_index("lat")
    lon = lax.axis_index("lon")
    t = lax.axis_index("tp")
    zh = lat // 2
    core = lat % 2
    ly = lon // 4
    lx = lon % 4

    def ring(value, by, count):
        return lax.rem(value + by + count, count)

    lat_p, lat_n = ring(lat, -1, 8), ring(lat, 1, 8)
    lon_p, lon_n = ring(lon, -1, 16), ring(lon, 1, 16)
    sib = (zh * 2 + (1 - core), lon, t)

    def tp_dev(d):
        return (lat, lon, ring(t, d, 4))

    def plane(o):
        return ring(ly, PLANE[o][0], 4), ring(lx, PLANE[o][1], 4)

    def plane_from(o):
        return ring(ly, -PLANE[o][0], 4), ring(lx, -PLANE[o][1], 4)

    def plane_dev(o):
        y, x = plane(o)
        return (lat, y * 4 + x, t)

    def z_dev(d):
        return (ring(zh, d, 4) * 2 + core, lon, t)

    def copy(src, dst, slot, dev, send_slot=None):
        return pltpu.make_async_remote_copy(
            src_ref=src, dst_ref=dst, send_sem=ssem.at[slot if send_slot is None else send_slot],
            recv_sem=rsem.at[slot], device_id=dev, device_id_type=MESH,
        )

    def send(src, dst, slot, dev, send_slot=None):
        copy(src, dst, slot, dev, send_slot).start()

    def got(dst, slot):
        copy(dst, dst, slot, sib).wait_recv()

    def sent(src, slot):
        copy(src, src, slot, sib).wait_send()

    own = []

    def keep(src, dst):
        own.append(pltpu.make_async_copy(src, dst, local_sem.at[len(own)]))
        own[-1].start()

    keep(fields_hbm, fields_grid)
    keep(cot_hbm, cot_grid)
    keep(wt_hbm, wt)

    z_pair = zh + 1 - 2 * (zh % 2)
    z_far = 3 - zh
    pair_devs = [sib, (z_pair * 2 + core, lon, t), (z_pair * 2 + (1 - core), lon, t)]

    partners = [plane_dev(o) for o in range(15)] + pair_devs
    partners += [(lat_p, lon, t), (lat_n, lon, t), (lat_p, lon_p, t), (lat_n, lon_n, t)]
    partners += [tp_dev(d) for d in (1, 2, 3)] + [(z_far * 2 + core, lon, ring(t, d, 4)) for d in range(4)]
    barrier = pltpu.get_barrier_semaphore()
    for dev in partners:
        pl.semaphore_signal(barrier, inc=1, device_id=dev, device_id_type=MESH)

    def keep_grid(grid, dst):
        keep(grid.at[1:3, 1:3], dst.at[0])
        keep(grid.at[1:3, 3], dst.at[1, :, 0])
        keep(grid.at[3, 1:3], dst.at[2, 0])
        keep(grid.at[3, 3], dst.at[3, 0, 0])

    x_own = xbuf.at[t]
    own[0].wait()
    cut_blocks(fields_grid, fields)
    keep_grid(fields, x_own)

    pl.semaphore_wait(barrier, len(partners))

    def halo_lon(grid, dst, base):
        send(grid.at[1:3, 0], dst.at[1, :, 1], base, (lat, lon_p, t))
        send(grid.at[3, 0], dst.at[3, 0, 1], base + 2, (lat, lon_p, t))

    def halo_lat(grid, dst, base):
        send(grid.at[0, 1:3], dst.at[2, 1], base + 1, (lat_p, lon, t))
        send(grid.at[0, 3], dst.at[3, 1, 0], base + 3, (lat_p, lon, t))
        send(grid.at[0, 0], dst.at[3, 1, 1], base + 4, (lat_p, lon_p, t))

    def halo_parts(dst):
        return [dst.at[1, :, 1], dst.at[2, 1], dst.at[3, 0, 1], dst.at[3, 1, 0], dst.at[3, 1, 1]]

    side = t // 2
    is_mid = (t == 1) | (t == 2)
    is_edge = jnp.logical_not(is_mid)
    partner = 2 * side + 1 - t % 2
    far_mid = 2 - side
    far_edge = 3 - 3 * side
    far_slot = jnp.where(is_mid, 1, 2)

    def on_line(where):
        return (lat, lon, where)

    def spread_start(name, n, src, dst, i):
        base = SLOTS[name] + i
        send(src, dst, base + n * far_slot, on_line(far_mid), base + n)

        @pl.when(is_mid)
        def _():
            send(src, dst, base + n, on_line(far_edge), base + 2 * n)

        send(src, dst, base, on_line(partner), base)

    def spread_relay(name, n, buf, i):
        base = SLOTS[name] + i

        @pl.when(is_mid)
        def _():
            chunk = buf.at[far_edge, i]
            got(chunk, base + 2 * n)
            send(chunk, chunk, base + 2 * n, on_line(partner), base + 3 * n)

    due = (t, partner, far_mid, far_edge)

    def spread_wait(name, n, buf, i, step):
        base = SLOTS[name] + i
        if step == 1:
            got(buf.at[partner, i], base)
        if step == 2:
            got(buf.at[far_mid, i], base + n)
        if step == 3:
            @pl.when(is_edge)
            def _():
                got(buf.at[far_edge, i], base + 2 * n)

    def spread_drain(name, n, chunk, i):
        base = SLOTS[name] + i
        sent(chunk, base)
        sent(chunk, base + n)

        @pl.when(is_mid)
        def _():
            sent(chunk, base + 2 * n)
            sent(chunk, base + 3 * n)

    def sum_start(name, part, recv, relay, g, term):
        base = SLOTS[name] + g
        part[far_edge, g] = term(far_edge)

        @pl.when(is_edge)
        def _():
            send(part.at[far_edge, g], relay.at[g], base + 6, on_line(partner), base + 4)

        part[far_mid, g] = term(far_mid)
        send(part.at[far_mid, g], recv.at[t, g], base + 2 * far_slot, on_line(far_mid), base + 2)
        part[partner, g] = term(partner)
        send(part.at[partner, g], recv.at[t, g], base, on_line(partner), base)
        part[t, g] = term(t)

    def sum_relay(name, part, recv, relay, g):
        base = SLOTS[name] + g

        @pl.when(is_mid)
        def _():
            got(relay.at[g], base + 6)
            part[far_edge, g] = (part[far_edge, g].astype(F32) + relay[g].astype(F32)).astype(BF)
            send(part.at[far_edge, g], recv.at[t, g], base + 2, on_line(far_edge), base + 4)

    def sum_end(name, part, recv, g):
        base = SLOTS[name] + g
        got(recv.at[partner, g], base)
        got(recv.at[far_mid, g], base + 2)

        @pl.when(is_mid)
        def _():
            got(recv.at[far_edge, g], base + 4)

        @pl.when(is_edge)
        def _():
            recv[far_edge, g] = jnp.zeros(recv.shape[2:], BF)

        total = part[t, g].astype(F32)
        for src in (partner, far_mid, far_edge):
            total = total + recv[src, g].astype(F32)
        return total

    def give_fields(w, src):
        spread_start("fields", 4, src, x_own.at[w], w)

    halo_lat(fields, x_own, SLOTS["halo_f"])
    halo_lon(fields, x_own, SLOTS["halo_f"])

    piece_rows = pl.ds(pl.multiple_of(lx * 48, 16), 48)
    has_piece = ly < 3

    def piece(y, x):
        rows = pl.ds(pl.multiple_of(x * 48, 16), 48)
        return wcol.at[1:4, rows, pl.ds(pl.multiple_of(y * 128, 128), 128)]

    @pl.when(has_piece)
    def _():
        for d in (1, 2, 3):
            cols = pl.ds(pl.multiple_of(ring(t, d, 4) * SH + ly * 128, 128), 128)
            here = pl.ds(pl.multiple_of(ly * 128, 128), 128)
            send(wout.at[piece_rows, cols], wcol.at[d, piece_rows, here], SLOTS["wcol_z"] + d - 1, tp_dev(d))

    give_fields(0, fields.at[1:3, 1:3])
    own[1].wait()
    cut_blocks(cot_grid, cot)
    keep_grid(cot, cbuf)
    keep(wout.at[:, pl.ds(pl.multiple_of(t * SH, 128), SH)], wcol.at[0])

    def place(n):
        a, b, c, d = (n >> 5) & 1, (n >> 4) & 1, (n >> 2) & 3, n & 3
        return 4 * a + c, 4 * b + d

    def iota(shape, dim):
        return lax.broadcasted_iota(jnp.int32, shape, dim)

    def hot(flag):
        return jnp.where(flag, 1.0, 0.0)

    row_of, col_of = place(iota((CELLS, CELLS), 0))
    order = hot(iota((CELLS, CELLS), 1) == row_of * WIN + col_of).astype(BF)
    swapped = nn(order, index[...].astype(F32).astype(BF)).astype(BF)
    idx = nt(swapped, order)
    for c in range(NPAIR // 128):
        idx_row[0:1, c * 128:(c + 1) * 128] = jnp.concatenate([idx[2 * c:2 * c + 1], idx[2 * c + 1:2 * c + 2]], axis=1)

    cell = iota((NWIN * CELLS, 16), 0)
    row_of, col_of = place(cell)
    row_of, col_of = row_of + WIN * (cell >> 7), col_of + WIN * ((cell >> 6) & 1)
    picked_rows = nn(hot(iota((NWIN * CELLS, 16), 1) == row_of).astype(BF), mask[...].astype(F32).astype(BF))
    labels = jnp.sum(hot(iota((NWIN * CELLS, 16), 1) == col_of) * picked_rows, axis=1, keepdims=True)
    lab_col[...] = labels + 4.0 * (iota((NWIN * CELLS, 1), 0) >> 6).astype(F32)

    own[4].wait()
    got(halo_parts(x_own)[0], SLOTS["halo_f"])
    give_fields(1, x_own.at[1])
    own[5].wait()
    got(halo_parts(x_own)[1], SLOTS["halo_f"] + 1)
    give_fields(2, x_own.at[2])
    own[6].wait()
    for part in (2, 3, 4):
        got(halo_parts(x_own)[part], SLOTS["halo_f"] + part)
    give_fields(3, x_own.at[3])

    @pl.when(has_piece)
    def _():
        for d in (1, 2, 3):
            here = pl.ds(pl.multiple_of(ly * 128, 128), 128)
            got(wcol.at[d, piece_rows, here], SLOTS["wcol_z"] + d - 1)
        for o in range(15):
            send(piece(ly, lx), piece(ly, lx), SLOTS["wcol_p"] + o, plane_dev(o))

    halo_lon(cot, cbuf, SLOTS["halo_c"])

    spread_relay("fields", 4, xbuf, 0)

    tab_pad[...] = jnp.zeros_like(tab_pad)
    tab_pad[0:HEADS, 0:table.shape[1]] = table[...]
    tab = jnp.concatenate([*split3(tab_pad[...]), jnp.zeros((8, TABLE), F32)], axis=0).astype(BF)
    entry = iota((TABLE, 512), 0).astype(F32)
    for c in range(NPAIR // 512):
        span = slice(c * 512, (c + 1) * 512)
        picked = hot(entry == idx_row[0:1, span]).astype(BF)
        onehot[:, span] = picked
        parts = nn(tab, picked)
        bias = parts[0:8] + parts[8:16] + parts[16:24]
        sig = 1.0 / (1.0 + jnp.exp(-bias))
        bsrow[:, span] = sig
        for k in range(8):
            for h in range(HEADS):
                at = 8 * c + k
                pair = jnp.concatenate([16.0 * sig[h:h + 1, k * CELLS:(k + 1) * CELLS]] * 2, axis=1)
                bsig[h, at:at + 1, :] = pair
                bsig[h, CELLS + at:CELLS + at + 1, :] = pair
    spread_relay("fields", 4, xbuf, 1)
    tacc[...] = jnp.zeros_like(tacc)
    sacc[...] = jnp.zeros_like(sacc)
    gacc[...] = jnp.zeros_like(gacc)
    scales = jnp.exp(logs[...])

    own[2].wait()
    own[3].wait()

    eye = iota((2 * CELLS, 2 * CELLS), 0) == iota((2 * CELLS, 2 * CELLS), 1)

    def forward(g):
        @pl.when(g == 1)
        def _():
            spread_relay("fields", 4, xbuf, 3)

        proj = jnp.zeros((2 * CELLS, 3 * AW), F32)
        for step, src in enumerate(due):
            for w in (2 * g, 2 * g + 1):
                spread_wait("fields", 4, xbuf, w, step)
            cols = pl.ds(pl.multiple_of(src * SH, 128), SH)
            proj = proj + nt(xbuf[src, pl.ds(2 * g, 2)].reshape(2 * CELLS, SH), wt[:, cols])

        @pl.when(g == 0)
        def _():
            spread_relay("fields", 4, xbuf, 2)

        column = lab_col[pl.ds(pl.multiple_of(2 * g * CELLS, 128), 128), :]
        row = jnp.sum(jnp.where(eye, column, 0.0), axis=0, keepdims=True)
        same = row == column
        heads = range(HEADS)

        def slot(kind, h):
            at = kind * AW + h * HD
            return proj[:, at:at + HD]

        q = [slot(0, h) for h in heads]
        k = [slot(1, h) for h in heads]
        v = [slot(2, h).astype(BF) for h in heads]
        rq = [lax.rsqrt(jnp.sum(q[h] * q[h], axis=1, keepdims=True) + 1e-06) for h in heads]
        rk = [lax.rsqrt(jnp.sum(k[h] * k[h], axis=1, keepdims=True) + 1e-06) for h in heads]
        q_hat = [(q[h] * rq[h]).astype(BF) for h in heads]
        k_hat = [(k[h] * rk[h]).astype(BF) for h in heads]
        cosine = [nt(q_hat[h], k_hat[h]) for h in heads]
        power = [scales[:, h:h + 1] * (cosine[h] - 1.0) + (bsig[h] - 16.0) for h in heads]
        weight = [jnp.where(same, jnp.exp(power[h]), 0.0) for h in heads]
        total = [jnp.sum(weight[h], axis=1, keepdims=True) for h in heads]
        prob = [(weight[h] * (1.0 / total[h])).astype(BF) for h in heads]
        attended = [nn(prob[h], v[h]).astype(BF) for h in heads]
        for i in (0, 1):
            for h in heads:
                at = i * AW + h * HD
                abuf[t, g, :, at:at + HD] = attended[h][i * CELLS:(i + 1) * CELLS]
        for h in heads:
            qs[g, h] = q_hat[h]
            ks[g, h] = k_hat[h]
            vs[g, h] = v[h]
            probs[g, h] = prob[h]
            coss[g, h] = cosine[h]
            rqs[g, h] = rq[h]
            rks[g, h] = rk[h]
        spread_start("att", 2, abuf.at[t, g], abuf.at[t, g], g)

    gain = gain_ref[...].reshape(1, SH)
    shift = shift_ref[...].reshape(1, SH)
    lane = iota((2 * CELLS, 128), 1)

    def unpack(pair):
        return jnp.concatenate([pair[:, :AW], pair[:, AW:]], axis=0)

    def cells_of(buf, g):
        return buf[pl.ds(2 * g, 2)].reshape(2 * CELLS, SH).astype(F32)

    def mix(g):
        total = jnp.zeros((2 * CELLS, SH), F32)
        for step, src in enumerate(due):
            spread_wait("att", 2, abuf, g, step)
            total = total + nn(unpack(abuf[src, g]), wcol[ring(t - src, 0, 4)])
        mixed[g] = total
        grad_norm = cells_of(cbuf, g) * gain
        packed = jnp.zeros((2 * CELLS, 128), F32)
        for i, v in enumerate((total, total * total, grad_norm, grad_norm * total)):
            packed = jnp.where(lane == i, jnp.sum(v, axis=1, keepdims=True), packed)
        stat_all[t, g] = jnp.transpose(packed)[0:8]
        mine = stat_all.at[t, g]
        for d in (1, 2, 3):
            send(mine, mine, SLOTS["stat"] + (d - 1) * 2 + g, tp_dev(d))

    def normalise(g):
        for d in (1, 2, 3):
            got(stat_all.at[ring(t, -d, 4), g], SLOTS["stat"] + (d - 1) * 2 + g)
        totals = stat_all[0, g] + stat_all[1, g] + stat_all[2, g] + stat_all[3, g]
        packed = jnp.transpose(jnp.concatenate([totals, jnp.zeros((120, 128), F32)], axis=0))
        mean = packed[:, 0:1] / CH
        variance = packed[:, 1:2] / CH - mean * mean
        inv_std = 1.0 / jnp.sqrt(variance + 1e-05)
        grad_mean = packed[:, 2:3] / CH
        cross_mean = inv_std * (packed[:, 3:4] - mean * packed[:, 2:3]) / CH
        normed = (mixed[g] - mean) * inv_std
        rows = cells_of(cbuf, g)
        grad = (inv_std * (rows * gain - grad_mean - normed * cross_mean)).astype(BF)
        gmix[g] = grad
        def term(dst):
            part = nt(grad, wcol[ring(t - dst, 0, 4)])
            return jnp.concatenate([part[:CELLS], part[CELLS:]], axis=1).astype(BF)

        sum_start("gatt", ga_send, ga_recv, ga_relay, g, term)
        base = xbuf[t, pl.ds(2 * g, 2)].reshape(2 * CELLS, SH).astype(F32)
        obuf[pl.ds(2 * g, 2)] = (base + (gain * normed + shift)).astype(BF).reshape(2, 2, 2, 16, SH)
        gacc[0:1, :] += jnp.sum(rows * normed, axis=0, keepdims=True)
        gacc[1:2, :] += jnp.sum(rows, axis=0, keepdims=True)

    def backward(g):
        total = sum_end("gatt", ga_send, ga_recv, g)
        grad_att = unpack(total.astype(BF))
        heads = range(HEADS)
        ga = [grad_att[:, h * HD:(h + 1) * HD] for h in heads]
        prob = [probs[g, h] for h in heads]
        q_hat = [qs[g, h] for h in heads]
        k_hat = [ks[g, h] for h in heads]
        grad_prob = [nt(ga[h], vs[g, h]) for h in heads]
        grads_v = [tn(prob[h], ga[h]) for h in heads]
        prob_f = [prob[h].astype(F32) for h in heads]
        inner = [jnp.sum(prob_f[h] * grad_prob[h], axis=1, keepdims=True) for h in heads]
        grad_logit = [prob_f[h] * (grad_prob[h] - inner[h]) for h in heads]
        grad_cos = [(grad_logit[h] * scales[:, h:h + 1]).astype(BF) for h in heads]
        gq = [nn(grad_cos[h], k_hat[h]) for h in heads]
        gk = [tn(grad_cos[h], q_hat[h]) for h in heads]
        for h in heads:
            tacc[h] += grad_logit[h]
            sacc[h] += grad_logit[h] * coss[g, h]
        q_float = [q_hat[h].astype(F32) for h in heads]
        k_float = [k_hat[h].astype(F32) for h in heads]
        q_in = [jnp.sum(q_float[h] * gq[h], axis=1, keepdims=True) for h in heads]
        k_in = [jnp.sum(k_float[h] * gk[h], axis=1, keepdims=True) for h in heads]
        grads_q = [(gq[h] - q_float[h] * q_in[h]) * rqs[g, h] for h in heads]
        grads_k = [(gk[h] - k_float[h] * k_in[h]) * rks[g, h] for h in heads]
        stacked = jnp.concatenate(grads_q + grads_k + grads_v, axis=1).astype(BF)
        def term(dst):
            return nn(stacked, wt[:, pl.ds(pl.multiple_of(dst * SH, 128), SH)]).astype(BF)

        sum_start("gsh", gs_send, gs_recv, gs_relay, g, term)

    def finish(g):
        total = sum_end("gsh", gs_send, gs_recv, g) + cells_of(cbuf, g)
        gobuf[pl.ds(2 * g, 2)] = total.astype(BF).reshape(2, 2, 2, 16, SH)

    def give_first(buf, out, base):
        out[1:3, 1:3] = buf[0]
        out[1:3, 3] = buf[1, :, 0]
        send(buf.at[1, :, 1], out.at[1:3, 0], base, (lat, lon_n, t))

    def give_second(buf, out, base):
        send(buf.at[2, 1], out.at[0, 1:3], base + 1, (lat_n, lon, t))
        send(buf.at[3, 0, 1], out.at[3, 0], base + 2, (lat, lon_n, t))
        send(buf.at[3, 1, 0], out.at[0, 3], base + 3, (lat_n, lon, t))
        send(buf.at[3, 1, 1], out.at[0, 0], base + 4, (lat_n, lon_n, t))
        out[3, 1:3] = buf[2, 0]
        out[3, 3] = buf[3, 0, 0]

    def back_parts(out):
        return [out.at[1:3, 0], out.at[0, 1:3], out.at[3, 0], out.at[0, 3], out.at[0, 0]]

    def weight_first():
        for group in range(4):
            wacc[group] = tn(unpack(abuf[group, 0]), gmix[0])

    def weight_start():
        for j in (0, 1):
            far = 2 * (1 - core) + j
            wc_send[j] = (wacc[far] + tn(unpack(abuf[far, 1]), gmix[1])).astype(BF)
        send(wc_send, wc_recv, SLOTS["w_core"], sib)
        for j in (0, 1):
            near = 2 * core + j
            wacc[near] = wacc[near] + tn(unpack(abuf[near, 1]), gmix[1])

    def rows_of(y, x):
        return pl.ds(pl.multiple_of(x * 48 + y * 16, 16), 16)

    def weight_plane():
        got(wc_recv, SLOTS["w_core"])
        for j in (0, 1):
            total = wacc[2 * core + j] + wc_recv[j].astype(F32)
            wacc[2 * core + j] = total
            wp_send[j] = total.astype(BF)
        for o in range(15):
            y, x = plane(o)

            @pl.when(y < 3)
            def _():
                send(wp_send.at[:, rows_of(y, x)], wp_recv.at[o], SLOTS["w_p"] + o, plane_dev(o))

    holder = t // 2 == core

    def weight_z():
        @pl.when(has_piece)
        def _():
            for o in range(15):
                got(wp_recv.at[o], SLOTS["w_p"] + o)
            for j in (0, 1):
                total = wacc[2 * core + j, rows_of(ly, lx), :]
                for o in range(15):
                    total = total + wp_recv[o, j].astype(F32)
                wp_sum[j] = total.astype(BF)
            send(wp_sum, wp_pair, SLOTS["w_pair"], (z_pair * 2 + core, lon, t))

    def weight_far():
        @pl.when(has_piece)
        def _():
            got(wp_pair, SLOTS["w_pair"])
            wp_both[...] = (wp_sum[...].astype(F32) + wp_pair[...].astype(F32)).astype(BF)
            for j in (0, 1):
                keeper = 2 * core + j
                slot = SLOTS["w_z"] + (zh // 2) * 4 + t
                send(wp_both.at[j], bz.at[zh // 2, t], slot, (z_far * 2 + core, lon, keeper), SLOTS["w_zs"] + 2 * j)

                @pl.when(keeper != t)
                def _():
                    send(wp_both.at[j], bz.at[zh // 2, t], slot, (lat, lon, keeper), SLOTS["w_zs"] + 2 * j + 1)

    def weight_back_plane():
        @pl.when(holder & has_piece)
        def _():
            bz[zh // 2, t] = wp_both[t % 2]
            for z in range(2):
                for src in range(4):
                    @pl.when((zh // 2 != z) | (t != src))
                    def _():
                        got(bz.at[z, src], SLOTS["w_z"] + z * 4 + src)

            for src in range(4):
                total = bz[0, src].astype(F32) + bz[1, src].astype(F32)
                out_w[rows_of(ly, lx), src * SH:(src + 1) * SH] = total.astype(BF)
            mine = out_w.at[rows_of(ly, lx)]
            for o in range(15):
                send(mine, mine, SLOTS["back_p"] + o, plane_dev(o))
            send(mine, mine, SLOTS["back_core"] + lx * 3 + ly, sib)

    def weight_back_core():
        @pl.when(holder)
        def _():
            for o in range(15):
                y, x = plane_from(o)

                @pl.when(y < 3)
                def _():
                    mine = out_w.at[rows_of(y, x)]
                    got(mine, SLOTS["back_p"] + o)
                    send(mine, mine, SLOTS["back_core"] + x * 3 + y, sib)

    def small_start():
        folded_t = [tacc[h, :CELLS, :CELLS] + tacc[h, CELLS:, CELLS:] for h in range(HEADS)]
        for c in range(NPAIR // 128):
            for h in range(HEADS):
                pair = [folded_t[h][2 * c + i:2 * c + i + 1, :] for i in (0, 1)]
                flat[h:h + 1, c * 128:(c + 1) * 128] = jnp.concatenate(pair, axis=1)
        spread = bsrow[0:HEADS, :]
        terms = flat[0:HEADS, :] * 16.0 * spread * (1.0 - spread)
        pad = jnp.zeros((8 - HEADS, NPAIR), F32)
        pieces = jnp.concatenate([v for p in split3(terms) for v in (p, pad)], axis=0).astype(BF)
        folded = nt(pieces, onehot[...])
        sm_p[lon] = folded[0:8] + folded[8:16] + folded[16:24]
        for h in range(HEADS):
            amount = jnp.sum(jnp.sum(sacc[h], axis=1, keepdims=True), axis=0, keepdims=True) * scales[:, h:h + 1]
            sm_p[lon, h:h + 1, TABLE - 1:TABLE] = amount
        sm_p[lon, 3:5, :] = gacc[0:2, 0:TABLE]
        sm_p[lon, 5:6, :] = jnp.concatenate([gacc[0:1, TABLE:SH], gacc[1:2, TABLE:SH]], axis=1)
        for o in range(15):
            send(sm_p.at[lon], sm_p.at[lon], SLOTS["s_p"] + o, plane_dev(o))

    def small_lat():
        for o in range(15):
            y, x = plane_from(o)
            got(sm_p.at[y * 4 + x], SLOTS["s_p"] + o)
        total = sm_p[0]
        for i in range(1, 16):
            total = total + sm_p[i]
        sm_l[2 * (zh % 2) + core] = total
        mine = sm_l.at[2 * (zh % 2) + core]
        for i, dev in enumerate(pair_devs):
            send(mine, mine, SLOTS["s_l"] + i, dev)

    def small_far():
        for i, where in enumerate((2 * (zh % 2) + 1 - core, 2 * (1 - zh % 2) + core, 2 * (1 - zh % 2) + 1 - core)):
            got(sm_l.at[where], SLOTS["s_l"] + i)
        sm_f[0] = sm_l[0] + sm_l[1] + sm_l[2] + sm_l[3]
        send(sm_f.at[0], sm_f.at[1], SLOTS["s_far"], (z_far * 2 + core, lon, t))

    def small_end():
        got(sm_f.at[1], SLOTS["s_far"])
        total = sm_f[0] + sm_f[1]
        out_s[...] = jnp.zeros_like(out_s)
        out_s[0:2, 0:TABLE] = total[3:5]
        out_s[0:1, TABLE:SH] = total[5:6, 0:128]
        out_s[1:2, TABLE:SH] = total[5:6, 128:256]
        out_s[2:5, 0:TABLE] = total[0:3]

    def both(body):
        def step(g, carry):
            body(g)
            return carry

        lax.fori_loop(0, GROUPS, step, 0)

    def first(g):
        forward(g)

        @pl.when(g == 0)
        def _():
            halo_lat(cot, cbuf, SLOTS["halo_c"])

    both(first)
    own[11].wait()
    for o in range(15):
        y, x = plane_from(o)

        @pl.when(y < 3)
        def _():
            got(piece(y, x), SLOTS["wcol_p"] + o)

    for i in (7, 8, 9, 10):
        own[i].wait()
    got(halo_parts(cbuf)[0], SLOTS["halo_c"])

    def drain_inputs():
        for base, parts in (("halo_f", halo_parts(x_own)), ("halo_c", halo_parts(cbuf))):
            for i in range(5):
                sent(parts[i], SLOTS[base] + i)
        for w in range(NWIN):
            spread_drain("fields", 4, xbuf.at[0, 0], w)

        @pl.when(has_piece)
        def _():
            for d in range(3):
                sent(wcol.at[0, 0:48, 0:128], SLOTS["wcol_z"] + d)
            for o in range(15):
                sent(wcol.at[1:4, 0:48, 0:128], SLOTS["wcol_p"] + o)

    def drain_middle():
        for g in range(GROUPS):
            spread_drain("att", 2, abuf.at[0, 0], g)
            for i in range(3):
                sent(stat_all.at[0, 0], SLOTS["stat"] + 2 * i + g)
                sent(ga_send.at[0, 0], SLOTS["gatt"] + 2 * i + g)
        sent(wc_send, SLOTS["w_core"])

    def drain_late():
        for i in range(5):
            sent(back_parts(out_f)[i], SLOTS["out_f"] + i)
        for o in range(15):
            sent(sm_p.at[0], SLOTS["s_p"] + o)

            @pl.when(plane(o)[0] < 3)
            def _():
                sent(wp_send.at[:, 0:16], SLOTS["w_p"] + o)

    def middle(g):
        @pl.when(g == 1)
        def _():
            for i in range(1, 5):
                got(halo_parts(cbuf)[i], SLOTS["halo_c"] + i)

        @pl.when(g == 0)
        def _():
            spread_relay("att", 2, abuf, 0)

        mix(g)

        @pl.when(g == 0)
        def _():
            spread_relay("att", 2, abuf, 1)

        @pl.when(g == 1)
        def _():
            sum_relay("gatt", ga_send, ga_recv, ga_relay, 0)
            weight_first()

        normalise(g)

    both(middle)
    weight_start()
    sum_relay("gatt", ga_send, ga_recv, ga_relay, 1)

    def last(g):
        @pl.when(g == 1)
        def _():
            weight_plane()
            sum_relay("gsh", gs_send, gs_recv, gs_relay, 0)
            give_first(obuf, out_f, SLOTS["out_f"])
            give_second(obuf, out_f, SLOTS["out_f"])

        backward(g)

    both(last)
    weight_z()
    sum_relay("gsh", gs_send, gs_recv, gs_relay, 1)
    small_start()
    weight_far()
    finish(0)
    give_first(gobuf, out_g, SLOTS["out_g"])
    small_lat()
    weight_back_plane()
    finish(1)
    give_second(gobuf, out_g, SLOTS["out_g"])
    small_far()
    drain_inputs()
    drain_middle()
    drain_late()
    weight_back_core()
    small_end()

    for i in range(5):
        got(back_parts(out_f)[i], SLOTS["out_f"] + i)
        got(back_parts(out_g)[i], SLOTS["out_g"] + i)

    for i in range(5):
        sent(back_parts(out_g)[i], SLOTS["out_g"] + i)
    for g in range(GROUPS):
        for i in range(3):
            sent(gs_send.at[0, 0], SLOTS["gsh"] + 2 * i + g)

    @pl.when(has_piece)
    def _():
        sent(wp_sum, SLOTS["w_pair"])
        for j in (0, 1):
            sent(wp_both.at[j], SLOTS["w_zs"] + 2 * j)

            @pl.when(2 * core + j != t)
            def _():
                sent(wp_both.at[j], SLOTS["w_zs"] + 2 * j + 1)

    @pl.when(holder & has_piece)
    def _():
        for o in range(15):
            sent(out_w.at[0:16], SLOTS["back_p"] + o)
        sent(out_w.at[0:16], SLOTS["back_core"] + lx * 3 + ly)

    @pl.when(holder)
    def _():
        for o in range(15):
            y, x = plane_from(o)

            @pl.when(y < 3)
            def _():
                sent(out_w.at[0:16], SLOTS["back_core"] + x * 3 + y)

    for i in range(3):
        sent(sm_l.at[0], SLOTS["s_l"] + i)
    sent(sm_f.at[0], SLOTS["s_far"])

    @pl.when(jnp.logical_not(holder))
    def _():
        for x in range(4):
            for y in range(3):
                got(out_w.at[x * 48 + y * 16:x * 48 + y * 16 + 16], SLOTS["back_core"] + x * 3 + y)


def per_device(
    fields, w_qkv, w_out, log_scale, bias_table, bias_index, mask_ids, norm_gain, norm_shift, cotangent
):
    rows = bias_table.shape[0]
    wt = w_qkv.transpose(1, 2, 0).reshape(3 * AW, CH)
    hbm = pl.BlockSpec(memory_space=pltpu.HBM)
    vmem = pl.BlockSpec(memory_space=pltpu.VMEM)
    scratch = [
        ((16, 16, SH), BF), ((16, 16, SH), BF), ((576, CH), BF), ((4, 4, 16, SH), BF), ((4, 4, 16, SH), BF), ((4, 4, 2, 2, 16, SH), BF), ((4, 2, 2, 16, SH), BF), ((4, AW, SH), BF),
        ((4, 2, CELLS, SH), BF), ((TABLE, NPAIR), BF), ((8, NPAIR), F32), ((8, NPAIR), F32), ((8, TABLE), F32),
        ((HEADS, 2 * CELLS, 2 * CELLS), F32), ((NWIN * CELLS, 1), F32),
        ((2, HEADS, 2 * CELLS, HD), BF), ((2, HEADS, 2 * CELLS, HD), BF), ((2, HEADS, 2 * CELLS, HD), BF),
        ((2, HEADS, 2 * CELLS, 2 * CELLS), BF), ((2, HEADS, 2 * CELLS, 2 * CELLS), F32),
        ((2, HEADS, 2 * CELLS, 1), F32), ((2, HEADS, 2 * CELLS, 1), F32),
        ((2, 2 * CELLS, SH), F32), ((4, 2, 8, 128), F32), ((2, 2 * CELLS, SH), BF),
        ((4, 2, CELLS, SH), BF), ((4, 2, CELLS, SH), BF), ((2, CELLS, SH), BF),
        ((4, 2, 2 * CELLS, SH), BF), ((4, 2, 2 * CELLS, SH), BF), ((2, 2 * CELLS, SH), BF),
        ((4, 2, 2, 16, SH), BF), ((4, 2, 2, 16, SH), BF),
        ((HEADS, 2 * CELLS, 2 * CELLS), F32), ((HEADS, 2 * CELLS, 2 * CELLS), F32), ((8, SH), F32), ((8, NPAIR), F32),
        ((2, AW, SH), BF), ((2, AW, SH), BF), ((4, AW, SH), F32),
        ((2, AW, SH), BF), ((15, 2, 16, SH), BF), ((2, 16, SH), BF), ((2, 16, SH), BF), ((2, 16, SH), BF),
        ((2, 4, 16, SH), BF), ((16, 8, TABLE), F32), ((4, 8, TABLE), F32), ((2, 8, TABLE), F32),
    ]
    out_f, out_g, out_w, out_s = pl.pallas_call(
        whole_kernel,
        out_shape=(
            jax.ShapeDtypeStruct((4, 4, 16, SH), BF),
            jax.ShapeDtypeStruct((4, 4, 16, SH), BF),
            jax.ShapeDtypeStruct((AW, CH), BF),
            jax.ShapeDtypeStruct((8, SH), F32),
        ),
        in_specs=[hbm, hbm, hbm, hbm, vmem, vmem, vmem, vmem, vmem, vmem],
        out_specs=(vmem, vmem, vmem, vmem),
        scratch_shapes=[pltpu.VMEM(shape, kind) for shape, kind in scratch] + [
            pltpu.SemaphoreType.DMA((12,)),
            pltpu.SemaphoreType.DMA((COUNT,)),
            pltpu.SemaphoreType.DMA((COUNT,)),
        ],
        compiler_params=pltpu.CompilerParams(
            collective_id=0, has_side_effects=True, vmem_limit_bytes=60 * 1024 * 1024
        ),
        cost_estimate=pl.CostEstimate(flops=2_000_000_000, bytes_accessed=5_000_000, transcendentals=200_000),
    )(
        fields, cotangent, wt, w_out, log_scale.reshape(1, HEADS), bias_table.T, bias_index, mask_ids,
        norm_gain, norm_shift,
    )
    shapes = (
        (fields.shape, BF), (fields.shape, BF), ((AW, CH), BF), ((HEADS, rows), F32), ((HEADS,), F32),
        ((SH,), F32), ((SH,), F32),
    )
    block_out, grad_fields, grad_w_out, grad_table, grad_scale, grad_gain, grad_shift = pl.pallas_call(
        write_kernel,
        out_shape=tuple(jax.ShapeDtypeStruct(shape, kind) for shape, kind in shapes),
        in_specs=[vmem] * 4,
        out_specs=(vmem,) * 7,
        compiler_params=pltpu.CompilerParams(vmem_limit_bytes=60 * 1024 * 1024),
        cost_estimate=pl.CostEstimate(flops=1_000_000, bytes_accessed=2_000_000, transcendentals=0),
    )(out_f, out_g, out_w, out_s)
    return (block_out, grad_fields, grad_w_out, grad_table.T, grad_scale, grad_gain, grad_shift)


def solution(mesh):
    in_specs = (
        P("lat", "lon", "tp"), P(None, None, "tp"), P("tp", None), P("tp"), P(None, "tp"), P(),
        P("lat", "lon"), P("tp"), P("tp"), P("lat", "lon", "tp"),
    )
    out_specs = (
        P("lat", "lon", "tp"), P("lat", "lon", "tp"), P("tp", None), P(None, "tp"), P("tp"), P("tp"), P("tp"),
    )
    return jax.shard_map(per_device, mesh=mesh, in_specs=in_specs, out_specs=out_specs, check_vma=False)
```
